32 devices in a mesh: rows: 16 (over z, x, core), cols: 2 (over y).
Axes of the slice: x: 2, y: 2, z: 4, core: 2. Of those that a mesh axis runs over, the one named last changes fastest.
Arguments:
- right_sides: float32 [4, 16, 128, 256], P(None, 'rows'), may hold values from -6 to 6
- factor_blocks: bfloat16 [3, 16, 2, 8, 256, 256], P(None, 'rows', 'cols'), may hold values from -0.125 to 0.125
- diag_inverses: bfloat16 [4, 16, 256, 256], P(None, 'rows')
- source_ids: int32 [3, 16, 2, 8], P(None, 'rows', 'cols'), may hold values from 0 to 47, as said below
- block_counts: int32 [3, 16, 2], P(None, 'rows', 'cols'), may hold values from 1 to 8, as said below
Outputs:
- solution: float32 [4, 16, 128, 256], P(None, 'rows', 'cols')
The draws below stay inside these ranges and needn't reach their ends.
Inputs may be any that keep to these rules, and one draw needn't show every extreme that they name: source_ids[l, t, c, k] = m * 16 + s names a supernode of a level m <= l with s % 2 == c. block_counts[l, t, c] slots of target t on group c hold blocks of the factor; slots at and past it are not part of the factor. In every level some target and group has all 8 slots live.
All inputs are finite; a program needn't handle non-finite values.
Results may differ from the reference program's by a relative error of at most 0.007.
Values may be sent and summed in bfloat16 or wider, within the bound.
No kernel may reach another device: no remote copies, remote signals or barrier semaphores. Data moves between devices by JAX's collectives and lax.ppermute only.
A program may use at most 128 MiB of HBM per device.

```python
import math
import jax
import jax.numpy as jnp
from jax import lax

W = 256
RHS = 128
LEV = 4
BPD = 8
SUPER = 16
COLGRP = 2


def draw_diag_inverses(key, part):
    first_key, second_key = jax.random.split(key)
    diagonal = jax.random.uniform(first_key, (LEV, SUPER, W), jnp.float32, 0.6, 1.4)
    spread = jax.random.normal(second_key, (LEV, SUPER, W, W), jnp.float32) * (0.5 / math.sqrt(W))
    identity = jnp.eye(W, dtype=jnp.float32)
    return (spread + identity * diagonal[..., None, :]).astype(jnp.bfloat16)


def draw_source_ids(key, part):
    first_key, second_key = jax.random.split(key)
    shape = (LEV - 1, SUPER, COLGRP, BPD)
    ceiling = (jnp.arange(LEV - 1, dtype=jnp.int32) + 1).reshape(LEV - 1, 1, 1, 1)
    source_level = jax.random.randint(first_key, shape, 0, 12 * LEV, dtype=jnp.int32) % ceiling
    quotient = jax.random.randint(second_key, shape, 0, SUPER // COLGRP, dtype=jnp.int32)
    column = jnp.arange(COLGRP, dtype=jnp.int32).reshape(1, 1, COLGRP, 1)
    chosen = source_level * SUPER + quotient * COLGRP + column
    chosen = chosen.at[0, 0, 0, 0].set(0)
    chosen = chosen.at[LEV - 2, 0, COLGRP - 1, 0].set((LEV - 1) * SUPER - 1)
    return chosen


def draw_block_counts(key, part):
    first_key, second_key, third_key = jax.random.split(key, 3)
    shape = (LEV - 1, SUPER, COLGRP)
    raw_draws = jax.random.randint(first_key, shape, 0, BPD, dtype=jnp.int32)
    counted = 1 + raw_draws * raw_draws // max(BPD - 1, 1)
    places = SUPER * COLGRP
    position = jnp.arange(places, dtype=jnp.int32).reshape(1, SUPER, COLGRP)
    busiest = jax.random.randint(second_key, (LEV - 1, 1, 1), 0, places, dtype=jnp.int32)
    lightest = (busiest + 1 + jax.random.randint(third_key, (LEV - 1, 1, 1), 0, places - 1, dtype=jnp.int32)) % places
    counted = jnp.where(position == busiest, BPD, counted)
    counted = jnp.where(position == lightest, 1, counted)
    return counted.astype(jnp.int32)


def levels(stream_key, shape, pieces, low, top_value):
    factor_of, own = 1.0, jax.random.fold_in(stream_key, 6)
    for dim, parts in pieces:
        steps = jnp.exp(jax.random.uniform(jax.random.fold_in(own, dim), (parts,), jnp.float32, low / len(pieces), top_value / len(pieces)))
        factor_of = factor_of * jnp.repeat(steps, shape[dim] // parts).reshape([-1 if axis == dim else 1 for axis in range(len(shape))])
    return factor_of


def scatter_about(rng, extent, scale, most, pieces=(), kind=jnp.bfloat16):
    entries = jax.random.normal(rng, extent, jnp.float32) * scale
    if len(pieces) > 0:
        entries = levels(rng, extent, pieces, -0.22, 0.18) * entries
    return jnp.clip(entries, min=-most, max=most).astype(kind)


def setup_inputs(seed: int = 0) -> dict:
    keys = jax.random.split(jax.random.key(seed), 6)
    return {
        "right_sides": scatter_about(keys[0], (LEV, SUPER, RHS, W), 1.0, 6.0, ((1, 16),), jnp.float32),
        "factor_blocks": scatter_about(keys[1], (LEV - 1, SUPER, COLGRP, BPD, W, W), (W * BPD) ** -0.5, 0.125, ((1, 16), (2, 2))),
        "diag_inverses": draw_diag_inverses(jax.random.fold_in(keys[5], 71), 0),
        "source_ids": draw_source_ids(jax.random.fold_in(keys[5], 71), 0),
        "block_counts": draw_block_counts(jax.random.fold_in(keys[5], 71), 0),
    }


def reference(right_sides, factor_blocks, diag_inverses, source_ids, block_counts):
    solved = jnp.zeros((LEV * SUPER, RHS, W), jnp.bfloat16)
    slot_range = jnp.arange(BPD, dtype=jnp.int32)
    solutions = []
    for level_index in range(LEV):
        if level_index == 0:
            update = jnp.zeros((SUPER, RHS, W), jnp.float32)
        else:
            current_store = solved

            def one_target(items):
                blocks, chosen_ids, live_counts = items
                inputs = current_store[chosen_ids].astype(jnp.float32)
                live_mask = (slot_range[None, :] < live_counts[:, None]).astype(jnp.float32)
                return jnp.einsum("ckaw,ckwb,ck->ab", inputs, blocks.astype(jnp.float32), live_mask)

            update = lax.map(one_target, (factor_blocks[level_index - 1], source_ids[level_index - 1], block_counts[level_index - 1]))
        reduced = (right_sides[level_index] - update).astype(jnp.bfloat16)
        solution = jnp.einsum("saw,swb->sab", reduced.astype(jnp.float32), diag_inverses[level_index].astype(jnp.float32))
        solutions.append(solution)
        solved = solved.at[level_index * SUPER:(level_index + 1) * SUPER].set(solution.astype(jnp.bfloat16))
    return jnp.stack(solutions)
```

```python
import functools

import jax
import jax.numpy as jnp
from jax import lax
from jax.experimental import pallas as pl
from jax.experimental.pallas import tpu as pltpu
from jax.sharding import PartitionSpec as P


def level_kernel(groups, ids_ref, counts_ref, store_ref, *refs):
    factor_refs = refs[:groups]
    rhs_ref, inverse_ref, out_ref, rounded_ref, gathered = refs[groups:]
    slots, width = factor_refs[0].shape[0], factor_refs[0].shape[1]
    update = None
    for g in range(groups):
        for k in range(slots):
            piece = store_ref[ids_ref[g, k]]
            live = jnp.where(k < counts_ref[g], 1.0, 0.0).astype(piece.dtype)
            gathered[:, k * width:(k + 1) * width] = piece * live
        term = jnp.dot(
            gathered[...],
            factor_refs[g][...].reshape(slots * width, width),
            preferred_element_type=jnp.float32,
        )
        update = term if update is None else update + term
    reduced = (rhs_ref[...] - update).astype(jnp.bfloat16)
    solved = jnp.dot(reduced, inverse_ref[...], preferred_element_type=jnp.float32)
    out_ref[...] = solved
    rounded_ref[...] = solved.astype(jnp.bfloat16)


def solve_level(ids, counts, store, factors, rhs, inverse):
    groups = len(factors)
    rows, width = rhs.shape
    slots = factors[0].shape[0]
    vmem = pl.BlockSpec(memory_space=pltpu.VMEM)
    smem = pl.BlockSpec(memory_space=pltpu.SMEM)
    return pl.pallas_call(
        functools.partial(level_kernel, groups),
        out_shape=(
            jax.ShapeDtypeStruct((rows, width), jnp.float32),
            jax.ShapeDtypeStruct((rows, width), jnp.bfloat16),
        ),
        in_specs=[smem, smem, vmem] + [vmem] * groups + [vmem, vmem],
        out_specs=(vmem, vmem),
        scratch_shapes=[pltpu.VMEM((rows, slots * width), jnp.bfloat16)],
        compiler_params=pltpu.CompilerParams(vmem_limit_bytes=32 * 1024 * 1024),
        cost_estimate=pl.CostEstimate(
            flops=2 * rows * width * width * (groups * slots + 1),
            bytes_accessed=groups * slots * width * width * 2,
            transcendentals=0,
        ),
    )(ids, counts, store, *factors, rhs, inverse)


def shards(right_sides, factor_blocks, diag_inverses, source_ids, block_counts):
    col_count = lax.axis_size("cols")
    level_count, _, rhs_count, width = right_sides.shape
    share_rows = rhs_count // col_count
    col_index = lax.axis_index("cols")

    described = jnp.concatenate([source_ids[:, 0, 0], block_counts[:, 0, 0][:, None]], axis=1)
    factors = [[factor_blocks[l, 0, 0]] for l in range(level_count - 1)]
    descriptions = [described]
    for shift in range(1, col_count):
        pairs = [(i, (i + shift) % col_count) for i in range(col_count)]
        descriptions.append(lax.ppermute(described, "cols", pairs))
    for l in range(level_count - 1):
        for shift in range(1, col_count):
            pairs = [(i, (i + shift) % col_count) for i in range(col_count)]
            factors[l].append(lax.ppermute(factor_blocks[l, 0, 0], "cols", pairs))
    descriptions = jnp.stack(descriptions)

    rhs = lax.dynamic_slice_in_dim(right_sides[:, 0], col_index * share_rows, share_rows, 1)
    solutions = []
    stores = []
    for l in range(level_count):
        if l == 0:
            own = jnp.dot(
                rhs[0].astype(jnp.bfloat16), diag_inverses[0, 0], preferred_element_type=jnp.float32
            )
            rounded = own.astype(jnp.bfloat16)
        else:
            ids = descriptions[:, l - 1, :-1]
            counts = descriptions[:, l - 1, -1]
            store = stores[0] if l == 1 else jnp.concatenate(stores, axis=0)
            own, rounded = solve_level(ids, counts, store, factors[l - 1], rhs[l], diag_inverses[l, 0])
        solutions.append(own)
        if l < level_count - 1:
            stores.append(lax.all_gather(rounded, "rows", axis=0))
    return jnp.stack(solutions)[:, None]


def solution(mesh):
    return jax.shard_map(
        shards,
        mesh=mesh,
        in_specs=(
            P(None, "rows", None, None),
            P(None, "rows", "cols", None, None, None),
            P(None, "rows", None, None),
            P(None, "rows", "cols", None),
            P(None, "rows", "cols"),
        ),
        out_specs=P(None, "rows", "cols", None),
        check_vma=False,
    )
```

```python
import functools

import jax
import jax.numpy as jnp
from jax import lax
from jax.experimental import pallas as pl
from jax.experimental.pallas import tpu as pltpu
from jax.sharding import PartitionSpec as P

VMEM_LIMIT = 32 * 1024 * 1024


def gather_slots(ids_ref, counts_ref, place, group, store_ref, gathered, slots, width):
    for k in range(slots):
        piece = store_ref[place(ids_ref[group, k])]
        live = jnp.where(k < counts_ref[group], 1.0, 0.0).astype(piece.dtype)
        gathered[:, k * width:(k + 1) * width] = piece * live


def flat_dot(gathered, factor_ref):
    slots, width = factor_ref.shape[0], factor_ref.shape[1]
    return jnp.dot(
        gathered[...],
        factor_ref[...].reshape(slots * width, width),
        preferred_element_type=jnp.float32,
    )


def pair_kernel(levels, chips, own_ref, ids_ref, counts_ref, *refs):
    pieces = refs[:levels * chips]
    factor_refs = refs[levels * chips:levels * chips + 2]
    first_ref, second_ref, store, gathered = refs[levels * chips + 2:]
    slots, width = factor_refs[0].shape[0], factor_refs[0].shape[1]
    chip, flipped = own_ref[0], own_ref[1]
    for i, piece in enumerate(pieces):
        store[i] = piece[...]

    def place(source):
        level, rest = source // (2 * chips), source % (2 * chips)
        return level * chips + jnp.bitwise_xor(rest // 2, chip)

    sums = []
    for g in range(2):
        gather_slots(ids_ref, counts_ref, place, g, store, gathered, slots, width)
        sums.append(flat_dot(gathered, factor_refs[g]))
    first_ref[...] = jnp.where(flipped == 0, sums[0], sums[1])
    second_ref[...] = jnp.where(flipped == 0, sums[1], sums[0])


def pair_sums(own, ids, counts, pieces, factors, chips):
    rows, width = pieces[0].shape
    levels = len(pieces) // chips
    slots = factors[0].shape[0]
    vmem = pl.BlockSpec(memory_space=pltpu.VMEM)
    smem = pl.BlockSpec(memory_space=pltpu.SMEM)
    part = jax.ShapeDtypeStruct((rows, width), jnp.float32)
    return pl.pallas_call(
        functools.partial(pair_kernel, levels, chips),
        out_shape=(part, part),
        in_specs=[smem] * 3 + [vmem] * (len(pieces) + 2),
        out_specs=(vmem, vmem),
        scratch_shapes=[
            pltpu.VMEM((len(pieces), rows, width), jnp.bfloat16),
            pltpu.VMEM((rows, slots * width), jnp.bfloat16),
        ],
        compiler_params=pltpu.CompilerParams(vmem_limit_bytes=VMEM_LIMIT),
        cost_estimate=pl.CostEstimate(
            flops=4 * rows * width * width * slots,
            bytes_accessed=2 * slots * width * width * 2,
            transcendentals=0,
        ),
    )(own, ids, counts, *pieces, *factors)


def paired_shards(row_count, right_sides, factor_blocks, diag_inverses, source_ids, block_counts):
    level_count, _, rhs_count, width = right_sides.shape
    share_rows = rhs_count // 2
    chips = row_count // 2
    row, col = lax.axis_index("rows"), lax.axis_index("cols")
    chip, core = row // 2, row % 2

    def over_both(move):
        pairs = []
        for j in range(chips):
            for k in range(2):
                for c in range(2):
                    tj, tk, tc = move(j, k, c)
                    pairs.append(((2 * j + k) * 2 + c, (2 * tj + tk) * 2 + tc))
        return pairs

    def swap_core(x):
        return lax.ppermute(x, "rows", [(i, i ^ 1) for i in range(row_count)])

    def spread(x):
        return [
            lax.ppermute(x, ("rows", "cols"), over_both(lambda j, k, c, d=d: (j ^ d, c, k)))
            for d in range(chips)
        ]

    def collect(first, second):
        return [
            lax.ppermute(x, ("rows", "cols"), over_both(lambda j, k, c, e=e: (j, c ^ e, k)))
            for e, x in enumerate((first, second))
        ]

    described = jnp.concatenate([source_ids[:, 0, 0], block_counts[:, 0, 0][:, None]], axis=1)
    descriptions = jnp.stack([described, swap_core(described)])
    factors = [
        (factor_blocks[l, 0, 0], swap_core(factor_blocks[l, 0, 0])) for l in range(level_count - 1)
    ]
    own = jnp.stack([chip, jnp.bitwise_xor(core, col)]).astype(jnp.int32)

    rhs = lax.dynamic_slice_in_dim(right_sides[:, 0], col * share_rows, share_rows, 1)
    solutions = []
    pieces = []
    for l in range(level_count):
        reduced = rhs[l]
        if l > 0:
            ids = descriptions[:, l - 1, :-1]
            counts = descriptions[:, l - 1, -1]
            first, second = pair_sums(own, ids, counts, pieces, factors[l - 1], chips)
            arrived = collect(first, second)
            reduced = reduced - (arrived[0] + arrived[1])
        solved = jnp.dot(
            reduced.astype(jnp.bfloat16), diag_inverses[l, 0], preferred_element_type=jnp.float32
        )
        solutions.append(solved)
        if l < level_count - 1:
            pieces += spread(solved.astype(jnp.bfloat16))
    return jnp.stack(solutions)[:, None]


def level_kernel(groups, ids_ref, counts_ref, store_ref, *refs):
    factor_refs = refs[:groups]
    rhs_ref, inverse_ref, out_ref, rounded_ref, gathered = refs[groups:]
    slots, width = factor_refs[0].shape[0], factor_refs[0].shape[1]
    update = None
    for g in range(groups):
        gather_slots(ids_ref, counts_ref, lambda s: s, g, store_ref, gathered, slots, width)
        term = flat_dot(gathered, factor_refs[g])
        update = term if update is None else update + term
    reduced = (rhs_ref[...] - update).astype(jnp.bfloat16)
    solved = jnp.dot(reduced, inverse_ref[...], preferred_element_type=jnp.float32)
    out_ref[...] = solved
    rounded_ref[...] = solved.astype(jnp.bfloat16)


def solve_level(ids, counts, store, factors, rhs, inverse):
    groups = len(factors)
    rows, width = rhs.shape
    slots = factors[0].shape[0]
    vmem = pl.BlockSpec(memory_space=pltpu.VMEM)
    smem = pl.BlockSpec(memory_space=pltpu.SMEM)
    return pl.pallas_call(
        functools.partial(level_kernel, groups),
        out_shape=(
            jax.ShapeDtypeStruct((rows, width), jnp.float32),
            jax.ShapeDtypeStruct((rows, width), jnp.bfloat16),
        ),
        in_specs=[smem, smem, vmem] + [vmem] * groups + [vmem, vmem],
        out_specs=(vmem, vmem),
        scratch_shapes=[pltpu.VMEM((rows, slots * width), jnp.bfloat16)],
        compiler_params=pltpu.CompilerParams(vmem_limit_bytes=VMEM_LIMIT),
        cost_estimate=pl.CostEstimate(
            flops=2 * rows * width * width * (groups * slots + 1),
            bytes_accessed=groups * slots * width * width * 2,
            transcendentals=0,
        ),
    )(ids, counts, store, *factors, rhs, inverse)


def rotated_shards(col_count, right_sides, factor_blocks, diag_inverses, source_ids, block_counts):
    level_count, _, rhs_count, width = right_sides.shape
    share_rows = rhs_count // col_count
    col_index = lax.axis_index("cols")

    described = jnp.concatenate([source_ids[:, 0, 0], block_counts[:, 0, 0][:, None]], axis=1)
    factors = [[factor_blocks[l, 0, 0]] for l in range(level_count - 1)]
    descriptions = [described]
    for shift in range(1, col_count):
        pairs = [(i, (i + shift) % col_count) for i in range(col_count)]
        descriptions.append(lax.ppermute(described, "cols", pairs))
    for l in range(level_count - 1):
        for shift in range(1, col_count):
            pairs = [(i, (i + shift) % col_count) for i in range(col_count)]
            factors[l].append(lax.ppermute(factor_blocks[l, 0, 0], "cols", pairs))
    descriptions = jnp.stack(descriptions)

    rhs = lax.dynamic_slice_in_dim(right_sides[:, 0], col_index * share_rows, share_rows, 1)
    solutions = []
    stores = []
    for l in range(level_count):
        if l == 0:
            own = jnp.dot(
                rhs[0].astype(jnp.bfloat16), diag_inverses[0, 0], preferred_element_type=jnp.float32
            )
            rounded = own.astype(jnp.bfloat16)
        else:
            ids = descriptions[:, l - 1, :-1]
            counts = descriptions[:, l - 1, -1]
            store = stores[0] if l == 1 else jnp.concatenate(stores, axis=0)
            own, rounded = solve_level(ids, counts, store, factors[l - 1], rhs[l], diag_inverses[l, 0])
        solutions.append(own)
        if l < level_count - 1:
            stores.append(lax.all_gather(rounded, "rows", axis=0))
    return jnp.stack(solutions)[:, None]


def solution(mesh):
    row_count, col_count = mesh.shape["rows"], mesh.shape["cols"]
    chips = row_count // 2
    if col_count == 2 and row_count == 2 * chips and chips & (chips - 1) == 0:
        shards = functools.partial(paired_shards, row_count)
    else:
        shards = functools.partial(rotated_shards, col_count)
    return jax.shard_map(
        shards,
        mesh=mesh,
        in_specs=(
            P(None, "rows", None, None),
            P(None, "rows", "cols", None, None, None),
            P(None, "rows", None, None),
            P(None, "rows", "cols", None),
            P(None, "rows", "cols"),
        ),
        out_specs=P(None, "rows", "cols", None),
        check_vma=False,
    )
```

```python
import functools

import jax
import jax.numpy as jnp
from jax import lax
from jax.experimental import pallas as pl
from jax.experimental.pallas import tpu as pltpu
from jax.sharding import PartitionSpec as P

VMEM_LIMIT = 32 * 1024 * 1024


def gather_slots(ids_ref, counts_ref, place, group, store_ref, gathered, slots, width):
    for k in range(slots):
        piece = store_ref[place(ids_ref[group, k])]
        live = jnp.where(k < counts_ref[group], 1.0, 0.0).astype(piece.dtype)
        gathered[:, k * width:(k + 1) * width] = piece * live


def flat_dot(gathered, factor_ref):
    slots, width = factor_ref.shape[0], factor_ref.shape[1]
    return jnp.dot(
        gathered[...],
        factor_ref[...].reshape(slots * width, width),
        preferred_element_type=jnp.float32,
    )


def pair_kernel(level, chips, flipped_ref, ids_ref, counts_ref, *refs):
    store_refs = refs[:level]
    factor_refs = refs[level:level + 2]
    kept_ref, other_ref, store, gathered = refs[level + 2:]
    slots, width = factor_refs[0].shape[3], factor_refs[0].shape[4]
    for m, piece in enumerate(store_refs):
        store[m * chips:(m + 1) * chips] = piece[...]

    def place(source):
        return source // (2 * chips) * chips + source % (2 * chips) // 2

    sums = []
    for g in range(2):
        gather_slots(ids_ref, counts_ref, place, g, store, gathered, slots, width)
        sums.append(flat_dot(gathered, factor_refs[g].at[level - 1, 0, 0]))
    flipped = flipped_ref[0]
    kept_ref[...] = jnp.where(flipped == 0, sums[0], sums[1])
    other_ref[...] = jnp.where(flipped == 0, sums[1], sums[0])


def pair_sums(flipped, ids, counts, stores, factors):
    level = len(stores)
    chips, rows, width = stores[0].shape
    slots = factors[0].shape[3]
    vmem = pl.BlockSpec(memory_space=pltpu.VMEM)
    smem = pl.BlockSpec(memory_space=pltpu.SMEM)
    part = jax.ShapeDtypeStruct((rows, width), jnp.float32)
    return pl.pallas_call(
        functools.partial(pair_kernel, level, chips),
        out_shape=(part, part),
        in_specs=[smem] * 3 + [vmem] * (level + 2),
        out_specs=(vmem, vmem),
        scratch_shapes=[
            pltpu.VMEM((level * chips, rows, width), jnp.bfloat16),
            pltpu.VMEM((rows, slots * width), jnp.bfloat16),
        ],
        compiler_params=pltpu.CompilerParams(vmem_limit_bytes=VMEM_LIMIT),
        cost_estimate=pl.CostEstimate(
            flops=4 * rows * width * width * slots,
            bytes_accessed=2 * slots * width * width * 2,
            transcendentals=0,
        ),
    )(flipped, ids, counts, *stores, *factors)


def paired_shards(row_count, right_sides, factor_blocks, diag_inverses, source_ids, block_counts):
    level_count, _, rhs_count, width = right_sides.shape
    share_rows = rhs_count // 2
    chips = row_count // 2
    row, col = lax.axis_index("rows"), lax.axis_index("cols")
    core = row % 2
    flipped = jnp.bitwise_xor(core, col).astype(jnp.int32)
    same_core = [[2 * j + k for j in range(chips)] for k in range(2)]

    def over_both(x, move):
        pairs = []
        for j in range(chips):
            for k in range(2):
                for c in range(2):
                    tj, tk, tc = move(j, k, c)
                    pairs.append(((2 * j + k) * 2 + c, (2 * tj + tk) * 2 + tc))
        return lax.ppermute(x, ("rows", "cols"), pairs)

    def swap_core(x):
        return lax.ppermute(x, "rows", [(i, i ^ 1) for i in range(row_count)])

    def transpose(x):
        return over_both(x, lambda j, k, c: (j, c, k))

    def spread(x, level):
        if level == 1:
            return lax.all_gather(x, "rows", axis_index_groups=same_core)
        copies = jnp.broadcast_to(x[None], (chips,) + x.shape)
        return lax.all_to_all(copies, "rows", 0, 0, axis_index_groups=same_core)

    def half(x, index):
        return lax.dynamic_slice_in_dim(x, index * share_rows, share_rows, 1)

    rhs = half(right_sides[:, 0], col)
    solved = jnp.dot(
        rhs[0].astype(jnp.bfloat16), diag_inverses[0, 0], preferred_element_type=jnp.float32
    )
    solutions = [solved]
    stores = [spread(transpose(solved.astype(jnp.bfloat16)), 0)]

    described = jnp.concatenate([source_ids[:, 0, 0], block_counts[:, 0, 0][:, None]], axis=1)
    descriptions = jnp.stack([described, swap_core(described)])
    factors = (factor_blocks, swap_core(factor_blocks))
    inner = slice(1, level_count - 1)
    inner_rhs = jnp.where(
        flipped == 0, half(right_sides[inner, 0], core), swap_core(half(right_sides[inner, 0], 1 - core))
    )
    inner_inverses = jnp.where(
        flipped == 0, diag_inverses[inner, 0], swap_core(diag_inverses[inner, 0])
    )

    for l in range(1, level_count):
        ids = descriptions[:, l - 1, :-1]
        counts = descriptions[:, l - 1, -1]
        kept, other = pair_sums(flipped[None], ids, counts, stores, factors)
        if l < level_count - 1:
            arrived = lax.ppermute(other, "cols", [(0, 1), (1, 0)])
            reduced = inner_rhs[l - 1] - (kept + arrived)
            inverse = inner_inverses[l - 1]
        else:
            first = over_both(kept, lambda j, k, c: (j, c, k))
            second = over_both(other, lambda j, k, c: (j, 1 - c, k))
            reduced = rhs[l] - (first + second)
            inverse = diag_inverses[l, 0]
        solved = jnp.dot(
            reduced.astype(jnp.bfloat16), inverse, preferred_element_type=jnp.float32
        )
        if l < level_count - 1:
            stores.append(spread(solved.astype(jnp.bfloat16), l))
            solutions.append(transpose(solved))
        else:
            solutions.append(solved)
    return jnp.stack(solutions)[:, None]


def level_kernel(groups, ids_ref, counts_ref, store_ref, *refs):
    factor_refs = refs[:groups]
    rhs_ref, inverse_ref, out_ref, rounded_ref, gathered = refs[groups:]
    slots, width = factor_refs[0].shape[0], factor_refs[0].shape[1]
    update = None
    for g in range(groups):
        gather_slots(ids_ref, counts_ref, lambda s: s, g, store_ref, gathered, slots, width)
        term = flat_dot(gathered, factor_refs[g])
        update = term if update is None else update + term
    reduced = (rhs_ref[...] - update).astype(jnp.bfloat16)
    solved = jnp.dot(reduced, inverse_ref[...], preferred_element_type=jnp.float32)
    out_ref[...] = solved
    rounded_ref[...] = solved.astype(jnp.bfloat16)


def solve_level(ids, counts, store, factors, rhs, inverse):
    groups = len(factors)
    rows, width = rhs.shape
    slots = factors[0].shape[0]
    vmem = pl.BlockSpec(memory_space=pltpu.VMEM)
    smem = pl.BlockSpec(memory_space=pltpu.SMEM)
    return pl.pallas_call(
        functools.partial(level_kernel, groups),
        out_shape=(
            jax.ShapeDtypeStruct((rows, width), jnp.float32),
            jax.ShapeDtypeStruct((rows, width), jnp.bfloat16),
        ),
        in_specs=[smem, smem, vmem] + [vmem] * groups + [vmem, vmem],
        out_specs=(vmem, vmem),
        scratch_shapes=[pltpu.VMEM((rows, slots * width), jnp.bfloat16)],
        compiler_params=pltpu.CompilerParams(vmem_limit_bytes=VMEM_LIMIT),
        cost_estimate=pl.CostEstimate(
            flops=2 * rows * width * width * (groups * slots + 1),
            bytes_accessed=groups * slots * width * width * 2,
            transcendentals=0,
        ),
    )(ids, counts, store, *factors, rhs, inverse)


def rotated_shards(col_count, right_sides, factor_blocks, diag_inverses, source_ids, block_counts):
    level_count, _, rhs_count, width = right_sides.shape
    share_rows = rhs_count // col_count
    col_index = lax.axis_index("cols")

    described = jnp.concatenate([source_ids[:, 0, 0], block_counts[:, 0, 0][:, None]], axis=1)
    factors = [[factor_blocks[l, 0, 0]] for l in range(level_count - 1)]
    descriptions = [described]
    for shift in range(1, col_count):
        pairs = [(i, (i + shift) % col_count) for i in range(col_count)]
        descriptions.append(lax.ppermute(described, "cols", pairs))
    for l in range(level_count - 1):
        for shift in range(1, col_count):
            pairs = [(i, (i + shift) % col_count) for i in range(col_count)]
            factors[l].append(lax.ppermute(factor_blocks[l, 0, 0], "cols", pairs))
    descriptions = jnp.stack(descriptions)

    rhs = lax.dynamic_slice_in_dim(right_sides[:, 0], col_index * share_rows, share_rows, 1)
    solutions = []
    stores = []
    for l in range(level_count):
        if l == 0:
            own = jnp.dot(
                rhs[0].astype(jnp.bfloat16), diag_inverses[0, 0], preferred_element_type=jnp.float32
            )
            rounded = own.astype(jnp.bfloat16)
        else:
            ids = descriptions[:, l - 1, :-1]
            counts = descriptions[:, l - 1, -1]
            store = stores[0] if l == 1 else jnp.concatenate(stores, axis=0)
            own, rounded = solve_level(ids, counts, store, factors[l - 1], rhs[l], diag_inverses[l, 0])
        solutions.append(own)
        if l < level_count - 1:
            stores.append(lax.all_gather(rounded, "rows", axis=0))
    return jnp.stack(solutions)[:, None]


def solution(mesh):
    row_count, col_count = mesh.shape["rows"], mesh.shape["cols"]
    chips = row_count // 2
    if col_count == 2 and row_count == 2 * chips:
        shards = functools.partial(paired_shards, row_count)
    else:
        shards = functools.partial(rotated_shards, col_count)
    return jax.shard_map(
        shards,
        mesh=mesh,
        in_specs=(
            P(None, "rows", None, None),
            P(None, "rows", "cols", None, None, None),
            P(None, "rows", None, None),
            P(None, "rows", "cols", None),
            P(None, "rows", "cols"),
        ),
        out_specs=P(None, "rows", "cols", None),
        check_vma=False,
    )
```

```python
import functools

import jax
import jax.numpy as jnp
from jax import lax
from jax.experimental import pallas as pl
from jax.experimental.pallas import tpu as pltpu
from jax.sharding import PartitionSpec as P

VMEM_LIMIT = 32 * 1024 * 1024


VMEM = pl.BlockSpec(memory_space=pltpu.VMEM)
SMEM = pl.BlockSpec(memory_space=pltpu.SMEM)


def flat_dot(gathered, factor_ref):
    slots, width = factor_ref.shape[0], factor_ref.shape[1]
    return jnp.dot(
        gathered[...],
        factor_ref[...].reshape(slots * width, width),
        preferred_element_type=jnp.float32,
    )


def run(kernel, outs, args, scratch=(), flops=0, transferred=0):
    return pl.pallas_call(
        kernel,
        out_shape=outs,
        in_specs=[SMEM if x.dtype == jnp.int32 else VMEM for x in args],
        out_specs=jax.tree.map(lambda _: VMEM, outs),
        scratch_shapes=list(scratch),
        compiler_params=pltpu.CompilerParams(vmem_limit_bytes=VMEM_LIMIT),
        cost_estimate=pl.CostEstimate(flops=flops, bytes_accessed=transferred, transcendentals=0),
    )(*args)


def half_of(ref, level, half, rows):
    return ref[level, 0, pl.ds(pl.multiple_of(half * rows, rows), rows), :]


def solve(reduced, inverse):
    return jnp.dot(reduced.astype(jnp.bfloat16), inverse, preferred_element_type=jnp.float32)


def first_kernel(place_ref, rhs_ref, inverse_ref, out_ref, rounded_ref):
    rows = out_ref.shape[0]
    solved = solve(half_of(rhs_ref, 0, place_ref[1], rows), inverse_ref[0, 0])
    out_ref[...] = solved
    rounded_ref[...] = solved.astype(jnp.bfloat16)


def sums_kernel(level, chips, place_ref, ids_ref, other_ids_ref, *refs):
    store_refs = refs[:level]
    factor_refs = (refs[level], refs[level + 1].at[level - 1, 0, 0])
    kept_ref, sent_ref, store, gathered = refs[-4:]
    slots, width = factor_refs[0].shape[0], factor_refs[0].shape[1]
    for m, piece in enumerate(store_refs):
        store[m * chips:(m + 1) * chips] = piece[...]
    sums = []
    for ids, factor_ref in zip((ids_ref, other_ids_ref), factor_refs):
        for k in range(slots):
            source = ids[level - 1, 0, 0, k]
            known = jnp.maximum(source, 0)
            piece = store[known // (2 * chips) * chips + known % (2 * chips) // 2]
            live = jnp.where(source >= 0, 1.0, 0.0).astype(piece.dtype)
            gathered[:, k * width:(k + 1) * width] = piece * live
        sums.append(flat_dot(gathered, factor_ref))
    straight = place_ref[0] == place_ref[1]
    kept_ref[...] = jnp.where(straight, sums[0], sums[1])
    sent_ref[...] = jnp.where(straight, sums[1], sums[0])


def inner_kernel(level, place_ref, kept_ref, arrived_ref, rhs_ref, other_rhs_ref, inverse_ref, other_inverse_ref, out_ref, copies_ref):
    rows = out_ref.shape[0]
    core = place_ref[0]
    straight = core == place_ref[1]
    rhs = jnp.where(straight, half_of(rhs_ref, level, core, rows), half_of(other_rhs_ref, level, core, rows))
    inverse = jnp.where(straight, inverse_ref[level, 0], other_inverse_ref[level, 0])
    solved = solve(rhs - (kept_ref[...] + arrived_ref[...]), inverse)
    out_ref[...] = solved
    rounded = solved.astype(jnp.bfloat16)
    for i in range(copies_ref.shape[0]):
        copies_ref[i] = rounded


def last_kernel(place_ref, first_ref, second_ref, rhs_ref, inverse_ref, *refs):
    done_refs, out_ref = refs[:-1], refs[-1]
    rows, level = out_ref.shape[2], len(done_refs)
    for m, done in enumerate(done_refs):
        out_ref[m, 0] = done[...]
    rhs = half_of(rhs_ref, level, place_ref[1], rows)
    out_ref[level, 0] = solve(rhs - (first_ref[...] + second_ref[...]), inverse_ref[level, 0])


def paired_shards(row_count, right_sides, factor_blocks, diag_inverses, source_ids, block_counts):
    level_count, _, rhs_count, width = right_sides.shape
    slots = factor_blocks.shape[3]
    rows = rhs_count // 2
    chips = row_count // 2
    row, col = lax.axis_index("rows"), lax.axis_index("cols")
    place = jnp.stack([row % 2, col]).astype(jnp.int32)
    same_core = [[2 * j + k for j in range(chips)] for k in range(2)]
    part = jax.ShapeDtypeStruct((rows, width), jnp.float32)
    rounded_part = jax.ShapeDtypeStruct((rows, width), jnp.bfloat16)
    copies = jax.ShapeDtypeStruct((chips, rows, width), jnp.bfloat16)
    solve_flops = 2 * rows * width * width

    def over_both(x, move):
        pairs = []
        for j in range(chips):
            for k in range(2):
                for c in range(2):
                    tj, tk, tc = move(j, k, c)
                    pairs.append(((2 * j + k) * 2 + c, (2 * tj + tk) * 2 + tc))
        return lax.ppermute(x, ("rows", "cols"), pairs)

    def swap_core(x):
        return lax.ppermute(x, "rows", [(i, i ^ 1) for i in range(row_count)])

    def transpose(x):
        return over_both(x, lambda j, k, c: (j, c, k))

    def spread(x):
        return lax.all_to_all(x, "rows", 0, 0, axis_index_groups=same_core)

    solved, rounded = run(
        first_kernel, (part, rounded_part), (place, right_sides, diag_inverses), flops=solve_flops
    )
    finished = [solved]
    moved = transpose(rounded)
    stores = [spread(jnp.broadcast_to(moved[None], copies.shape))]

    live_ids = jnp.where(
        jnp.arange(slots, dtype=jnp.int32) < block_counts[..., None], source_ids, -1
    )
    other_factors = swap_core(factor_blocks)
    other_ids = swap_core(live_ids)
    other_inverses = swap_core(diag_inverses)
    other_rhs = swap_core(right_sides)

    for l in range(1, level_count):
        kept, sent = run(
            functools.partial(sums_kernel, l, chips),
            (part, part),
            (place, live_ids, other_ids, *stores, factor_blocks[l - 1, 0, 0], other_factors)
            + tuple(finished[1:]),
            scratch=(
                pltpu.VMEM((l * chips, rows, width), jnp.bfloat16),
                pltpu.VMEM((rows, slots * width), jnp.bfloat16),
            ),
            flops=2 * slots * solve_flops,
            transferred=2 * slots * width * width * 2,
        )
        if l < level_count - 1:
            arrived = lax.ppermute(sent, "cols", [(0, 1), (1, 0)])
            solved, copied = run(
                functools.partial(inner_kernel, l),
                (part, copies),
                (place, kept, arrived, right_sides, other_rhs, diag_inverses, other_inverses),
                flops=solve_flops,
            )
            finished.append(transpose(solved))
            stores.append(spread(copied))
        else:
            first = over_both(kept, lambda j, k, c: (j, c, k))
            second = over_both(sent, lambda j, k, c: (j, 1 - c, k))
            return run(
                last_kernel,
                jax.ShapeDtypeStruct((level_count, 1, rows, width), jnp.float32),
                (place, first, second, right_sides, diag_inverses, *finished),
                flops=solve_flops,
            )


def gather_slots(ids_ref, counts_ref, group, store_ref, gathered, slots, width):
    for k in range(slots):
        piece = store_ref[ids_ref[group, k]]
        live = jnp.where(k < counts_ref[group], 1.0, 0.0).astype(piece.dtype)
        gathered[:, k * width:(k + 1) * width] = piece * live


def level_kernel(groups, ids_ref, counts_ref, store_ref, *refs):
    factor_refs = refs[:groups]
    rhs_ref, inverse_ref, out_ref, rounded_ref, gathered = refs[groups:]
    slots, width = factor_refs[0].shape[0], factor_refs[0].shape[1]
    update = None
    for g in range(groups):
        gather_slots(ids_ref, counts_ref, g, store_ref, gathered, slots, width)
        term = flat_dot(gathered, factor_refs[g])
        update = term if update is None else update + term
    reduced = (rhs_ref[...] - update).astype(jnp.bfloat16)
    solved = jnp.dot(reduced, inverse_ref[...], preferred_element_type=jnp.float32)
    out_ref[...] = solved
    rounded_ref[...] = solved.astype(jnp.bfloat16)


def solve_level(ids, counts, store, factors, rhs, inverse):
    groups = len(factors)
    rows, width = rhs.shape
    slots = factors[0].shape[0]
    vmem = pl.BlockSpec(memory_space=pltpu.VMEM)
    smem = pl.BlockSpec(memory_space=pltpu.SMEM)
    return pl.pallas_call(
        functools.partial(level_kernel, groups),
        out_shape=(
            jax.ShapeDtypeStruct((rows, width), jnp.float32),
            jax.ShapeDtypeStruct((rows, width), jnp.bfloat16),
        ),
        in_specs=[smem, smem, vmem] + [vmem] * groups + [vmem, vmem],
        out_specs=(vmem, vmem),
        scratch_shapes=[pltpu.VMEM((rows, slots * width), jnp.bfloat16)],
        compiler_params=pltpu.CompilerParams(vmem_limit_bytes=VMEM_LIMIT),
        cost_estimate=pl.CostEstimate(
            flops=2 * rows * width * width * (groups * slots + 1),
            bytes_accessed=groups * slots * width * width * 2,
            transcendentals=0,
        ),
    )(ids, counts, store, *factors, rhs, inverse)


def rotated_shards(col_count, right_sides, factor_blocks, diag_inverses, source_ids, block_counts):
    level_count, _, rhs_count, width = right_sides.shape
    share_rows = rhs_count // col_count
    col_index = lax.axis_index("cols")

    described = jnp.concatenate([source_ids[:, 0, 0], block_counts[:, 0, 0][:, None]], axis=1)
    factors = [[factor_blocks[l, 0, 0]] for l in range(level_count - 1)]
    descriptions = [described]
    for shift in range(1, col_count):
        pairs = [(i, (i + shift) % col_count) for i in range(col_count)]
        descriptions.append(lax.ppermute(described, "cols", pairs))
    for l in range(level_count - 1):
        for shift in range(1, col_count):
            pairs = [(i, (i + shift) % col_count) for i in range(col_count)]
            factors[l].append(lax.ppermute(factor_blocks[l, 0, 0], "cols", pairs))
    descriptions = jnp.stack(descriptions)

    rhs = lax.dynamic_slice_in_dim(right_sides[:, 0], col_index * share_rows, share_rows, 1)
    solutions = []
    stores = []
    for l in range(level_count):
        if l == 0:
            own = jnp.dot(
                rhs[0].astype(jnp.bfloat16), diag_inverses[0, 0], preferred_element_type=jnp.float32
            )
            rounded = own.astype(jnp.bfloat16)
        else:
            ids = descriptions[:, l - 1, :-1]
            counts = descriptions[:, l - 1, -1]
            store = stores[0] if l == 1 else jnp.concatenate(stores, axis=0)
            own, rounded = solve_level(ids, counts, store, factors[l - 1], rhs[l], diag_inverses[l, 0])
        solutions.append(own)
        if l < level_count - 1:
            stores.append(lax.all_gather(rounded, "rows", axis=0))
    return jnp.stack(solutions)[:, None]


def solution(mesh):
    row_count, col_count = mesh.shape["rows"], mesh.shape["cols"]
    chips = row_count // 2
    if col_count == 2 and row_count == 2 * chips:
        shards = functools.partial(paired_shards, row_count)
    else:
        shards = functools.partial(rotated_shards, col_count)
    return jax.shard_map(
        shards,
        mesh=mesh,
        in_specs=(
            P(None, "rows", None, None),
            P(None, "rows", "cols", None, None, None),
            P(None, "rows", None, None),
            P(None, "rows", "cols", None),
            P(None, "rows", "cols"),
        ),
        out_specs=P(None, "rows", "cols", None),
        check_vma=False,
    )
```

```python
import functools

import jax
import jax.numpy as jnp
from jax import lax
from jax.experimental import pallas as pl
from jax.experimental.pallas import tpu as pltpu
from jax.sharding import PartitionSpec as P

VMEM_LIMIT = 16 * 1024 * 1024


VMEM = pl.BlockSpec(memory_space=pltpu.VMEM)
SMEM = pl.BlockSpec(memory_space=pltpu.SMEM)
ANY = pl.BlockSpec(memory_space=pl.ANY)
HBM = pl.BlockSpec(memory_space=pltpu.HBM)


def flat_dot(gathered, factor_ref):
    slots, width = factor_ref.shape[0], factor_ref.shape[1]
    return jnp.dot(
        gathered[...],
        factor_ref[...].reshape(slots * width, width),
        preferred_element_type=jnp.float32,
    )


def run(kernel, outs, args, scratch=(), flops=0, transferred=0):
    return pl.pallas_call(
        kernel,
        out_shape=tuple(pltpu.HBM(x.shape, x.dtype) if spec is HBM else x for x, spec in outs),
        in_specs=[spec for _, spec in args],
        out_specs=tuple(spec for _, spec in outs),
        scratch_shapes=list(scratch),
        compiler_params=pltpu.CompilerParams(vmem_limit_bytes=VMEM_LIMIT),
        cost_estimate=pl.CostEstimate(flops=flops, bytes_accessed=transferred, transcendentals=0),
    )(*(pltpu.with_memory_space_constraint(x, pltpu.HBM) if spec is HBM else x for x, spec in args))


def half_of(ref, level, half, rows):
    return ref.at[level, 0, pl.ds(pl.multiple_of(half * rows, rows), rows), :]


def solve(reduced, inverse):
    return jnp.dot(reduced.astype(jnp.bfloat16), inverse, preferred_element_type=jnp.float32)


def start_copies(pairs, sems):
    copies = [pltpu.make_async_copy(src, dst, sems.at[i]) for i, (src, dst) in enumerate(pairs)]
    for copy in copies:
        copy.start()
    return copies


def live_kernel(ids_ref, counts_ref, live_ids_ref):
    for l in range(ids_ref.shape[0]):
        for k in range(ids_ref.shape[3]):
            live = k < counts_ref[l, 0, 0]
            live_ids_ref[l, 0, 0, k] = jnp.where(live, ids_ref[l, 0, 0, k], -1)


def first_kernel(place_ref, rhs_ref, inverse_ref, out_ref, rounded_ref, rhs, inverse, sems):
    rows = out_ref.shape[0]
    copies = start_copies(
        [(half_of(rhs_ref, 0, place_ref[1], rows), rhs), (inverse_ref.at[0, 0], inverse)], sems
    )
    for copy in copies:
        copy.wait()
    solved = solve(rhs[...], inverse[...])
    out_ref[...] = solved
    rounded_ref[...] = solved.astype(jnp.bfloat16)


def sums_kernel(level, chips, inner, place_ref, ids_ref, other_ids_ref, *refs):
    store_refs = refs[:level]
    own_factor_ref, other_factor_ref, rhs_ref, other_rhs_ref, inverse_ref, other_inverse_ref = refs[level:level + 6]
    kept_ref, sent_ref, own_rhs_ref, own_inverse_ref = refs[-10:-6]
    store, gathered, own_factor, rhs, inverse, sems = refs[-6:]
    slots, width = own_factor.shape[0], own_factor.shape[1]
    rows = kept_ref.shape[0]
    core, col = place_ref[0], place_ref[1]
    straight = core == col
    if inner:
        pairs = [
            (half_of(rhs_ref, level, core, rows), rhs.at[0]),
            (half_of(other_rhs_ref, level, core, rows), rhs.at[1]),
            (inverse_ref.at[level, 0], inverse.at[0]),
            (other_inverse_ref.at[level, 0], inverse.at[1]),
        ]
    else:
        pairs = [
            (half_of(rhs_ref, level, col, rows), own_rhs_ref),
            (inverse_ref.at[level, 0], own_inverse_ref),
        ]
    copies = start_copies([(own_factor_ref.at[level - 1, 0, 0], own_factor)] + pairs, sems)
    for m, piece in enumerate(store_refs):
        store[m * chips:(m + 1) * chips] = piece[...]

    def group_sum(ids, factor_ref):
        for k in range(slots):
            source = ids[level - 1, 0, 0, k]
            known = jnp.maximum(source, 0)
            piece = store[known // (2 * chips) * chips + known % (2 * chips) // 2]
            live = jnp.where(source >= 0, 1.0, 0.0).astype(piece.dtype)
            gathered[:, k * width:(k + 1) * width] = piece * live
        return flat_dot(gathered, factor_ref)

    other = group_sum(other_ids_ref, other_factor_ref.at[level - 1, 0, 0])
    copies[0].wait()
    own = group_sum(ids_ref, own_factor)
    kept_ref[...] = jnp.where(straight, own, other)
    sent_ref[...] = jnp.where(straight, other, own)
    for copy in copies[1:]:
        copy.wait()
    if inner:
        own_rhs_ref[...] = jnp.where(straight, rhs[0], rhs[1])
        own_inverse_ref[...] = jnp.where(straight, inverse[0], inverse[1])


def copies_kernel(rounded_ref, copies_ref, sems):
    for copy in start_copies([(rounded_ref, copies_ref.at[i]) for i in range(copies_ref.shape[0])], sems):
        copy.wait()


def inner_kernel(kept_ref, arrived_ref, rhs_ref, inverse_ref, out_ref, copies_ref, rounded, sems):
    solved = solve(rhs_ref[...] - (kept_ref[...] + arrived_ref[...]), inverse_ref[...])
    rounded[...] = solved.astype(jnp.bfloat16)
    copies = start_copies([(rounded, copies_ref.at[i]) for i in range(copies_ref.shape[0])], sems)
    out_ref[...] = solved
    for copy in copies:
        copy.wait()


def last_kernel(first_ref, second_ref, rhs_ref, inverse_ref, *refs):
    done_refs, out_ref = refs[:-1], refs[-1]
    for m, done in enumerate(done_refs):
        out_ref[m, 0] = done[...]
    solved = solve(rhs_ref[...] - (first_ref[...] + second_ref[...]), inverse_ref[...])
    out_ref[len(done_refs), 0] = solved


def paired_shards(row_count, right_sides, factor_blocks, diag_inverses, source_ids, block_counts):
    level_count, _, rhs_count, width = right_sides.shape
    slots = factor_blocks.shape[3]
    rows = rhs_count // 2
    chips = row_count // 2
    row, col = lax.axis_index("rows"), lax.axis_index("cols")
    place = jnp.stack([row % 2, col]).astype(jnp.int32)
    same_core = [[2 * j + k for j in range(chips)] for k in range(2)]
    part = jax.ShapeDtypeStruct((rows, width), jnp.float32)
    rounded_part = jax.ShapeDtypeStruct((rows, width), jnp.bfloat16)
    square = jax.ShapeDtypeStruct((width, width), jnp.bfloat16)
    copies = jax.ShapeDtypeStruct((chips, rows, width), jnp.bfloat16)
    solve_flops = 2 * rows * width * width

    def over_both(x, move):
        pairs = []
        for j in range(chips):
            for k in range(2):
                for c in range(2):
                    tj, tk, tc = move(j, k, c)
                    pairs.append(((2 * j + k) * 2 + c, (2 * tj + tk) * 2 + tc))
        return lax.ppermute(x, ("rows", "cols"), pairs)

    def swap_core(x):
        return lax.ppermute(x, "rows", [(i, i ^ 1) for i in range(row_count)])

    def transpose(x):
        return over_both(x, lambda j, k, c: (j, c, k))

    def spread(x):
        return lax.all_to_all(x, "rows", 0, 0, axis_index_groups=same_core)

    solved, rounded = run(
        first_kernel,
        ((part, VMEM), (rounded_part, VMEM)),
        ((place, SMEM), (right_sides, HBM), (diag_inverses, HBM)),
        scratch=(
            pltpu.VMEM(part.shape, part.dtype),
            pltpu.VMEM(square.shape, square.dtype),
            pltpu.SemaphoreType.DMA((2,)),
        ),
        flops=solve_flops,
    )
    finished = [solved]
    moved = transpose(rounded)
    copied, = run(
        copies_kernel,
        ((copies, HBM),),
        ((moved, VMEM),),
        scratch=(pltpu.SemaphoreType.DMA((chips,)),),
    )
    stores = [spread(copied)]

    live_ids, = run(
        live_kernel,
        ((jax.ShapeDtypeStruct(source_ids.shape, source_ids.dtype), SMEM),),
        ((source_ids, SMEM), (block_counts, SMEM)),
    )
    other_factors = swap_core(factor_blocks)
    other_ids = swap_core(live_ids)
    other_inverses = swap_core(diag_inverses)
    other_rhs = swap_core(right_sides)

    for l in range(1, level_count):
        inner = l < level_count - 1
        kept, sent, rhs, inverse = run(
            functools.partial(sums_kernel, l, chips, inner),
            ((part, VMEM), (part, VMEM), (part, VMEM), (square, VMEM)),
            ((place, SMEM), (live_ids, SMEM), (other_ids, SMEM))
            + tuple((store, VMEM) for store in stores)
            + ((factor_blocks, HBM), (other_factors, VMEM))
            + ((right_sides, HBM), (other_rhs, ANY), (diag_inverses, HBM), (other_inverses, ANY))
            + tuple((x, ANY) for x in finished[1:]),
            scratch=(
                pltpu.VMEM((l * chips, rows, width), jnp.bfloat16),
                pltpu.VMEM((rows, slots * width), jnp.bfloat16),
                pltpu.VMEM((slots, width, width), jnp.bfloat16),
                pltpu.VMEM((2, rows, width), jnp.float32),
                pltpu.VMEM((2, width, width), jnp.bfloat16),
                pltpu.SemaphoreType.DMA((5,)),
            ),
            flops=2 * slots * solve_flops,
            transferred=2 * slots * width * width * 2,
        )
        if inner:
            arrived = lax.ppermute(sent, "cols", [(0, 1), (1, 0)])
            solved, copied = run(
                inner_kernel,
                ((part, VMEM), (copies, HBM)),
                ((kept, VMEM), (arrived, VMEM), (rhs, VMEM), (inverse, VMEM)),
                scratch=(
                    pltpu.VMEM((rows, width), jnp.bfloat16),
                    pltpu.SemaphoreType.DMA((chips,)),
                ),
                flops=solve_flops,
            )
            finished.append(transpose(solved))
            stores.append(spread(copied))
        else:
            first = over_both(kept, lambda j, k, c: (j, c, k))
            second = over_both(sent, lambda j, k, c: (j, 1 - c, k))
            out = jax.ShapeDtypeStruct((level_count, 1, rows, width), jnp.float32)
            return run(
                last_kernel,
                ((out, VMEM),),
                tuple((x, VMEM) for x in (first, second, rhs, inverse, *finished)),
                flops=solve_flops,
            )[0]


def gather_slots(ids_ref, counts_ref, group, store_ref, gathered, slots, width):
    for k in range(slots):
        piece = store_ref[ids_ref[group, k]]
        live = jnp.where(k < counts_ref[group], 1.0, 0.0).astype(piece.dtype)
        gathered[:, k * width:(k + 1) * width] = piece * live


def level_kernel(groups, ids_ref, counts_ref, store_ref, *refs):
    factor_refs = refs[:groups]
    rhs_ref, inverse_ref, out_ref, rounded_ref, gathered = refs[groups:]
    slots, width = factor_refs[0].shape[0], factor_refs[0].shape[1]
    update = None
    for g in range(groups):
        gather_slots(ids_ref, counts_ref, g, store_ref, gathered, slots, width)
        term = flat_dot(gathered, factor_refs[g])
        update = term if update is None else update + term
    reduced = (rhs_ref[...] - update).astype(jnp.bfloat16)
    solved = jnp.dot(reduced, inverse_ref[...], preferred_element_type=jnp.float32)
    out_ref[...] = solved
    rounded_ref[...] = solved.astype(jnp.bfloat16)


def solve_level(ids, counts, store, factors, rhs, inverse):
    groups = len(factors)
    rows, width = rhs.shape
    slots = factors[0].shape[0]
    vmem = pl.BlockSpec(memory_space=pltpu.VMEM)
    smem = pl.BlockSpec(memory_space=pltpu.SMEM)
    return pl.pallas_call(
        functools.partial(level_kernel, groups),
        out_shape=(
            jax.ShapeDtypeStruct((rows, width), jnp.float32),
            jax.ShapeDtypeStruct((rows, width), jnp.bfloat16),
        ),
        in_specs=[smem, smem, vmem] + [vmem] * groups + [vmem, vmem],
        out_specs=(vmem, vmem),
        scratch_shapes=[pltpu.VMEM((rows, slots * width), jnp.bfloat16)],
        compiler_params=pltpu.CompilerParams(vmem_limit_bytes=VMEM_LIMIT),
        cost_estimate=pl.CostEstimate(
            flops=2 * rows * width * width * (groups * slots + 1),
            bytes_accessed=groups * slots * width * width * 2,
            transcendentals=0,
        ),
    )(ids, counts, store, *factors, rhs, inverse)


def rotated_shards(col_count, right_sides, factor_blocks, diag_inverses, source_ids, block_counts):
    level_count, _, rhs_count, width = right_sides.shape
    share_rows = rhs_count // col_count
    col_index = lax.axis_index("cols")

    described = jnp.concatenate([source_ids[:, 0, 0], block_counts[:, 0, 0][:, None]], axis=1)
    factors = [[factor_blocks[l, 0, 0]] for l in range(level_count - 1)]
    descriptions = [described]
    for shift in range(1, col_count):
        pairs = [(i, (i + shift) % col_count) for i in range(col_count)]
        descriptions.append(lax.ppermute(described, "cols", pairs))
    for l in range(level_count - 1):
        for shift in range(1, col_count):
            pairs = [(i, (i + shift) % col_count) for i in range(col_count)]
            factors[l].append(lax.ppermute(factor_blocks[l, 0, 0], "cols", pairs))
    descriptions = jnp.stack(descriptions)

    rhs = lax.dynamic_slice_in_dim(right_sides[:, 0], col_index * share_rows, share_rows, 1)
    solutions = []
    stores = []
    for l in range(level_count):
        if l == 0:
            own = jnp.dot(
                rhs[0].astype(jnp.bfloat16), diag_inverses[0, 0], preferred_element_type=jnp.float32
            )
            rounded = own.astype(jnp.bfloat16)
        else:
            ids = descriptions[:, l - 1, :-1]
            counts = descriptions[:, l - 1, -1]
            store = stores[0] if l == 1 else jnp.concatenate(stores, axis=0)
            own, rounded = solve_level(ids, counts, store, factors[l - 1], rhs[l], diag_inverses[l, 0])
        solutions.append(own)
        if l < level_count - 1:
            stores.append(lax.all_gather(rounded, "rows", axis=0))
    return jnp.stack(solutions)[:, None]


def solution(mesh):
    row_count, col_count = mesh.shape["rows"], mesh.shape["cols"]
    chips = row_count // 2
    if col_count == 2 and row_count == 2 * chips:
        shards = functools.partial(paired_shards, row_count)
    else:
        shards = functools.partial(rotated_shards, col_count)
    return jax.shard_map(
        shards,
        mesh=mesh,
        in_specs=(
            P(None, "rows", None, None),
            P(None, "rows", "cols", None, None, None),
            P(None, "rows", None, None),
            P(None, "rows", "cols", None),
            P(None, "rows", "cols"),
        ),
        out_specs=P(None, "rows", "cols", None),
        check_vma=False,
    )
```

```python
import functools

import jax
import jax.numpy as jnp
from jax import lax
from jax.experimental import pallas as pl
from jax.experimental.pallas import tpu as pltpu
from jax.sharding import PartitionSpec as P

VMEM_LIMIT = 16 * 1024 * 1024


VMEM = pl.BlockSpec(memory_space=pltpu.VMEM)
SMEM = pl.BlockSpec(memory_space=pltpu.SMEM)
ANY = pl.BlockSpec(memory_space=pl.ANY)
HBM = pl.BlockSpec(memory_space=pltpu.HBM)


def flat_dot(gathered, factor_ref):
    slots, width = factor_ref.shape[0], factor_ref.shape[1]
    return jnp.dot(
        gathered[...],
        factor_ref[...].reshape(slots * width, width),
        preferred_element_type=jnp.float32,
    )


def run(kernel, outs, args, scratch=(), flops=0, transferred=0):
    return pl.pallas_call(
        kernel,
        out_shape=tuple(pltpu.HBM(x.shape, x.dtype) if spec is HBM else x for x, spec in outs),
        in_specs=[spec for _, spec in args],
        out_specs=tuple(spec for _, spec in outs),
        scratch_shapes=list(scratch),
        compiler_params=pltpu.CompilerParams(vmem_limit_bytes=VMEM_LIMIT),
        cost_estimate=pl.CostEstimate(flops=flops, bytes_accessed=transferred, transcendentals=0),
    )(*(pltpu.with_memory_space_constraint(x, pltpu.HBM) if spec is HBM else x for x, spec in args))


def half_of(ref, level, half, rows):
    return ref.at[level, 0, pl.ds(pl.multiple_of(half * rows, rows), rows), :]


def solve(reduced, inverse):
    return jnp.dot(reduced.astype(jnp.bfloat16), inverse, preferred_element_type=jnp.float32)


def start_copies(pairs, sems):
    copies = [pltpu.make_async_copy(src, dst, sems.at[i]) for i, (src, dst) in enumerate(pairs)]
    for copy in copies:
        copy.start()
    return copies


def own_place():
    return lax.rem(lax.axis_index("rows"), 2), lax.axis_index("cols")


def first_kernel(rhs_ref, inverse_ref, out_ref, rounded_ref, rhs, inverse, sems):
    _, col = own_place()
    copies = start_copies(
        [(half_of(rhs_ref, 0, col, out_ref.shape[0]), rhs), (inverse_ref.at[0, 0], inverse)], sems
    )
    for copy in copies:
        copy.wait()
    solved = solve(rhs[...], inverse[...])
    out_ref[...] = solved
    rounded_ref[...] = solved.astype(jnp.bfloat16)


def copies_kernel(rounded_ref, copies_ref, sems):
    for copy in start_copies([(rounded_ref, copies_ref.at[i]) for i in range(copies_ref.shape[0])], sems):
        copy.wait()


def stage_kernel(
    factor_ref, rhs_ref, other_rhs_ref, inverse_ref, other_inverse_ref,
    own_factor_ref, own_rhs_ref, own_inverse_ref, rhs, inverse, sems,
):
    core, col = own_place()
    straight = core == col
    levels, rows = own_rhs_ref.shape[0], own_rhs_ref.shape[1]
    pairs = [
        (factor_ref.at[:, 0, 0], own_factor_ref),
        (half_of(rhs_ref, levels, col, rows), own_rhs_ref.at[levels - 1]),
        (inverse_ref.at[levels, 0], own_inverse_ref.at[levels - 1]),
    ]
    for l in range(1, levels):
        pairs += [
            (half_of(rhs_ref, l, core, rows), rhs.at[0, l - 1]),
            (half_of(other_rhs_ref, l, core, rows), rhs.at[1, l - 1]),
            (inverse_ref.at[l, 0], inverse.at[0, l - 1]),
            (other_inverse_ref.at[l, 0], inverse.at[1, l - 1]),
        ]
    for copy in start_copies(pairs, sems):
        copy.wait()
    for l in range(levels - 1):
        own_rhs_ref[l] = jnp.where(straight, rhs[0, l], rhs[1, l])
        own_inverse_ref[l] = jnp.where(straight, inverse[0, l], inverse[1, l])


def sums_kernel(level, chips, ids_ref, other_ids_ref, counts_ref, other_counts_ref, *refs):
    store_refs = refs[:level]
    factor_refs = (refs[level].at[level - 1], refs[level + 1].at[level - 1, 0, 0])
    kept_ref, sent_ref, store, gathered = refs[-4:]
    slots, width = factor_refs[0].shape[0], factor_refs[0].shape[1]
    core, col = own_place()
    for m, piece in enumerate(store_refs):
        store[m * chips:(m + 1) * chips] = piece[...]
    sums = []
    for ids, counts, factor_ref in zip((ids_ref, other_ids_ref), (counts_ref, other_counts_ref), factor_refs):
        for k in range(slots):
            source = ids[level - 1, 0, 0, k]
            piece = store[source // (2 * chips) * chips + source % (2 * chips) // 2]
            live = jnp.where(k < counts[level - 1], 1.0, 0.0).astype(piece.dtype)
            gathered[:, k * width:(k + 1) * width] = piece * live
        sums.append(flat_dot(gathered, factor_ref))
    straight = core == col
    kept_ref[...] = jnp.where(straight, sums[0], sums[1])
    sent_ref[...] = jnp.where(straight, sums[1], sums[0])


def inner_kernel(level, kept_ref, arrived_ref, rhs_ref, inverse_ref, out_ref, copies_ref, rounded, sems):
    solved = solve(rhs_ref[level - 1] - (kept_ref[...] + arrived_ref[...]), inverse_ref[level - 1])
    rounded[...] = solved.astype(jnp.bfloat16)
    copies = start_copies([(rounded, copies_ref.at[i]) for i in range(copies_ref.shape[0])], sems)
    out_ref[...] = solved
    for copy in copies:
        copy.wait()


def last_kernel(first_ref, second_ref, rhs_ref, inverse_ref, *refs):
    done_refs, out_ref = refs[:-1], refs[-1]
    level = len(done_refs)
    for m, done in enumerate(done_refs):
        out_ref[m, 0] = done[...]
    solved = solve(rhs_ref[level - 1] - (first_ref[...] + second_ref[...]), inverse_ref[level - 1])
    out_ref[level, 0] = solved


def paired_shards(row_count, right_sides, factor_blocks, diag_inverses, source_ids, block_counts):
    level_count, _, rhs_count, width = right_sides.shape
    slots = factor_blocks.shape[3]
    rows = rhs_count // 2
    chips = row_count // 2
    later = level_count - 1
    same_core = [[2 * j + k for j in range(chips)] for k in range(2)]
    part = jax.ShapeDtypeStruct((rows, width), jnp.float32)
    rounded_part = jax.ShapeDtypeStruct((rows, width), jnp.bfloat16)
    copies = jax.ShapeDtypeStruct((chips, rows, width), jnp.bfloat16)
    solve_flops = 2 * rows * width * width

    def over_both(x, move):
        pairs = []
        for j in range(chips):
            for k in range(2):
                for c in range(2):
                    tj, tk, tc = move(j, k, c)
                    pairs.append(((2 * j + k) * 2 + c, (2 * tj + tk) * 2 + tc))
        return lax.ppermute(x, ("rows", "cols"), pairs)

    def swap_core(x):
        return lax.ppermute(x, "rows", [(i, i ^ 1) for i in range(row_count)])

    def transpose(x):
        return over_both(x, lambda j, k, c: (j, c, k))

    def spread(x):
        return lax.all_to_all(x, "rows", 0, 0, axis_index_groups=same_core)

    solved, rounded = run(
        first_kernel,
        ((part, VMEM), (rounded_part, VMEM)),
        ((right_sides, HBM), (diag_inverses, HBM)),
        scratch=(
            pltpu.VMEM((rows, width), jnp.float32),
            pltpu.VMEM((width, width), jnp.bfloat16),
            pltpu.SemaphoreType.DMA((2,)),
        ),
        flops=solve_flops,
    )
    finished = [solved]
    copied, = run(
        copies_kernel,
        ((copies, HBM),),
        ((transpose(rounded), VMEM),),
        scratch=(pltpu.SemaphoreType.DMA((chips,)),),
    )
    stores = [spread(copied)]

    counts = block_counts.reshape(later)
    slot_args = tuple((x, SMEM) for x in (source_ids, swap_core(source_ids), counts, swap_core(counts)))
    other_factors = swap_core(factor_blocks)
    own_factors, rhs, inverses = run(
        stage_kernel,
        (
            (jax.ShapeDtypeStruct((later, slots, width, width), jnp.bfloat16), VMEM),
            (jax.ShapeDtypeStruct((later, rows, width), jnp.float32), VMEM),
            (jax.ShapeDtypeStruct((later, width, width), jnp.bfloat16), VMEM),
        ),
        (
            (factor_blocks, HBM),
            (right_sides, HBM),
            (swap_core(right_sides), ANY),
            (diag_inverses, HBM),
            (swap_core(diag_inverses), ANY),
        ),
        scratch=(
            pltpu.VMEM((2, later - 1, rows, width), jnp.float32),
            pltpu.VMEM((2, later - 1, width, width), jnp.bfloat16),
            pltpu.SemaphoreType.DMA((3 + 4 * (later - 1),)),
        ),
        transferred=2 * later * slots * width * width * 2,
    )

    for l in range(1, level_count):
        kept, sent = run(
            functools.partial(sums_kernel, l, chips),
            ((part, VMEM), (part, VMEM)),
            slot_args
            + tuple((store, VMEM) for store in stores)
            + ((own_factors, VMEM), (other_factors, VMEM))
            + tuple((x, ANY) for x in finished[1:]),
            scratch=(
                pltpu.VMEM((l * chips, rows, width), jnp.bfloat16),
                pltpu.VMEM((rows, slots * width), jnp.bfloat16),
            ),
            flops=2 * slots * solve_flops,
            transferred=2 * slots * width * width * 2,
        )
        if l < later:
            arrived = lax.ppermute(sent, "cols", [(0, 1), (1, 0)])
            solved, copied = run(
                functools.partial(inner_kernel, l),
                ((part, VMEM), (copies, HBM)),
                ((kept, VMEM), (arrived, VMEM), (rhs, VMEM), (inverses, VMEM)),
                scratch=(
                    pltpu.VMEM((rows, width), jnp.bfloat16),
                    pltpu.SemaphoreType.DMA((chips,)),
                ),
                flops=solve_flops,
            )
            finished.append(transpose(solved))
            stores.append(spread(copied))
    first = over_both(kept, lambda j, k, c: (j, c, k))
    second = over_both(sent, lambda j, k, c: (j, 1 - c, k))
    out, = run(
        last_kernel,
        ((jax.ShapeDtypeStruct((level_count, 1, rows, width), jnp.float32), VMEM),),
        tuple((x, VMEM) for x in (first, second, rhs, inverses, *finished)),
        flops=solve_flops,
    )
    return out


def gather_slots(ids_ref, counts_ref, group, store_ref, gathered, slots, width):
    for k in range(slots):
        piece = store_ref[ids_ref[group, k]]
        live = jnp.where(k < counts_ref[group], 1.0, 0.0).astype(piece.dtype)
        gathered[:, k * width:(k + 1) * width] = piece * live


def level_kernel(groups, ids_ref, counts_ref, store_ref, *refs):
    factor_refs = refs[:groups]
    rhs_ref, inverse_ref, out_ref, rounded_ref, gathered = refs[groups:]
    slots, width = factor_refs[0].shape[0], factor_refs[0].shape[1]
    update = None
    for g in range(groups):
        gather_slots(ids_ref, counts_ref, g, store_ref, gathered, slots, width)
        term = flat_dot(gathered, factor_refs[g])
        update = term if update is None else update + term
    reduced = (rhs_ref[...] - update).astype(jnp.bfloat16)
    solved = jnp.dot(reduced, inverse_ref[...], preferred_element_type=jnp.float32)
    out_ref[...] = solved
    rounded_ref[...] = solved.astype(jnp.bfloat16)


def solve_level(ids, counts, store, factors, rhs, inverse):
    groups = len(factors)
    rows, width = rhs.shape
    slots = factors[0].shape[0]
    vmem = pl.BlockSpec(memory_space=pltpu.VMEM)
    smem = pl.BlockSpec(memory_space=pltpu.SMEM)
    return pl.pallas_call(
        functools.partial(level_kernel, groups),
        out_shape=(
            jax.ShapeDtypeStruct((rows, width), jnp.float32),
            jax.ShapeDtypeStruct((rows, width), jnp.bfloat16),
        ),
        in_specs=[smem, smem, vmem] + [vmem] * groups + [vmem, vmem],
        out_specs=(vmem, vmem),
        scratch_shapes=[pltpu.VMEM((rows, slots * width), jnp.bfloat16)],
        compiler_params=pltpu.CompilerParams(vmem_limit_bytes=VMEM_LIMIT),
        cost_estimate=pl.CostEstimate(
            flops=2 * rows * width * width * (groups * slots + 1),
            bytes_accessed=groups * slots * width * width * 2,
            transcendentals=0,
        ),
    )(ids, counts, store, *factors, rhs, inverse)


def rotated_shards(col_count, right_sides, factor_blocks, diag_inverses, source_ids, block_counts):
    level_count, _, rhs_count, width = right_sides.shape
    share_rows = rhs_count // col_count
    col_index = lax.axis_index("cols")

    described = jnp.concatenate([source_ids[:, 0, 0], block_counts[:, 0, 0][:, None]], axis=1)
    factors = [[factor_blocks[l, 0, 0]] for l in range(level_count - 1)]
    descriptions = [described]
    for shift in range(1, col_count):
        pairs = [(i, (i + shift) % col_count) for i in range(col_count)]
        descriptions.append(lax.ppermute(described, "cols", pairs))
    for l in range(level_count - 1):
        for shift in range(1, col_count):
            pairs = [(i, (i + shift) % col_count) for i in range(col_count)]
            factors[l].append(lax.ppermute(factor_blocks[l, 0, 0], "cols", pairs))
    descriptions = jnp.stack(descriptions)

    rhs = lax.dynamic_slice_in_dim(right_sides[:, 0], col_index * share_rows, share_rows, 1)
    solutions = []
    stores = []
    for l in range(level_count):
        if l == 0:
            own = jnp.dot(
                rhs[0].astype(jnp.bfloat16), diag_inverses[0, 0], preferred_element_type=jnp.float32
            )
            rounded = own.astype(jnp.bfloat16)
        else:
            ids = descriptions[:, l - 1, :-1]
            counts = descriptions[:, l - 1, -1]
            store = stores[0] if l == 1 else jnp.concatenate(stores, axis=0)
            own, rounded = solve_level(ids, counts, store, factors[l - 1], rhs[l], diag_inverses[l, 0])
        solutions.append(own)
        if l < level_count - 1:
            stores.append(lax.all_gather(rounded, "rows", axis=0))
    return jnp.stack(solutions)[:, None]


def solution(mesh):
    row_count, col_count = mesh.shape["rows"], mesh.shape["cols"]
    chips = row_count // 2
    if col_count == 2 and row_count == 2 * chips:
        shards = functools.partial(paired_shards, row_count)
    else:
        shards = functools.partial(rotated_shards, col_count)
    return jax.shard_map(
        shards,
        mesh=mesh,
        in_specs=(
            P(None, "rows", None, None),
            P(None, "rows", "cols", None, None, None),
            P(None, "rows", None, None),
            P(None, "rows", "cols", None),
            P(None, "rows", "cols"),
        ),
        out_specs=P(None, "rows", "cols", None),
        check_vma=False,
    )
```

```python
import functools

import jax
import jax.numpy as jnp
from jax import lax
from jax.experimental import pallas as pl
from jax.experimental.pallas import tpu as pltpu
from jax.sharding import PartitionSpec as P

VMEM_LIMIT = 16 * 1024 * 1024


VMEM = pl.BlockSpec(memory_space=pltpu.VMEM)
SMEM = pl.BlockSpec(memory_space=pltpu.SMEM)
ANY = pl.BlockSpec(memory_space=pl.ANY)
HBM = pl.BlockSpec(memory_space=pltpu.HBM)
FIXED = pl.BlockSpec(memory_space=pltpu.VMEM)
PLACES = {id(HBM): pltpu.HBM, id(FIXED): pltpu.VMEM}


def flat_dot(gathered, factor_ref):
    slots, width = factor_ref.shape[0], factor_ref.shape[1]
    return jnp.dot(
        gathered[...],
        factor_ref[...].reshape(slots * width, width),
        preferred_element_type=jnp.float32,
    )


def run(kernel, outs, args, scratch=(), flops=0, transferred=0):
    out_shape = tuple(PLACES[id(spec)](x.shape, x.dtype) if id(spec) in PLACES else x for x, spec in outs)
    args = tuple(
        (pltpu.with_memory_space_constraint(x, PLACES[id(spec)]) if id(spec) in PLACES else x, spec)
        for x, spec in args
    )
    return pl.pallas_call(
        kernel,
        out_shape=out_shape,
        in_specs=[spec for _, spec in args],
        out_specs=tuple(spec for _, spec in outs),
        scratch_shapes=list(scratch),
        compiler_params=pltpu.CompilerParams(vmem_limit_bytes=VMEM_LIMIT),
        cost_estimate=pl.CostEstimate(flops=flops, bytes_accessed=transferred, transcendentals=0),
    )(*(x for x, _ in args))


def half_of(ref, level, half, rows):
    return ref.at[level, 0, pl.ds(pl.multiple_of(half * rows, rows), rows), :]


def solve(reduced, inverse):
    return jnp.dot(reduced.astype(jnp.bfloat16), inverse, preferred_element_type=jnp.float32)


def start_copies(pairs, sems):
    copies = [pltpu.make_async_copy(src, dst, sems.at[i]) for i, (src, dst) in enumerate(pairs)]
    for copy in copies:
        copy.start()
    return copies


def own_place():
    return lax.rem(lax.axis_index("rows"), 2), lax.axis_index("cols")


def first_kernel(rhs_ref, inverse_ref, out_ref, rounded_ref, rhs, inverse, sems):
    _, col = own_place()
    copies = start_copies(
        [(half_of(rhs_ref, 0, col, out_ref.shape[0]), rhs), (inverse_ref.at[0, 0], inverse)], sems
    )
    for copy in copies:
        copy.wait()
    solved = solve(rhs[...], inverse[...])
    out_ref[...] = solved
    rounded_ref[...] = solved.astype(jnp.bfloat16)


def copies_kernel(rounded_ref, copies_ref):
    for i in range(copies_ref.shape[0]):
        copies_ref[i] = rounded_ref[...]


def slot_sum(level, store_level, chips, ids_ref, counts_ref, store_ref, factor_ref, gathered):
    slots, width = factor_ref.shape[0], factor_ref.shape[1]
    for k in range(slots):
        source = ids_ref[level - 1, 0, 0, k]
        source_level, place = source // (2 * chips), source % (2 * chips) // 2
        live = k < counts_ref[level - 1]
        if store_level is None:
            live = jnp.logical_and(live, source_level < level - 1)
            place = jnp.minimum(source_level, level - 2) * chips + place
        else:
            live = jnp.logical_and(live, source_level == store_level)
        piece = store_ref[place]
        gathered[:, k * width:(k + 1) * width] = piece * jnp.where(live, 1.0, 0.0).astype(piece.dtype)
    return flat_dot(gathered, factor_ref)


def stage_kernel(level, later, chips, *refs):
    inner = level < later
    slot_refs = refs[:4]
    factor_ref, other_factor_ref, rhs_ref, other_rhs_ref, inverse_ref, other_inverse_ref = refs[4:10]
    store_refs = refs[10:9 + level]
    outs = refs[-7 if level == 1 else -11:]
    staged_ref, own_rhs_ref, own_inverse_ref = outs[:3]
    rhs, inverse, sems, factor_sems = outs[-4:]
    core, col = own_place()
    straight = core == col
    rows = own_rhs_ref.shape[0]
    if inner:
        pairs = [
            (half_of(rhs_ref, level, core, rows), rhs.at[0]),
            (half_of(other_rhs_ref, level, core, rows), rhs.at[1]),
            (inverse_ref.at[level, 0], inverse.at[0]),
            (other_inverse_ref.at[level, 0], inverse.at[1]),
        ]
    else:
        pairs = [
            (half_of(rhs_ref, level, col, rows), own_rhs_ref),
            (inverse_ref.at[level, 0], own_inverse_ref),
        ]
    factor_copies = start_copies(
        [
            (factor_ref.at[level - 1, 0, 0], staged_ref.at[0]),
            (other_factor_ref.at[level - 1, 0, 0], staged_ref.at[1]),
        ],
        factor_sems,
    )
    copies = start_copies(pairs, sems)
    if level > 1:
        older_refs, store, gathered = outs[3:5], outs[5], outs[6]
        for m, piece in enumerate(store_refs):
            store[m * chips:(m + 1) * chips] = piece[...]
    for g in range(2):
        factor_copies[g].wait()
        if level > 1:
            older_refs[g][...] = slot_sum(
                level, None, chips, slot_refs[g], slot_refs[2 + g], store, staged_ref.at[g], gathered
            )
    for copy in copies:
        copy.wait()
    if inner:
        own_rhs_ref[...] = jnp.where(straight, rhs[0], rhs[1])
        own_inverse_ref[...] = jnp.where(straight, inverse[0], inverse[1])


def sums_kernel(level, chips, *refs):
    slot_refs, store_ref, staged_ref = refs[:4], refs[4], refs[5]
    older_refs = refs[6:8]
    kept_ref, sent_ref, gathered = refs[-3:]
    core, col = own_place()
    sums = []
    for g in range(2):
        total = slot_sum(
            level, level - 1, chips, slot_refs[g], slot_refs[2 + g], store_ref, staged_ref.at[g], gathered
        )
        sums.append(total + older_refs[g][...] if level > 1 else total)
    straight = core == col
    kept_ref[...] = jnp.where(straight, sums[0], sums[1])
    sent_ref[...] = jnp.where(straight, sums[1], sums[0])


def inner_kernel(kept_ref, arrived_ref, rhs_ref, inverse_ref, out_ref, copies_ref):
    solved = solve(rhs_ref[...] - (kept_ref[...] + arrived_ref[...]), inverse_ref[...])
    out_ref[...] = solved
    rounded = solved.astype(jnp.bfloat16)
    for i in range(copies_ref.shape[0]):
        copies_ref[i] = rounded


def last_kernel(first_ref, second_ref, rhs_ref, inverse_ref, *refs):
    done_refs, out_ref = refs[:-1], refs[-1]
    level = len(done_refs)
    for m, done in enumerate(done_refs):
        out_ref[m, 0] = done[...]
    solved = solve(rhs_ref[...] - (first_ref[...] + second_ref[...]), inverse_ref[...])
    out_ref[level, 0] = solved


def paired_shards(row_count, right_sides, factor_blocks, diag_inverses, source_ids, block_counts):
    level_count, _, rhs_count, width = right_sides.shape
    slots = factor_blocks.shape[3]
    rows = rhs_count // 2
    chips = row_count // 2
    later = level_count - 1
    same_core = [[2 * j + k for j in range(chips)] for k in range(2)]
    part = jax.ShapeDtypeStruct((rows, width), jnp.float32)
    rounded_part = jax.ShapeDtypeStruct((rows, width), jnp.bfloat16)
    square = jax.ShapeDtypeStruct((width, width), jnp.bfloat16)
    copies = jax.ShapeDtypeStruct((chips, rows, width), jnp.bfloat16)
    solve_flops = 2 * rows * width * width

    def over_both(x, move):
        pairs = []
        for j in range(chips):
            for k in range(2):
                for c in range(2):
                    tj, tk, tc = move(j, k, c)
                    pairs.append(((2 * j + k) * 2 + c, (2 * tj + tk) * 2 + tc))
        return lax.ppermute(x, ("rows", "cols"), pairs)

    def swap_core(x):
        return lax.ppermute(x, "rows", [(i, i ^ 1) for i in range(row_count)])

    def transpose(x):
        return over_both(x, lambda j, k, c: (j, c, k))

    def spread(x):
        return lax.all_to_all(x, "rows", 0, 0, axis_index_groups=same_core)

    solved, rounded = run(
        first_kernel,
        ((part, VMEM), (rounded_part, VMEM)),
        ((right_sides, HBM), (diag_inverses, HBM)),
        scratch=(
            pltpu.VMEM((rows, width), jnp.float32),
            pltpu.VMEM((width, width), jnp.bfloat16),
            pltpu.SemaphoreType.DMA((2,)),
        ),
        flops=solve_flops,
    )
    finished = [solved]
    copied, = run(copies_kernel, ((copies, VMEM),), ((transpose(rounded), VMEM),))
    stores = [spread(copied)]

    counts = block_counts.reshape(later)
    slot_args = tuple((x, SMEM) for x in (source_ids, swap_core(source_ids), counts, swap_core(counts)))
    staged_args = (
        (factor_blocks, HBM),
        (swap_core(factor_blocks), ANY),
        (right_sides, HBM),
        (swap_core(right_sides), ANY),
        (diag_inverses, HBM),
        (swap_core(diag_inverses), ANY),
    )
    staged_shape = jax.ShapeDtypeStruct((2, slots, width, width), jnp.bfloat16)
    gathered = pltpu.VMEM((rows, slots * width), jnp.bfloat16)
    after = ()
    for l in range(1, level_count):
        staged, rhs, inverse, *older = run(
            functools.partial(stage_kernel, l, later, chips),
            ((staged_shape, FIXED), (part, VMEM), (square, VMEM)) + ((part, VMEM), (part, VMEM)) * (l > 1),
            slot_args + staged_args + tuple((x, VMEM) for x in stores[:l - 1]) + after,
            scratch=((pltpu.VMEM(((l - 1) * chips, rows, width), jnp.bfloat16), gathered) if l > 1 else ())
            + (
                pltpu.VMEM((2, rows, width), jnp.float32),
                pltpu.VMEM((2, width, width), jnp.bfloat16),
                pltpu.SemaphoreType.DMA((4,)),
                pltpu.SemaphoreType.DMA((2,)),
            ),
            flops=2 * slots * solve_flops * (l > 1),
            transferred=2 * slots * width * width * 2,
        )
        kept, sent = run(
            functools.partial(sums_kernel, l, chips),
            ((part, VMEM), (part, VMEM)),
            slot_args
            + ((stores[-1], VMEM), (staged, FIXED))
            + tuple((x, VMEM) for x in older)
            + tuple((x, ANY) for x in finished[1:]),
            scratch=(gathered,),
            flops=2 * slots * solve_flops,
            transferred=2 * slots * width * width * 2,
        )
        after = ((kept, ANY),)
        if l < later:
            arrived = lax.ppermute(sent, "cols", [(0, 1), (1, 0)])
            solved, copied = run(
                inner_kernel,
                ((part, VMEM), (copies, VMEM)),
                tuple((x, VMEM) for x in (kept, arrived, rhs, inverse)),
                flops=solve_flops,
            )
            finished.append(transpose(solved))
            stores.append(spread(copied))
    first = over_both(kept, lambda j, k, c: (j, c, k))
    second = over_both(sent, lambda j, k, c: (j, 1 - c, k))
    out, = run(
        last_kernel,
        ((jax.ShapeDtypeStruct((level_count, 1, rows, width), jnp.float32), VMEM),),
        tuple((x, VMEM) for x in (first, second, rhs, inverse, *finished)),
        flops=solve_flops,
    )
    return out


def gather_slots(ids_ref, counts_ref, group, store_ref, gathered, slots, width):
    for k in range(slots):
        piece = store_ref[ids_ref[group, k]]
        live = jnp.where(k < counts_ref[group], 1.0, 0.0).astype(piece.dtype)
        gathered[:, k * width:(k + 1) * width] = piece * live


def level_kernel(groups, ids_ref, counts_ref, store_ref, *refs):
    factor_refs = refs[:groups]
    rhs_ref, inverse_ref, out_ref, rounded_ref, gathered = refs[groups:]
    slots, width = factor_refs[0].shape[0], factor_refs[0].shape[1]
    update = None
    for g in range(groups):
        gather_slots(ids_ref, counts_ref, g, store_ref, gathered, slots, width)
        term = flat_dot(gathered, factor_refs[g])
        update = term if update is None else update + term
    reduced = (rhs_ref[...] - update).astype(jnp.bfloat16)
    solved = jnp.dot(reduced, inverse_ref[...], preferred_element_type=jnp.float32)
    out_ref[...] = solved
    rounded_ref[...] = solved.astype(jnp.bfloat16)


def solve_level(ids, counts, store, factors, rhs, inverse):
    groups = len(factors)
    rows, width = rhs.shape
    slots = factors[0].shape[0]
    vmem = pl.BlockSpec(memory_space=pltpu.VMEM)
    smem = pl.BlockSpec(memory_space=pltpu.SMEM)
    return pl.pallas_call(
        functools.partial(level_kernel, groups),
        out_shape=(
            jax.ShapeDtypeStruct((rows, width), jnp.float32),
            jax.ShapeDtypeStruct((rows, width), jnp.bfloat16),
        ),
        in_specs=[smem, smem, vmem] + [vmem] * groups + [vmem, vmem],
        out_specs=(vmem, vmem),
        scratch_shapes=[pltpu.VMEM((rows, slots * width), jnp.bfloat16)],
        compiler_params=pltpu.CompilerParams(vmem_limit_bytes=VMEM_LIMIT),
        cost_estimate=pl.CostEstimate(
            flops=2 * rows * width * width * (groups * slots + 1),
            bytes_accessed=groups * slots * width * width * 2,
            transcendentals=0,
        ),
    )(ids, counts, store, *factors, rhs, inverse)


def rotated_shards(col_count, right_sides, factor_blocks, diag_inverses, source_ids, block_counts):
    level_count, _, rhs_count, width = right_sides.shape
    share_rows = rhs_count // col_count
    col_index = lax.axis_index("cols")

    described = jnp.concatenate([source_ids[:, 0, 0], block_counts[:, 0, 0][:, None]], axis=1)
    factors = [[factor_blocks[l, 0, 0]] for l in range(level_count - 1)]
    descriptions = [described]
    for shift in range(1, col_count):
        pairs = [(i, (i + shift) % col_count) for i in range(col_count)]
        descriptions.append(lax.ppermute(described, "cols", pairs))
    for l in range(level_count - 1):
        for shift in range(1, col_count):
            pairs = [(i, (i + shift) % col_count) for i in range(col_count)]
            factors[l].append(lax.ppermute(factor_blocks[l, 0, 0], "cols", pairs))
    descriptions = jnp.stack(descriptions)

    rhs = lax.dynamic_slice_in_dim(right_sides[:, 0], col_index * share_rows, share_rows, 1)
    solutions = []
    stores = []
    for l in range(level_count):
        if l == 0:
            own = jnp.dot(
                rhs[0].astype(jnp.bfloat16), diag_inverses[0, 0], preferred_element_type=jnp.float32
            )
            rounded = own.astype(jnp.bfloat16)
        else:
            ids = descriptions[:, l - 1, :-1]
            counts = descriptions[:, l - 1, -1]
            store = stores[0] if l == 1 else jnp.concatenate(stores, axis=0)
            own, rounded = solve_level(ids, counts, store, factors[l - 1], rhs[l], diag_inverses[l, 0])
        solutions.append(own)
        if l < level_count - 1:
            stores.append(lax.all_gather(rounded, "rows", axis=0))
    return jnp.stack(solutions)[:, None]


def solution(mesh):
    row_count, col_count = mesh.shape["rows"], mesh.shape["cols"]
    chips = row_count // 2
    if col_count == 2 and row_count == 2 * chips:
        shards = functools.partial(paired_shards, row_count)
    else:
        shards = functools.partial(rotated_shards, col_count)
    return jax.shard_map(
        shards,
        mesh=mesh,
        in_specs=(
            P(None, "rows", None, None),
            P(None, "rows", "cols", None, None, None),
            P(None, "rows", None, None),
            P(None, "rows", "cols", None),
            P(None, "rows", "cols"),
        ),
        out_specs=P(None, "rows", "cols", None),
        check_vma=False,
    )
```

```python
import functools

import jax
import jax.numpy as jnp
from jax import lax
from jax.experimental import pallas as pl
from jax.experimental.pallas import tpu as pltpu
from jax.sharding import PartitionSpec as P

VMEM_LIMIT = 16 * 1024 * 1024


VMEM = pl.BlockSpec(memory_space=pltpu.VMEM)
SMEM = pl.BlockSpec(memory_space=pltpu.SMEM)
ANY = pl.BlockSpec(memory_space=pl.ANY)
HBM = pl.BlockSpec(memory_space=pltpu.HBM)


def flat_dot(gathered, factor_ref):
    slots, width = factor_ref.shape[0], factor_ref.shape[1]
    return jnp.dot(
        gathered[...],
        factor_ref[...].reshape(slots * width, width),
        preferred_element_type=jnp.float32,
    )


def run(kernel, outs, args, scratch=(), flops=0, transferred=0):
    return pl.pallas_call(
        kernel,
        out_shape=tuple(pltpu.HBM(x.shape, x.dtype) if spec is HBM else x for x, spec in outs),
        in_specs=[spec for _, spec in args],
        out_specs=tuple(spec for _, spec in outs),
        scratch_shapes=list(scratch),
        compiler_params=pltpu.CompilerParams(vmem_limit_bytes=VMEM_LIMIT),
        cost_estimate=pl.CostEstimate(flops=flops, bytes_accessed=transferred, transcendentals=0),
    )(*(pltpu.with_memory_space_constraint(x, pltpu.HBM) if spec is HBM else x for x, spec in args))


def half_of(ref, level, half, rows):
    return ref.at[level, 0, pl.ds(pl.multiple_of(half * rows, rows), rows), :]


def solve(reduced, inverse):
    return jnp.dot(reduced.astype(jnp.bfloat16), inverse, preferred_element_type=jnp.float32)


def start_copies(pairs, sems):
    copies = [pltpu.make_async_copy(src, dst, sems.at[i]) for i, (src, dst) in enumerate(pairs)]
    for copy in copies:
        copy.start()
    return copies


def own_place():
    return lax.rem(lax.axis_index("rows"), 2), lax.axis_index("cols")


def first_kernel(rhs_ref, inverse_ref, out_ref, rounded_ref, rhs, inverse, solved, sems):
    _, col = own_place()
    for copy in start_copies(
        [(half_of(rhs_ref, 0, col, rhs.shape[0]), rhs), (inverse_ref.at[0, 0], inverse)], sems
    ):
        copy.wait()
    solved[...] = solve(rhs[...], inverse[...])
    out = pltpu.make_async_copy(solved, out_ref, sems.at[2])
    out.start()
    rounded_ref[...] = solved[...].astype(jnp.bfloat16)
    out.wait()


def copies_kernel(rounded_ref, *refs):
    copies_ref, sems = refs[-2:]
    for copy in start_copies([(rounded_ref, copies_ref.at[i]) for i in range(copies_ref.shape[0])], sems):
        copy.wait()


def gather_level(level, older, chips, ids_ref, counts_ref, store, gathered, slots):
    width = store.shape[2]
    for i, k in enumerate(slots):
        source = ids_ref[level - 1, 0, 0, k]
        source_level, place = source // (2 * chips), source % (2 * chips) // 2
        if older:
            wanted = source_level < level - 1
            place = jnp.minimum(source_level, level - 2) * chips + place
        else:
            wanted = source_level == level - 1
        live = jnp.logical_and(k < counts_ref[level - 1], wanted)
        gathered[:, i * width:(i + 1) * width] = store[place] * jnp.where(live, 1.0, 0.0).astype(store.dtype)


def group_sums(level, older, chips, slot_refs, store, own_factor_ref, other_factor_ref, gathered, own_factor, sems):
    ids_ref, other_ids_ref, counts_ref, other_counts_ref = slot_refs
    slots = own_factor.shape[0]
    half = slots // 2
    parts = (range(half), range(half, slots))
    copies = start_copies(
        [
            (own_factor_ref.at[level - 1, 0, 0, pl.ds(part[0], len(part))], own_factor.at[pl.ds(part[0], len(part))])
            for part in parts
        ],
        sems,
    )
    yield None
    gather_level(level, older, chips, other_ids_ref, other_counts_ref, store, gathered, range(slots))
    other = flat_dot(gathered, other_factor_ref.at[level - 1, 0, 0])
    own = None
    width = store.shape[2]
    for part, copy in zip(parts, copies):
        piece = gathered.at[:, pl.ds(part[0] * width, len(part) * width)]
        gather_level(level, older, chips, ids_ref, counts_ref, store, piece, part)
        copy.wait()
        term = flat_dot(piece, own_factor.at[pl.ds(part[0], len(part))])
        own = term if own is None else own + term
    yield own, other


def older_kernel(level, chips, *refs):
    slot_refs, (own_factor_ref, other_factor_ref) = refs[:4], refs[4:6]
    store_refs = refs[6:5 + level]
    out_ref, store, gathered, own_factor, sums, sems, store_sems = refs[5 + level:]
    copies = start_copies(
        [(piece, store.at[pl.ds(m * chips, chips)]) for m, piece in enumerate(store_refs)], store_sems
    )
    work = group_sums(
        level, True, chips, slot_refs, store, own_factor_ref, other_factor_ref, gathered, own_factor, sems
    )
    next(work)
    for copy in copies:
        copy.wait()
    sums[0], sums[1] = next(work)
    out = pltpu.make_async_copy(sums, out_ref, store_sems.at[0])
    out.start()
    out.wait()


def sums_kernel(level, chips, *refs):
    slot_refs, (own_factor_ref, other_factor_ref, store_ref) = refs[:4], refs[4:7]
    kept_ref, sent_ref, store, gathered, own_factor, older, sems, store_sems = refs[-8:]
    core, col = own_place()
    pairs = [(store_ref, store)] + ([(refs[7], older)] if level > 1 else [])
    copies = start_copies(pairs, store_sems)
    work = group_sums(
        level, False, chips, slot_refs, store, own_factor_ref, other_factor_ref, gathered, own_factor, sems
    )
    next(work)
    for copy in copies:
        copy.wait()
    own, other = next(work)
    if level > 1:
        own, other = own + older[0], other + older[1]
    straight = core == col
    kept_ref[...] = jnp.where(straight, own, other)
    sent_ref[...] = jnp.where(straight, other, own)


def select_kernel(level, inner, rhs_ref, other_rhs_ref, inverse_ref, other_inverse_ref, *refs):
    own_rhs_ref, own_inverse_ref, rhs, inverse, sems = refs[-5:]
    core, col = own_place()
    rows = own_rhs_ref.shape[0]
    if inner:
        pairs = [
            (half_of(rhs_ref, level, core, rows), rhs.at[0]),
            (half_of(other_rhs_ref, level, core, rows), rhs.at[1]),
            (inverse_ref.at[level, 0], inverse.at[0]),
            (other_inverse_ref.at[level, 0], inverse.at[1]),
        ]
    else:
        pairs = [
            (half_of(rhs_ref, level, col, rows), own_rhs_ref),
            (inverse_ref.at[level, 0], own_inverse_ref),
        ]
    for copy in start_copies(pairs, sems):
        copy.wait()
    if inner:
        straight = core == col
        own_rhs_ref[...] = jnp.where(straight, rhs[0], rhs[1])
        own_inverse_ref[...] = jnp.where(straight, inverse[0], inverse[1])


def inner_kernel(kept_ref, arrived_ref, rhs_ref, inverse_ref, out_ref, copies_ref, solved, rounded, sems):
    solved[...] = solve(rhs_ref[...] - (kept_ref[...] + arrived_ref[...]), inverse_ref[...])
    rounded[...] = solved[...].astype(jnp.bfloat16)
    chips = copies_ref.shape[0]
    for copy in start_copies([(rounded, copies_ref.at[i]) for i in range(chips)] + [(solved, out_ref)], sems):
        copy.wait()


def last_kernel(first_ref, second_ref, rhs_ref, inverse_ref, *refs):
    done_refs, (out_ref, solved, sems) = refs[:-3], refs[-3:]
    level = len(done_refs)
    copies = start_copies([(done, out_ref.at[m, 0]) for m, done in enumerate(done_refs)], sems)
    solved[...] = solve(rhs_ref[...] - (first_ref[...] + second_ref[...]), inverse_ref[...])
    out = pltpu.make_async_copy(solved, out_ref.at[level, 0], sems.at[level])
    out.start()
    for copy in copies + [out]:
        copy.wait()


def paired_shards(row_count, right_sides, factor_blocks, diag_inverses, source_ids, block_counts):
    level_count, _, rhs_count, width = right_sides.shape
    slots = factor_blocks.shape[3]
    rows = rhs_count // 2
    chips = row_count // 2
    later = level_count - 1
    same_core = [[2 * j + k for j in range(chips)] for k in range(2)]
    part = jax.ShapeDtypeStruct((rows, width), jnp.float32)
    rounded_part = jax.ShapeDtypeStruct((rows, width), jnp.bfloat16)
    square = jax.ShapeDtypeStruct((width, width), jnp.bfloat16)
    copies = jax.ShapeDtypeStruct((chips, rows, width), jnp.bfloat16)
    solve_flops = 2 * rows * width * width
    group_bytes = slots * width * width * 2

    def buffer(x):
        return pltpu.VMEM(x.shape, x.dtype)

    def over_both(x, move):
        pairs = []
        for j in range(chips):
            for k in range(2):
                for c in range(2):
                    tj, tk, tc = move(j, k, c)
                    pairs.append(((2 * j + k) * 2 + c, (2 * tj + tk) * 2 + tc))
        return lax.ppermute(x, ("rows", "cols"), pairs)

    def swap_core(x):
        return lax.ppermute(x, "rows", [(i, i ^ 1) for i in range(row_count)])

    def transpose(x):
        return over_both(x, lambda j, k, c: (j, c, k))

    def spread(x):
        return lax.all_to_all(x, "rows", 0, 0, axis_index_groups=same_core)

    solved, rounded = run(
        first_kernel,
        ((part, HBM), (rounded_part, VMEM)),
        ((right_sides, HBM), (diag_inverses, HBM)),
        scratch=(buffer(part), buffer(square), buffer(part), pltpu.SemaphoreType.DMA((3,))),
        flops=solve_flops,
    )
    finished = [solved]
    counts = block_counts.reshape(later)
    other_ids, other_counts = swap_core(source_ids), swap_core(counts)
    copied, = run(
        copies_kernel,
        ((copies, HBM),),
        ((transpose(rounded), VMEM), (other_ids, ANY), (other_counts, ANY)),
        scratch=(pltpu.SemaphoreType.DMA((chips,)),),
    )
    stores = [spread(copied)]

    slot_args = tuple((x, SMEM) for x in (source_ids, other_ids, counts, other_counts))
    factor_args = ((factor_blocks, HBM), (swap_core(factor_blocks), VMEM))
    select_args = (
        (right_sides, HBM),
        (swap_core(right_sides), ANY),
        (diag_inverses, HBM),
        (swap_core(diag_inverses), ANY),
    )
    gathered = pltpu.VMEM((rows, slots * width), jnp.bfloat16)
    own_factor = pltpu.VMEM((slots, width, width), jnp.bfloat16)
    sums = pltpu.VMEM((2, rows, width), jnp.float32)
    older = ()
    for l in range(1, level_count):
        inner = l < later
        kept, sent = run(
            functools.partial(sums_kernel, l, chips),
            ((part, VMEM), (part, VMEM)),
            slot_args + factor_args + ((stores[-1], ANY),) + older + tuple((x, ANY) for x in finished[1:]),
            scratch=(
                buffer(copies), gathered, own_factor, sums,
                pltpu.SemaphoreType.DMA((2,)), pltpu.SemaphoreType.DMA((2,)),
            ),
            flops=2 * slots * solve_flops,
            transferred=2 * group_bytes,
        )
        rhs, inverse = run(
            functools.partial(select_kernel, l, inner),
            ((part, VMEM), (square, VMEM)),
            select_args + ((kept, ANY),),
            scratch=(
                sums, pltpu.VMEM((2, width, width), jnp.bfloat16), pltpu.SemaphoreType.DMA((4,)),
            ),
            transferred=4 * width * width * 2,
        )
        if inner:
            arrived = lax.ppermute(sent, "cols", [(0, 1), (1, 0)])
            solved, copied = run(
                inner_kernel,
                ((part, HBM), (copies, HBM)),
                tuple((x, VMEM) for x in (kept, arrived, rhs, inverse)),
                scratch=(buffer(part), buffer(rounded_part), pltpu.SemaphoreType.DMA((chips + 1,))),
                flops=solve_flops,
            )
            older_sums, = run(
                functools.partial(older_kernel, l + 1, chips),
                ((jax.ShapeDtypeStruct((2, rows, width), jnp.float32), HBM),),
                slot_args + factor_args + tuple((x, ANY) for x in stores) ,
                scratch=(
                    pltpu.VMEM((l * chips, rows, width), jnp.bfloat16), gathered, own_factor, sums,
                    pltpu.SemaphoreType.DMA((2,)), pltpu.SemaphoreType.DMA((l,)),
                ),
                flops=2 * slots * solve_flops,
                transferred=2 * group_bytes,
            )
            older = ((older_sums, HBM),)
            finished.append(transpose(solved))
            stores.append(spread(copied))
    first = over_both(kept, lambda j, k, c: (j, c, k))
    second = over_both(sent, lambda j, k, c: (j, 1 - c, k))
    out, = run(
        last_kernel,
        ((jax.ShapeDtypeStruct((level_count, 1, rows, width), jnp.float32), ANY),),
        tuple((x, VMEM) for x in (first, second, rhs, inverse)) + tuple((x, ANY) for x in finished),
        scratch=(buffer(part), pltpu.SemaphoreType.DMA((level_count,))),
        flops=solve_flops,
    )
    return out


def gather_slots(ids_ref, counts_ref, group, store_ref, gathered, slots, width):
    for k in range(slots):
        piece = store_ref[ids_ref[group, k]]
        live = jnp.where(k < counts_ref[group], 1.0, 0.0).astype(piece.dtype)
        gathered[:, k * width:(k + 1) * width] = piece * live


def level_kernel(groups, ids_ref, counts_ref, store_ref, *refs):
    factor_refs = refs[:groups]
    rhs_ref, inverse_ref, out_ref, rounded_ref, gathered = refs[groups:]
    slots, width = factor_refs[0].shape[0], factor_refs[0].shape[1]
    update = None
    for g in range(groups):
        gather_slots(ids_ref, counts_ref, g, store_ref, gathered, slots, width)
        term = flat_dot(gathered, factor_refs[g])
        update = term if update is None else update + term
    reduced = (rhs_ref[...] - update).astype(jnp.bfloat16)
    solved = jnp.dot(reduced, inverse_ref[...], preferred_element_type=jnp.float32)
    out_ref[...] = solved
    rounded_ref[...] = solved.astype(jnp.bfloat16)


def solve_level(ids, counts, store, factors, rhs, inverse):
    groups = len(factors)
    rows, width = rhs.shape
    slots = factors[0].shape[0]
    vmem = pl.BlockSpec(memory_space=pltpu.VMEM)
    smem = pl.BlockSpec(memory_space=pltpu.SMEM)
    return pl.pallas_call(
        functools.partial(level_kernel, groups),
        out_shape=(
            jax.ShapeDtypeStruct((rows, width), jnp.float32),
            jax.ShapeDtypeStruct((rows, width), jnp.bfloat16),
        ),
        in_specs=[smem, smem, vmem] + [vmem] * groups + [vmem, vmem],
        out_specs=(vmem, vmem),
        scratch_shapes=[pltpu.VMEM((rows, slots * width), jnp.bfloat16)],
        compiler_params=pltpu.CompilerParams(vmem_limit_bytes=VMEM_LIMIT),
        cost_estimate=pl.CostEstimate(
            flops=2 * rows * width * width * (groups * slots + 1),
            bytes_accessed=groups * slots * width * width * 2,
            transcendentals=0,
        ),
    )(ids, counts, store, *factors, rhs, inverse)


def rotated_shards(col_count, right_sides, factor_blocks, diag_inverses, source_ids, block_counts):
    level_count, _, rhs_count, width = right_sides.shape
    share_rows = rhs_count // col_count
    col_index = lax.axis_index("cols")

    described = jnp.concatenate([source_ids[:, 0, 0], block_counts[:, 0, 0][:, None]], axis=1)
    factors = [[factor_blocks[l, 0, 0]] for l in range(level_count - 1)]
    descriptions = [described]
    for shift in range(1, col_count):
        pairs = [(i, (i + shift) % col_count) for i in range(col_count)]
        descriptions.append(lax.ppermute(described, "cols", pairs))
    for l in range(level_count - 1):
        for shift in range(1, col_count):
            pairs = [(i, (i + shift) % col_count) for i in range(col_count)]
            factors[l].append(lax.ppermute(factor_blocks[l, 0, 0], "cols", pairs))
    descriptions = jnp.stack(descriptions)

    rhs = lax.dynamic_slice_in_dim(right_sides[:, 0], col_index * share_rows, share_rows, 1)
    solutions = []
    stores = []
    for l in range(level_count):
        if l == 0:
            own = jnp.dot(
                rhs[0].astype(jnp.bfloat16), diag_inverses[0, 0], preferred_element_type=jnp.float32
            )
            rounded = own.astype(jnp.bfloat16)
        else:
            ids = descriptions[:, l - 1, :-1]
            counts = descriptions[:, l - 1, -1]
            store = stores[0] if l == 1 else jnp.concatenate(stores, axis=0)
            own, rounded = solve_level(ids, counts, store, factors[l - 1], rhs[l], diag_inverses[l, 0])
        solutions.append(own)
        if l < level_count - 1:
            stores.append(lax.all_gather(rounded, "rows", axis=0))
    return jnp.stack(solutions)[:, None]


def solution(mesh):
    row_count, col_count = mesh.shape["rows"], mesh.shape["cols"]
    chips = row_count // 2
    if col_count == 2 and row_count == 2 * chips:
        shards = functools.partial(paired_shards, row_count)
    else:
        shards = functools.partial(rotated_shards, col_count)
    return jax.shard_map(
        shards,
        mesh=mesh,
        in_specs=(
            P(None, "rows", None, None),
            P(None, "rows", "cols", None, None, None),
            P(None, "rows", None, None),
            P(None, "rows", "cols", None),
            P(None, "rows", "cols"),
        ),
        out_specs=P(None, "rows", "cols", None),
        check_vma=False,
    )
```

```python
import functools

import jax
import jax.numpy as jnp
from jax import lax
from jax.experimental import pallas as pl
from jax.experimental.pallas import tpu as pltpu
from jax.sharding import PartitionSpec as P

VMEM_LIMIT = 16 * 1024 * 1024


VMEM = pl.BlockSpec(memory_space=pltpu.VMEM)
SMEM = pl.BlockSpec(memory_space=pltpu.SMEM)
ANY = pl.BlockSpec(memory_space=pl.ANY)
HBM = pl.BlockSpec(memory_space=pltpu.HBM)


def flat_dot(gathered, factor_ref):
    slots, width = factor_ref.shape[0], factor_ref.shape[1]
    return jnp.dot(
        gathered[...],
        factor_ref[...].reshape(slots * width, width),
        preferred_element_type=jnp.float32,
    )


def run(kernel, outs, args, scratch=(), flops=0, transferred=0):
    return pl.pallas_call(
        kernel,
        out_shape=tuple(pltpu.HBM(x.shape, x.dtype) if spec is HBM else x for x, spec in outs),
        in_specs=[spec for _, spec in args],
        out_specs=tuple(spec for _, spec in outs),
        scratch_shapes=list(scratch),
        compiler_params=pltpu.CompilerParams(vmem_limit_bytes=VMEM_LIMIT),
        cost_estimate=pl.CostEstimate(flops=flops, bytes_accessed=transferred, transcendentals=0),
    )(*(pltpu.with_memory_space_constraint(x, pltpu.HBM) if spec is HBM else x for x, spec in args))


def half_of(ref, level, half, rows):
    return ref.at[level, 0, pl.ds(pl.multiple_of(half * rows, rows), rows), :]


def rows_of(half, rows):
    return pl.ds(pl.multiple_of(half * rows, rows), rows)


def solve(reduced, inverse):
    return jnp.dot(reduced.astype(jnp.bfloat16), inverse, preferred_element_type=jnp.float32)


def start_copies(pairs, sems):
    copies = [pltpu.make_async_copy(src, dst, sems.at[i]) for i, (src, dst) in enumerate(pairs)]
    for copy in copies:
        copy.start()
    return copies


def gather_pieces(level, targets, half, ids_ref, counts_ref, store_refs, gathered):
    rows, width = gathered.shape[0], store_refs[0].shape[2]
    for k in range(ids_ref.shape[3]):
        source = ids_ref[level - 1, 0, 0, k]
        place = lax.rem(source, targets)
        piece = store_refs[0][place] if half is None else store_refs[0][place, rows_of(half, rows), :]
        for m, store in enumerate(store_refs[1:], 1):
            piece = jnp.where(source >= m * targets, store[place], piece)
        live = jnp.where(k < counts_ref[level - 1, 0, 0], 1.0, 0.0).astype(piece.dtype)
        gathered[:, k * width:(k + 1) * width] = piece * live


def first_kernel(
    rhs_ref, inverse_ref, factor_ref, out_ref, rounded_ref, first_factor_ref, second_factor_ref,
    rhs, inverse, solved, sems,
):
    col = lax.axis_index("cols")
    copies = start_copies(
        [
            (rhs_ref.at[0, 0], rhs),
            (inverse_ref.at[0, 0], inverse),
            (factor_ref.at[1, 0, 0], second_factor_ref),
            (factor_ref.at[0, 0, 0], first_factor_ref),
        ],
        sems,
    )
    copies[0].wait()
    copies[1].wait()
    solved[...] = solve(rhs[...], inverse[...])
    out = pltpu.make_async_copy(solved.at[rows_of(col, out_ref.shape[0]), :], out_ref, sems.at[0])
    out.start()
    rounded_ref[...] = solved[...].astype(jnp.bfloat16)
    for copy in copies[2:] + [out]:
        copy.wait()


def shared_kernel(targets, ids_ref, counts_ref, store_ref, factor_ref, *refs):
    kept_ref, sent_ref, gathered, total = refs[-4:]
    rows = kept_ref.shape[0]
    col = lax.axis_index("cols")
    gather_pieces(1, targets, None, ids_ref, counts_ref, (store_ref,), gathered)
    total[...] = flat_dot(gathered, factor_ref)
    kept_ref[...] = total[rows_of(col, rows), :]
    sent_ref[...] = total[rows_of(1 - col, rows), :]


def fetch_kernel(rhs_ref, inverse_ref, factor_ref, after_ref, own_rhs_ref, own_inverse_ref, own_factor_ref, sems):
    del after_ref
    rows = own_rhs_ref.shape[1]
    col = lax.axis_index("cols")
    pairs = [(factor_ref.at[factor_ref.shape[0] - 1, 0, 0], own_factor_ref)]
    for l in range(own_rhs_ref.shape[0]):
        pairs += [
            (half_of(rhs_ref, l + 1, col, rows), own_rhs_ref.at[l]),
            (inverse_ref.at[l + 1, 0], own_inverse_ref.at[l]),
        ]
    for copy in start_copies(pairs, sems):
        copy.wait()


def shared_solve_kernel(kept_ref, arrived_ref, rhs_ref, inverse_ref, out_ref, rounded_ref):
    solved = solve(rhs_ref[0] - (kept_ref[...] + arrived_ref[...]), inverse_ref[0])
    out_ref[...] = solved
    rounded_ref[...] = solved.astype(jnp.bfloat16)


def level_sum(level, targets, refs, gathered):
    ids_ref, other_ids_ref, counts_ref, other_counts_ref = refs[:4]
    factor_ref, other_factor_ref = refs[4:6]
    store_refs = refs[6:6 + level]
    col = lax.axis_index("cols")
    gather_pieces(level, targets, col, ids_ref, counts_ref, store_refs, gathered)
    own = flat_dot(gathered, factor_ref)
    gather_pieces(level, targets, col, other_ids_ref, other_counts_ref, store_refs, gathered)
    return own + flat_dot(gathered, other_factor_ref)


def whole_kernel(level, targets, *refs):
    rhs_ref, inverse_ref, out_ref, rounded_ref, gathered = refs[6 + level:]
    update = level_sum(level, targets, refs, gathered)
    solved = solve(rhs_ref[level - 1] - update, inverse_ref[level - 1])
    out_ref[...] = solved
    rounded_ref[...] = solved.astype(jnp.bfloat16)


def last_kernel(level, targets, *refs):
    rhs_ref, inverse_ref = refs[6 + level:8 + level]
    done_refs = refs[8 + level:8 + 2 * level]
    out_ref, gathered, solved, sems = refs[8 + 2 * level:]
    copies = start_copies([(done, out_ref.at[m, 0]) for m, done in enumerate(done_refs)], sems)
    update = level_sum(level, targets, refs, gathered)
    solved[...] = solve(rhs_ref[level - 1] - update, inverse_ref[level - 1])
    out = pltpu.make_async_copy(solved, out_ref.at[level, 0], sems.at[level])
    out.start()
    for copy in copies + [out]:
        copy.wait()


def paired_shards(targets, right_sides, factor_blocks, diag_inverses, source_ids, block_counts):
    level_count, _, rhs_count, width = right_sides.shape
    slots = factor_blocks.shape[3]
    rows = rhs_count // 2
    later = level_count - 1
    part = jax.ShapeDtypeStruct((rows, width), jnp.float32)
    rounded_part = jax.ShapeDtypeStruct((rows, width), jnp.bfloat16)
    blocks = jax.ShapeDtypeStruct((slots, width, width), jnp.bfloat16)
    whole = (rhs_count, width)
    flops = 2 * rows * width * width
    block_bytes = slots * width * width * 2

    def swap(x):
        return lax.ppermute(x, "cols", [(0, 1), (1, 0)])

    solved, rounded, first_blocks, second_blocks = run(
        first_kernel,
        ((part, HBM), (jax.ShapeDtypeStruct(whole, jnp.bfloat16), VMEM), (blocks, VMEM), (blocks, VMEM)),
        ((right_sides, HBM), (diag_inverses, HBM), (factor_blocks, HBM)),
        scratch=(
            pltpu.VMEM(whole, jnp.float32),
            pltpu.VMEM((width, width), jnp.bfloat16),
            pltpu.VMEM(whole, jnp.float32),
            pltpu.SemaphoreType.DMA((4,)),
        ),
        flops=2 * flops,
        transferred=2 * block_bytes,
    )
    finished = [solved]
    slot_args = tuple((x, SMEM) for x in (source_ids, swap(source_ids), block_counts, swap(block_counts)))
    other_blocks = [swap(second_blocks)]
    own_blocks = [second_blocks]
    stores = [lax.all_gather(rounded, "rows", axis=0)]

    kept, sent = run(
        functools.partial(shared_kernel, targets),
        ((part, VMEM), (part, VMEM)),
        (slot_args[0], slot_args[2], (stores[0], VMEM), (first_blocks, VMEM))
        + ((slot_args[1][0], ANY), (slot_args[3][0], ANY)),
        scratch=(pltpu.VMEM((rhs_count, slots * width), jnp.bfloat16), pltpu.VMEM(whole, jnp.float32)),
        flops=2 * slots * flops,
        transferred=block_bytes,
    )
    arrived = swap(sent)
    rhs, inverses, last_blocks = run(
        fetch_kernel,
        (
            (jax.ShapeDtypeStruct((later, rows, width), jnp.float32), VMEM),
            (jax.ShapeDtypeStruct((later, width, width), jnp.bfloat16), VMEM),
            (blocks, VMEM),
        ),
        ((right_sides, HBM), (diag_inverses, HBM), (factor_blocks, HBM), (kept, ANY)),
        scratch=(pltpu.SemaphoreType.DMA((1 + 2 * later,)),),
        transferred=block_bytes,
    )
    solved, rounded = run(
        shared_solve_kernel,
        ((part, VMEM), (rounded_part, VMEM)),
        ((kept, VMEM), (arrived, VMEM), (rhs, VMEM), (inverses, VMEM)),
        flops=flops,
    )
    finished.append(solved)
    own_blocks.append(last_blocks)
    other_blocks.append(swap(last_blocks))

    for l in range(2, level_count):
        stores.append(lax.all_gather(rounded, "rows", axis=0))
        args = (
            slot_args
            + ((own_blocks[l - 2], VMEM), (other_blocks[l - 2], VMEM))
            + tuple((x, VMEM) for x in stores)
            + ((rhs, VMEM), (inverses, VMEM))
        )
        gathered = pltpu.VMEM((rows, slots * width), jnp.bfloat16)
        if l < later:
            solved, rounded = run(
                functools.partial(whole_kernel, l, targets),
                ((part, VMEM), (rounded_part, VMEM)),
                args,
                scratch=(gathered,),
                flops=(2 * slots + 1) * flops,
                transferred=2 * block_bytes,
            )
            finished.append(solved)
    out, = run(
        functools.partial(last_kernel, later, targets),
        ((jax.ShapeDtypeStruct((level_count, 1, rows, width), jnp.float32), ANY),),
        args + tuple((x, ANY) for x in finished),
        scratch=(
            gathered,
            pltpu.VMEM((rows, width), jnp.float32),
            pltpu.SemaphoreType.DMA((level_count,)),
        ),
        flops=(2 * slots + 1) * flops,
        transferred=2 * block_bytes,
    )
    return out


def gather_slots(ids_ref, counts_ref, group, store_ref, gathered, slots, width):
    for k in range(slots):
        piece = store_ref[ids_ref[group, k]]
        live = jnp.where(k < counts_ref[group], 1.0, 0.0).astype(piece.dtype)
        gathered[:, k * width:(k + 1) * width] = piece * live


def level_kernel(groups, ids_ref, counts_ref, store_ref, *refs):
    factor_refs = refs[:groups]
    rhs_ref, inverse_ref, out_ref, rounded_ref, gathered = refs[groups:]
    slots, width = factor_refs[0].shape[0], factor_refs[0].shape[1]
    update = None
    for g in range(groups):
        gather_slots(ids_ref, counts_ref, g, store_ref, gathered, slots, width)
        term = flat_dot(gathered, factor_refs[g])
        update = term if update is None else update + term
    reduced = (rhs_ref[...] - update).astype(jnp.bfloat16)
    solved = jnp.dot(reduced, inverse_ref[...], preferred_element_type=jnp.float32)
    out_ref[...] = solved
    rounded_ref[...] = solved.astype(jnp.bfloat16)


def solve_level(ids, counts, store, factors, rhs, inverse):
    groups = len(factors)
    rows, width = rhs.shape
    slots = factors[0].shape[0]
    vmem = pl.BlockSpec(memory_space=pltpu.VMEM)
    smem = pl.BlockSpec(memory_space=pltpu.SMEM)
    return pl.pallas_call(
        functools.partial(level_kernel, groups),
        out_shape=(
            jax.ShapeDtypeStruct((rows, width), jnp.float32),
            jax.ShapeDtypeStruct((rows, width), jnp.bfloat16),
        ),
        in_specs=[smem, smem, vmem] + [vmem] * groups + [vmem, vmem],
        out_specs=(vmem, vmem),
        scratch_shapes=[pltpu.VMEM((rows, slots * width), jnp.bfloat16)],
        compiler_params=pltpu.CompilerParams(vmem_limit_bytes=VMEM_LIMIT),
        cost_estimate=pl.CostEstimate(
            flops=2 * rows * width * width * (groups * slots + 1),
            bytes_accessed=groups * slots * width * width * 2,
            transcendentals=0,
        ),
    )(ids, counts, store, *factors, rhs, inverse)


def rotated_shards(col_count, right_sides, factor_blocks, diag_inverses, source_ids, block_counts):
    level_count, _, rhs_count, width = right_sides.shape
    share_rows = rhs_count // col_count
    col_index = lax.axis_index("cols")

    described = jnp.concatenate([source_ids[:, 0, 0], block_counts[:, 0, 0][:, None]], axis=1)
    factors = [[factor_blocks[l, 0, 0]] for l in range(level_count - 1)]
    descriptions = [described]
    for shift in range(1, col_count):
        pairs = [(i, (i + shift) % col_count) for i in range(col_count)]
        descriptions.append(lax.ppermute(described, "cols", pairs))
    for l in range(level_count - 1):
        for shift in range(1, col_count):
            pairs = [(i, (i + shift) % col_count) for i in range(col_count)]
            factors[l].append(lax.ppermute(factor_blocks[l, 0, 0], "cols", pairs))
    descriptions = jnp.stack(descriptions)

    rhs = lax.dynamic_slice_in_dim(right_sides[:, 0], col_index * share_rows, share_rows, 1)
    solutions = []
    stores = []
    for l in range(level_count):
        if l == 0:
            own = jnp.dot(
                rhs[0].astype(jnp.bfloat16), diag_inverses[0, 0], preferred_element_type=jnp.float32
            )
            rounded = own.astype(jnp.bfloat16)
        else:
            ids = descriptions[:, l - 1, :-1]
            counts = descriptions[:, l - 1, -1]
            store = stores[0] if l == 1 else jnp.concatenate(stores, axis=0)
            own, rounded = solve_level(ids, counts, store, factors[l - 1], rhs[l], diag_inverses[l, 0])
        solutions.append(own)
        if l < level_count - 1:
            stores.append(lax.all_gather(rounded, "rows", axis=0))
    return jnp.stack(solutions)[:, None]


def solution(mesh):
    row_count, col_count = mesh.shape["rows"], mesh.shape["cols"]
    if col_count == 2:
        shards = functools.partial(paired_shards, row_count)
    else:
        shards = functools.partial(rotated_shards, col_count)
    return jax.shard_map(
        shards,
        mesh=mesh,
        in_specs=(
            P(None, "rows", None, None),
            P(None, "rows", "cols", None, None, None),
            P(None, "rows", None, None),
            P(None, "rows", "cols", None),
            P(None, "rows", "cols"),
        ),
        out_specs=P(None, "rows", "cols", None),
        check_vma=False,
    )
```

```python
import functools

import jax
import jax.numpy as jnp
from jax import lax
from jax.experimental import pallas as pl
from jax.experimental.pallas import tpu as pltpu
from jax.sharding import PartitionSpec as P

VMEM_LIMIT = 16 * 1024 * 1024


VMEM = pl.BlockSpec(memory_space=pltpu.VMEM)
SMEM = pl.BlockSpec(memory_space=pltpu.SMEM)
ANY = pl.BlockSpec(memory_space=pl.ANY)
HBM = pl.BlockSpec(memory_space=pltpu.HBM)
FIXED = pl.BlockSpec(memory_space=pltpu.VMEM)
PLACES = {id(HBM): pltpu.HBM, id(FIXED): pltpu.VMEM}


def flat_dot(gathered, factor_ref):
    slots, width = factor_ref.shape[0], factor_ref.shape[1]
    return jnp.dot(
        gathered[...],
        factor_ref[...].reshape(slots * width, width),
        preferred_element_type=jnp.float32,
    )


def run(kernel, outs, args, scratch=(), flops=0, transferred=0):
    out_shape = tuple(PLACES[id(spec)](x.shape, x.dtype) if id(spec) in PLACES else x for x, spec in outs)
    args = tuple(
        (pltpu.with_memory_space_constraint(x, PLACES[id(spec)]) if id(spec) in PLACES else x, spec)
        for x, spec in args
    )
    return pl.pallas_call(
        kernel,
        out_shape=out_shape,
        in_specs=[spec for _, spec in args],
        out_specs=tuple(spec for _, spec in outs),
        scratch_shapes=list(scratch),
        compiler_params=pltpu.CompilerParams(vmem_limit_bytes=VMEM_LIMIT),
        cost_estimate=pl.CostEstimate(flops=flops, bytes_accessed=transferred, transcendentals=0),
    )(*(x for x, _ in args))


def half_of(ref, level, half, rows):
    return ref.at[level, 0, pl.ds(pl.multiple_of(half * rows, rows), rows), :]


def solve(reduced, inverse):
    return jnp.dot(reduced.astype(jnp.bfloat16), inverse, preferred_element_type=jnp.float32)


def start_copies(pairs, sems):
    copies = [pltpu.make_async_copy(src, dst, sems.at[i]) for i, (src, dst) in enumerate(pairs)]
    for copy in copies:
        copy.start()
    return copies


def own_place():
    return lax.rem(lax.axis_index("rows"), 2), lax.axis_index("cols")


def first_kernel(rhs_ref, inverse_ref, out_ref, rounded_ref, rhs, inverse, sems):
    _, col = own_place()
    copies = start_copies(
        [(half_of(rhs_ref, 0, col, out_ref.shape[0]), rhs), (inverse_ref.at[0, 0], inverse)], sems
    )
    for copy in copies:
        copy.wait()
    solved = solve(rhs[...], inverse[...])
    out_ref[...] = solved
    rounded_ref[...] = solved.astype(jnp.bfloat16)


def copies_kernel(rounded_ref, *refs):
    copies_ref = refs[-1]
    for i in range(copies_ref.shape[0]):
        copies_ref[i] = rounded_ref[...]


def slot_sum(level, store_level, chips, ids_ref, counts_ref, store_ref, factor_ref, gathered):
    slots, width = factor_ref.shape[0], factor_ref.shape[1]
    for k in range(slots):
        source = ids_ref[level - 1, 0, 0, k]
        source_level, place = source // (2 * chips), source % (2 * chips) // 2
        live = k < counts_ref[level - 1]
        if store_level is None:
            live = jnp.logical_and(live, source_level < level - 1)
            place = jnp.minimum(source_level, level - 2) * chips + place
        else:
            live = jnp.logical_and(live, source_level == store_level)
        piece = store_ref[place]
        gathered[:, k * width:(k + 1) * width] = piece * jnp.where(live, 1.0, 0.0).astype(piece.dtype)
    return flat_dot(gathered, factor_ref)


def stage_kernel(level, later, chips, *refs):
    inner = level < later
    slot_refs = refs[:4]
    factor_ref, other_factor_ref, rhs_ref, other_rhs_ref, inverse_ref, other_inverse_ref = refs[4:10]
    store_refs = refs[10:9 + level]
    outs = refs[-7 if level == 1 else -11:]
    staged_ref, own_rhs_ref, own_inverse_ref = outs[:3]
    rhs, inverse, sems, factor_sems = outs[-4:]
    core, col = own_place()
    straight = core == col
    rows = own_rhs_ref.shape[0]
    if inner:
        pairs = [
            (half_of(rhs_ref, level, core, rows), rhs.at[0]),
            (half_of(other_rhs_ref, level, core, rows), rhs.at[1]),
            (inverse_ref.at[level, 0], inverse.at[0]),
            (other_inverse_ref.at[level, 0], inverse.at[1]),
        ]
    else:
        pairs = [
            (half_of(rhs_ref, level, col, rows), own_rhs_ref),
            (inverse_ref.at[level, 0], own_inverse_ref),
        ]
    factor_copies = start_copies(
        [
            (factor_ref.at[level - 1, 0, 0], staged_ref.at[0]),
            (other_factor_ref.at[level - 1, 0, 0], staged_ref.at[1]),
        ],
        factor_sems,
    )
    copies = start_copies(pairs, sems)
    if level > 1:
        older_refs, store, gathered = outs[3:5], outs[5], outs[6]
        for m, piece in enumerate(store_refs):
            store[m * chips:(m + 1) * chips] = piece[...]
    for g in range(2):
        factor_copies[g].wait()
        if level > 1:
            older_refs[g][...] = slot_sum(
                level, None, chips, slot_refs[g], slot_refs[2 + g], store, staged_ref.at[g], gathered
            )
    for copy in copies:
        copy.wait()
    if inner:
        own_rhs_ref[...] = jnp.where(straight, rhs[0], rhs[1])
        own_inverse_ref[...] = jnp.where(straight, inverse[0], inverse[1])


def sums_kernel(level, chips, *refs):
    slot_refs, store_ref, staged_ref = refs[:4], refs[4], refs[5]
    older_refs = refs[6:8]
    kept_ref, sent_ref, gathered = refs[-3:]
    core, col = own_place()
    sums = []
    for g in range(2):
        total = slot_sum(
            level, level - 1, chips, slot_refs[g], slot_refs[2 + g], store_ref, staged_ref.at[g], gathered
        )
        sums.append(total + older_refs[g][...] if level > 1 else total)
    straight = core == col
    kept_ref[...] = jnp.where(straight, sums[0], sums[1])
    sent_ref[...] = jnp.where(straight, sums[1], sums[0])


def inner_kernel(kept_ref, arrived_ref, rhs_ref, inverse_ref, out_ref, copies_ref):
    solved = solve(rhs_ref[...] - (kept_ref[...] + arrived_ref[...]), inverse_ref[...])
    out_ref[...] = solved
    rounded = solved.astype(jnp.bfloat16)
    for i in range(copies_ref.shape[0]):
        copies_ref[i] = rounded


def last_kernel(first_ref, second_ref, rhs_ref, inverse_ref, *refs):
    done_refs, out_ref = refs[:-1], refs[-1]
    level = len(done_refs)
    for m, done in enumerate(done_refs):
        out_ref[m, 0] = done[...]
    solved = solve(rhs_ref[...] - (first_ref[...] + second_ref[...]), inverse_ref[...])
    out_ref[level, 0] = solved


def paired_shards(row_count, right_sides, factor_blocks, diag_inverses, source_ids, block_counts):
    level_count, _, rhs_count, width = right_sides.shape
    slots = factor_blocks.shape[3]
    rows = rhs_count // 2
    chips = row_count // 2
    later = level_count - 1
    same_core = [[2 * j + k for j in range(chips)] for k in range(2)]
    part = jax.ShapeDtypeStruct((rows, width), jnp.float32)
    rounded_part = jax.ShapeDtypeStruct((rows, width), jnp.bfloat16)
    square = jax.ShapeDtypeStruct((width, width), jnp.bfloat16)
    copies = jax.ShapeDtypeStruct((chips, rows, width), jnp.bfloat16)
    solve_flops = 2 * rows * width * width

    def over_both(x, move):
        pairs = []
        for j in range(chips):
            for k in range(2):
                for c in range(2):
                    tj, tk, tc = move(j, k, c)
                    pairs.append(((2 * j + k) * 2 + c, (2 * tj + tk) * 2 + tc))
        return lax.ppermute(x, ("rows", "cols"), pairs)

    def swap_core(x):
        return lax.ppermute(x, "rows", [(i, i ^ 1) for i in range(row_count)])

    def transpose(x):
        return over_both(x, lambda j, k, c: (j, c, k))

    def spread(x):
        return lax.all_to_all(x, "rows", 0, 0, axis_index_groups=same_core)

    solved, rounded = run(
        first_kernel,
        ((part, VMEM), (rounded_part, VMEM)),
        ((right_sides, HBM), (diag_inverses, HBM)),
        scratch=(
            pltpu.VMEM((rows, width), jnp.float32),
            pltpu.VMEM((width, width), jnp.bfloat16),
            pltpu.SemaphoreType.DMA((2,)),
        ),
        flops=solve_flops,
    )
    finished = [solved]
    counts = block_counts.reshape(later)
    other_ids, other_counts = swap_core(source_ids), swap_core(counts)
    copied, = run(
        copies_kernel,
        ((copies, VMEM),),
        ((transpose(rounded), VMEM), (other_ids, ANY), (other_counts, ANY)),
    )
    stores = [spread(copied)]

    slot_args = tuple((x, SMEM) for x in (source_ids, other_ids, counts, other_counts))
    staged_args = (
        (factor_blocks, HBM),
        (swap_core(factor_blocks), HBM),
        (right_sides, HBM),
        (swap_core(right_sides), ANY),
        (diag_inverses, HBM),
        (swap_core(diag_inverses), ANY),
    )
    staged_shape = jax.ShapeDtypeStruct((2, slots, width, width), jnp.bfloat16)
    gathered = pltpu.VMEM((rows, slots * width), jnp.bfloat16)
    after = ()
    for l in range(1, level_count):
        staged, rhs, inverse, *older = run(
            functools.partial(stage_kernel, l, later, chips),
            ((staged_shape, FIXED), (part, VMEM), (square, VMEM)) + ((part, VMEM), (part, VMEM)) * (l > 1),
            slot_args + staged_args + tuple((x, VMEM) for x in stores[:l - 1]) + after,
            scratch=((pltpu.VMEM(((l - 1) * chips, rows, width), jnp.bfloat16), gathered) if l > 1 else ())
            + (
                pltpu.VMEM((2, rows, width), jnp.float32),
                pltpu.VMEM((2, width, width), jnp.bfloat16),
                pltpu.SemaphoreType.DMA((4,)),
                pltpu.SemaphoreType.DMA((2,)),
            ),
            flops=2 * slots * solve_flops * (l > 1),
            transferred=2 * slots * width * width * 2,
        )
        kept, sent = run(
            functools.partial(sums_kernel, l, chips),
            ((part, VMEM), (part, VMEM)),
            slot_args
            + ((stores[-1], VMEM), (staged, FIXED))
            + tuple((x, VMEM) for x in older)
            + tuple((x, ANY) for x in finished[1:]),
            scratch=(gathered,),
            flops=2 * slots * solve_flops,
            transferred=2 * slots * width * width * 2,
        )
        after = ((kept, ANY),)
        if l < later:
            arrived = lax.ppermute(sent, "cols", [(0, 1), (1, 0)])
            solved, copied = run(
                inner_kernel,
                ((part, VMEM), (copies, VMEM)),
                tuple((x, VMEM) for x in (kept, arrived, rhs, inverse)),
                flops=solve_flops,
            )
            finished.append(transpose(solved))
            stores.append(spread(copied))
    first = over_both(kept, lambda j, k, c: (j, c, k))
    second = over_both(sent, lambda j, k, c: (j, 1 - c, k))
    out, = run(
        last_kernel,
        ((jax.ShapeDtypeStruct((level_count, 1, rows, width), jnp.float32), VMEM),),
        tuple((x, VMEM) for x in (first, second, rhs, inverse, *finished)),
        flops=solve_flops,
    )
    return out


def gather_slots(ids_ref, counts_ref, group, store_ref, gathered, slots, width):
    for k in range(slots):
        piece = store_ref[ids_ref[group, k]]
        live = jnp.where(k < counts_ref[group], 1.0, 0.0).astype(piece.dtype)
        gathered[:, k * width:(k + 1) * width] = piece * live


def level_kernel(groups, ids_ref, counts_ref, store_ref, *refs):
    factor_refs = refs[:groups]
    rhs_ref, inverse_ref, out_ref, rounded_ref, gathered = refs[groups:]
    slots, width = factor_refs[0].shape[0], factor_refs[0].shape[1]
    update = None
    for g in range(groups):
        gather_slots(ids_ref, counts_ref, g, store_ref, gathered, slots, width)
        term = flat_dot(gathered, factor_refs[g])
        update = term if update is None else update + term
    reduced = (rhs_ref[...] - update).astype(jnp.bfloat16)
    solved = jnp.dot(reduced, inverse_ref[...], preferred_element_type=jnp.float32)
    out_ref[...] = solved
    rounded_ref[...] = solved.astype(jnp.bfloat16)


def solve_level(ids, counts, store, factors, rhs, inverse):
    groups = len(factors)
    rows, width = rhs.shape
    slots = factors[0].shape[0]
    vmem = pl.BlockSpec(memory_space=pltpu.VMEM)
    smem = pl.BlockSpec(memory_space=pltpu.SMEM)
    return pl.pallas_call(
        functools.partial(level_kernel, groups),
        out_shape=(
            jax.ShapeDtypeStruct((rows, width), jnp.float32),
            jax.ShapeDtypeStruct((rows, width), jnp.bfloat16),
        ),
        in_specs=[smem, smem, vmem] + [vmem] * groups + [vmem, vmem],
        out_specs=(vmem, vmem),
        scratch_shapes=[pltpu.VMEM((rows, slots * width), jnp.bfloat16)],
        compiler_params=pltpu.CompilerParams(vmem_limit_bytes=VMEM_LIMIT),
        cost_estimate=pl.CostEstimate(
            flops=2 * rows * width * width * (groups * slots + 1),
            bytes_accessed=groups * slots * width * width * 2,
            transcendentals=0,
        ),
    )(ids, counts, store, *factors, rhs, inverse)


def rotated_shards(col_count, right_sides, factor_blocks, diag_inverses, source_ids, block_counts):
    level_count, _, rhs_count, width = right_sides.shape
    share_rows = rhs_count // col_count
    col_index = lax.axis_index("cols")

    described = jnp.concatenate([source_ids[:, 0, 0], block_counts[:, 0, 0][:, None]], axis=1)
    factors = [[factor_blocks[l, 0, 0]] for l in range(level_count - 1)]
    descriptions = [described]
    for shift in range(1, col_count):
        pairs = [(i, (i + shift) % col_count) for i in range(col_count)]
        descriptions.append(lax.ppermute(described, "cols", pairs))
    for l in range(level_count - 1):
        for shift in range(1, col_count):
            pairs = [(i, (i + shift) % col_count) for i in range(col_count)]
            factors[l].append(lax.ppermute(factor_blocks[l, 0, 0], "cols", pairs))
    descriptions = jnp.stack(descriptions)

    rhs = lax.dynamic_slice_in_dim(right_sides[:, 0], col_index * share_rows, share_rows, 1)
    solutions = []
    stores = []
    for l in range(level_count):
        if l == 0:
            own = jnp.dot(
                rhs[0].astype(jnp.bfloat16), diag_inverses[0, 0], preferred_element_type=jnp.float32
            )
            rounded = own.astype(jnp.bfloat16)
        else:
            ids = descriptions[:, l - 1, :-1]
            counts = descriptions[:, l - 1, -1]
            store = stores[0] if l == 1 else jnp.concatenate(stores, axis=0)
            own, rounded = solve_level(ids, counts, store, factors[l - 1], rhs[l], diag_inverses[l, 0])
        solutions.append(own)
        if l < level_count - 1:
            stores.append(lax.all_gather(rounded, "rows", axis=0))
    return jnp.stack(solutions)[:, None]


def solution(mesh):
    row_count, col_count = mesh.shape["rows"], mesh.shape["cols"]
    chips = row_count // 2
    if col_count == 2 and row_count == 2 * chips:
        shards = functools.partial(paired_shards, row_count)
    else:
        shards = functools.partial(rotated_shards, col_count)
    return jax.shard_map(
        shards,
        mesh=mesh,
        in_specs=(
            P(None, "rows", None, None),
            P(None, "rows", "cols", None, None, None),
            P(None, "rows", None, None),
            P(None, "rows", "cols", None),
            P(None, "rows", "cols"),
        ),
        out_specs=P(None, "rows", "cols", None),
        check_vma=False,
    )
```

```python
import functools

import jax
import jax.numpy as jnp
from jax import lax
from jax.experimental import pallas as pl
from jax.experimental.pallas import tpu as pltpu
from jax.sharding import PartitionSpec as P

VMEM_LIMIT = 16 * 1024 * 1024


VMEM = pl.BlockSpec(memory_space=pltpu.VMEM)
SMEM = pl.BlockSpec(memory_space=pltpu.SMEM)
ANY = pl.BlockSpec(memory_space=pl.ANY)
HBM = pl.BlockSpec(memory_space=pltpu.HBM)
FIXED = pl.BlockSpec(memory_space=pltpu.VMEM)
PLACES = {id(HBM): pltpu.HBM, id(FIXED): pltpu.VMEM}


def flat_dot(gathered, factor_ref):
    slots, width = factor_ref.shape[0], factor_ref.shape[1]
    return jnp.dot(
        gathered[...],
        factor_ref[...].reshape(slots * width, width),
        preferred_element_type=jnp.float32,
    )


def run(kernel, outs, args, scratch=(), flops=0, transferred=0):
    out_shape = tuple(PLACES[id(spec)](x.shape, x.dtype) if id(spec) in PLACES else x for x, spec in outs)
    args = tuple(
        (pltpu.with_memory_space_constraint(x, PLACES[id(spec)]) if id(spec) in PLACES else x, spec)
        for x, spec in args
    )
    return pl.pallas_call(
        kernel,
        out_shape=out_shape,
        in_specs=[spec for _, spec in args],
        out_specs=tuple(spec for _, spec in outs),
        scratch_shapes=list(scratch),
        compiler_params=pltpu.CompilerParams(vmem_limit_bytes=VMEM_LIMIT),
        cost_estimate=pl.CostEstimate(flops=flops, bytes_accessed=transferred, transcendentals=0),
    )(*(x for x, _ in args))


def half_of(ref, level, half, rows):
    return ref.at[level, 0, pl.ds(pl.multiple_of(half * rows, rows), rows), :]


def solve(reduced, inverse):
    return jnp.dot(reduced.astype(jnp.bfloat16), inverse, preferred_element_type=jnp.float32)


def start_copies(pairs, sems):
    copies = [pltpu.make_async_copy(src, dst, sems.at[i]) for i, (src, dst) in enumerate(pairs)]
    for copy in copies:
        copy.start()
    return copies


def own_place():
    return lax.rem(lax.axis_index("rows"), 2), lax.axis_index("cols")


def first_kernel(
    ids_ref, counts_ref, rhs_ref, inverse_ref, out_ref, rounded_ref, live_ids_ref,
    ids, counts, rhs, inverse, sems,
):
    _, col = own_place()
    copies = start_copies(
        [
            (ids_ref, ids),
            (counts_ref, counts),
            (half_of(rhs_ref, 0, col, out_ref.shape[0]), rhs),
            (inverse_ref.at[0, 0], inverse),
        ],
        sems,
    )
    copies[0].wait()
    copies[1].wait()
    for l in range(ids.shape[0]):
        for k in range(ids.shape[3]):
            live_ids_ref[l, 0, 0, k] = jnp.where(k < counts[l], ids[l, 0, 0, k], -1)
    copies[2].wait()
    copies[3].wait()
    solved = solve(rhs[...], inverse[...])
    out_ref[...] = solved
    rounded_ref[...] = solved.astype(jnp.bfloat16)


def copies_kernel(rounded_ref, copies_ref):
    for i in range(copies_ref.shape[0]):
        copies_ref[i] = rounded_ref[...]


def slot_sum(level, store_level, chips, ids_ref, store_ref, factor_ref, gathered):
    slots, width = factor_ref.shape[0], factor_ref.shape[1]
    for k in range(slots):
        source_id = ids_ref[level - 1, 0, 0, k]
        source = jnp.maximum(source_id, 0)
        source_level, place = source // (2 * chips), source % (2 * chips) // 2
        live = source_id >= 0
        if store_level is None:
            live = jnp.logical_and(live, source_level < level - 1)
            place = jnp.minimum(source_level, level - 2) * chips + place
        else:
            live = jnp.logical_and(live, source_level == store_level)
        piece = store_ref[place]
        gathered[:, k * width:(k + 1) * width] = piece * jnp.where(live, 1.0, 0.0).astype(piece.dtype)
    return flat_dot(gathered, factor_ref)


def stage_kernel(level, later, chips, *refs):
    inner = level < later
    slot_refs = refs[:2]
    factor_ref, other_factor_ref, rhs_ref, other_rhs_ref, inverse_ref, other_inverse_ref = refs[2:8]
    store_refs = refs[8:7 + level]
    outs = refs[-7 if level == 1 else -11:]
    staged_ref, own_rhs_ref, own_inverse_ref = outs[:3]
    rhs, inverse, sems, factor_sems = outs[-4:]
    core, col = own_place()
    straight = core == col
    rows = own_rhs_ref.shape[0]
    if inner:
        pairs = [
            (half_of(rhs_ref, level, core, rows), rhs.at[0]),
            (half_of(other_rhs_ref, level, core, rows), rhs.at[1]),
            (inverse_ref.at[level, 0], inverse.at[0]),
            (other_inverse_ref.at[level, 0], inverse.at[1]),
        ]
    else:
        pairs = [
            (half_of(rhs_ref, level, col, rows), own_rhs_ref),
            (inverse_ref.at[level, 0], own_inverse_ref),
        ]
    factor_copies = start_copies(
        [
            (factor_ref.at[level - 1, 0, 0], staged_ref.at[0]),
            (other_factor_ref.at[level - 1, 0, 0], staged_ref.at[1]),
        ],
        factor_sems,
    )
    copies = start_copies(pairs, sems)
    if level > 1:
        older_refs, store, gathered = outs[3:5], outs[5], outs[6]
        for m, piece in enumerate(store_refs):
            store[m * chips:(m + 1) * chips] = piece[...]
    for g in range(2):
        factor_copies[g].wait()
        if level > 1:
            older_refs[g][...] = slot_sum(
                level, None, chips, slot_refs[g], store, staged_ref.at[g], gathered
            )
    for copy in copies:
        copy.wait()
    if inner:
        own_rhs_ref[...] = jnp.where(straight, rhs[0], rhs[1])
        own_inverse_ref[...] = jnp.where(straight, inverse[0], inverse[1])


def sums_kernel(level, chips, *refs):
    slot_refs, store_ref, staged_ref = refs[:2], refs[2], refs[3]
    older_refs = refs[4:6]
    kept_ref, sent_ref, gathered = refs[-3:]
    core, col = own_place()
    sums = []
    for g in range(2):
        total = slot_sum(level, level - 1, chips, slot_refs[g], store_ref, staged_ref.at[g], gathered)
        sums.append(total + older_refs[g][...] if level > 1 else total)
    straight = core == col
    kept_ref[...] = jnp.where(straight, sums[0], sums[1])
    sent_ref[...] = jnp.where(straight, sums[1], sums[0])


def inner_kernel(kept_ref, arrived_ref, rhs_ref, inverse_ref, out_ref, copies_ref):
    solved = solve(rhs_ref[...] - (kept_ref[...] + arrived_ref[...]), inverse_ref[...])
    out_ref[...] = solved
    rounded = solved.astype(jnp.bfloat16)
    for i in range(copies_ref.shape[0]):
        copies_ref[i] = rounded


def last_kernel(first_ref, second_ref, rhs_ref, inverse_ref, *refs):
    done_refs, out_ref = refs[:-1], refs[-1]
    level = len(done_refs)
    for m, done in enumerate(done_refs):
        out_ref[m, 0] = done[...]
    solved = solve(rhs_ref[...] - (first_ref[...] + second_ref[...]), inverse_ref[...])
    out_ref[level, 0] = solved


def paired_shards(row_count, right_sides, factor_blocks, diag_inverses, source_ids, block_counts):
    level_count, _, rhs_count, width = right_sides.shape
    slots = factor_blocks.shape[3]
    rows = rhs_count // 2
    chips = row_count // 2
    later = level_count - 1
    same_core = [[2 * j + k for j in range(chips)] for k in range(2)]
    part = jax.ShapeDtypeStruct((rows, width), jnp.float32)
    rounded_part = jax.ShapeDtypeStruct((rows, width), jnp.bfloat16)
    square = jax.ShapeDtypeStruct((width, width), jnp.bfloat16)
    copies = jax.ShapeDtypeStruct((chips, rows, width), jnp.bfloat16)
    solve_flops = 2 * rows * width * width

    def over_both(x, move):
        pairs = []
        for j in range(chips):
            for k in range(2):
                for c in range(2):
                    tj, tk, tc = move(j, k, c)
                    pairs.append(((2 * j + k) * 2 + c, (2 * tj + tk) * 2 + tc))
        return lax.ppermute(x, ("rows", "cols"), pairs)

    def swap_core(x):
        return lax.ppermute(x, "rows", [(i, i ^ 1) for i in range(row_count)])

    def transpose(x):
        return over_both(x, lambda j, k, c: (j, c, k))

    def spread(x):
        return lax.all_to_all(x, "rows", 0, 0, axis_index_groups=same_core)

    counts = block_counts.reshape(later)
    solved, rounded, live_ids = run(
        first_kernel,
        (
            (part, VMEM),
            (rounded_part, VMEM),
            (jax.ShapeDtypeStruct(source_ids.shape, source_ids.dtype), SMEM),
        ),
        ((source_ids, HBM), (counts, HBM), (right_sides, HBM), (diag_inverses, HBM)),
        scratch=(
            pltpu.SMEM(source_ids.shape, source_ids.dtype),
            pltpu.SMEM(counts.shape, counts.dtype),
            pltpu.VMEM((rows, width), jnp.float32),
            pltpu.VMEM((width, width), jnp.bfloat16),
            pltpu.SemaphoreType.DMA((4,)),
        ),
        flops=solve_flops,
    )
    finished = [solved]
    copied, = run(copies_kernel, ((copies, VMEM),), ((transpose(rounded), VMEM),))
    stores = [spread(copied)]

    slot_args = ((live_ids, SMEM), (swap_core(live_ids), SMEM))
    staged_args = (
        (factor_blocks, HBM),
        (swap_core(factor_blocks), HBM),
        (right_sides, HBM),
        (swap_core(right_sides), HBM),
        (diag_inverses, HBM),
        (swap_core(diag_inverses), HBM),
    )
    staged_shape = jax.ShapeDtypeStruct((2, slots, width, width), jnp.bfloat16)
    gathered = pltpu.VMEM((rows, slots * width), jnp.bfloat16)
    after = ()
    for l in range(1, level_count):
        staged, rhs, inverse, *older = run(
            functools.partial(stage_kernel, l, later, chips),
            ((staged_shape, FIXED), (part, VMEM), (square, VMEM)) + ((part, VMEM), (part, VMEM)) * (l > 1),
            slot_args + staged_args + tuple((x, VMEM) for x in stores[:l - 1]) + after,
            scratch=((pltpu.VMEM(((l - 1) * chips, rows, width), jnp.bfloat16), gathered) if l > 1 else ())
            + (
                pltpu.VMEM((2, rows, width), jnp.float32),
                pltpu.VMEM((2, width, width), jnp.bfloat16),
                pltpu.SemaphoreType.DMA((4,)),
                pltpu.SemaphoreType.DMA((2,)),
            ),
            flops=2 * slots * solve_flops * (l > 1),
            transferred=2 * slots * width * width * 2,
        )
        kept, sent = run(
            functools.partial(sums_kernel, l, chips),
            ((part, VMEM), (part, VMEM)),
            slot_args
            + ((stores[-1], VMEM), (staged, FIXED))
            + tuple((x, VMEM) for x in older)
            + tuple((x, ANY) for x in finished[1:]),
            scratch=(gathered,),
            flops=2 * slots * solve_flops,
            transferred=2 * slots * width * width * 2,
        )
        after = ((kept, ANY),)
        if l < later:
            arrived = lax.ppermute(sent, "cols", [(0, 1), (1, 0)])
            solved, copied = run(
                inner_kernel,
                ((part, VMEM), (copies, VMEM)),
                tuple((x, VMEM) for x in (kept, arrived, rhs, inverse)),
                flops=solve_flops,
            )
            finished.append(transpose(solved))
            stores.append(spread(copied))
    first = over_both(kept, lambda j, k, c: (j, c, k))
    second = over_both(sent, lambda j, k, c: (j, 1 - c, k))
    out, = run(
        last_kernel,
        ((jax.ShapeDtypeStruct((level_count, 1, rows, width), jnp.float32), VMEM),),
        tuple((x, VMEM) for x in (first, second, rhs, inverse, *finished)),
        flops=solve_flops,
    )
    return out


def gather_slots(ids_ref, counts_ref, group, store_ref, gathered, slots, width):
    for k in range(slots):
        piece = store_ref[ids_ref[group, k]]
        live = jnp.where(k < counts_ref[group], 1.0, 0.0).astype(piece.dtype)
        gathered[:, k * width:(k + 1) * width] = piece * live


def level_kernel(groups, ids_ref, counts_ref, store_ref, *refs):
    factor_refs = refs[:groups]
    rhs_ref, inverse_ref, out_ref, rounded_ref, gathered = refs[groups:]
    slots, width = factor_refs[0].shape[0], factor_refs[0].shape[1]
    update = None
    for g in range(groups):
        gather_slots(ids_ref, counts_ref, g, store_ref, gathered, slots, width)
        term = flat_dot(gathered, factor_refs[g])
        update = term if update is None else update + term
    reduced = (rhs_ref[...] - update).astype(jnp.bfloat16)
    solved = jnp.dot(reduced, inverse_ref[...], preferred_element_type=jnp.float32)
    out_ref[...] = solved
    rounded_ref[...] = solved.astype(jnp.bfloat16)


def solve_level(ids, counts, store, factors, rhs, inverse):
    groups = len(factors)
    rows, width = rhs.shape
    slots = factors[0].shape[0]
    vmem = pl.BlockSpec(memory_space=pltpu.VMEM)
    smem = pl.BlockSpec(memory_space=pltpu.SMEM)
    return pl.pallas_call(
        functools.partial(level_kernel, groups),
        out_shape=(
            jax.ShapeDtypeStruct((rows, width), jnp.float32),
            jax.ShapeDtypeStruct((rows, width), jnp.bfloat16),
        ),
        in_specs=[smem, smem, vmem] + [vmem] * groups + [vmem, vmem],
        out_specs=(vmem, vmem),
        scratch_shapes=[pltpu.VMEM((rows, slots * width), jnp.bfloat16)],
        compiler_params=pltpu.CompilerParams(vmem_limit_bytes=VMEM_LIMIT),
        cost_estimate=pl.CostEstimate(
            flops=2 * rows * width * width * (groups * slots + 1),
            bytes_accessed=groups * slots * width * width * 2,
            transcendentals=0,
        ),
    )(ids, counts, store, *factors, rhs, inverse)


def rotated_shards(col_count, right_sides, factor_blocks, diag_inverses, source_ids, block_counts):
    level_count, _, rhs_count, width = right_sides.shape
    share_rows = rhs_count // col_count
    col_index = lax.axis_index("cols")

    described = jnp.concatenate([source_ids[:, 0, 0], block_counts[:, 0, 0][:, None]], axis=1)
    factors = [[factor_blocks[l, 0, 0]] for l in range(level_count - 1)]
    descriptions = [described]
    for shift in range(1, col_count):
        pairs = [(i, (i + shift) % col_count) for i in range(col_count)]
        descriptions.append(lax.ppermute(described, "cols", pairs))
    for l in range(level_count - 1):
        for shift in range(1, col_count):
            pairs = [(i, (i + shift) % col_count) for i in range(col_count)]
            factors[l].append(lax.ppermute(factor_blocks[l, 0, 0], "cols", pairs))
    descriptions = jnp.stack(descriptions)

    rhs = lax.dynamic_slice_in_dim(right_sides[:, 0], col_index * share_rows, share_rows, 1)
    solutions = []
    stores = []
    for l in range(level_count):
        if l == 0:
            own = jnp.dot(
                rhs[0].astype(jnp.bfloat16), diag_inverses[0, 0], preferred_element_type=jnp.float32
            )
            rounded = own.astype(jnp.bfloat16)
        else:
            ids = descriptions[:, l - 1, :-1]
            counts = descriptions[:, l - 1, -1]
            store = stores[0] if l == 1 else jnp.concatenate(stores, axis=0)
            own, rounded = solve_level(ids, counts, store, factors[l - 1], rhs[l], diag_inverses[l, 0])
        solutions.append(own)
        if l < level_count - 1:
            stores.append(lax.all_gather(rounded, "rows", axis=0))
    return jnp.stack(solutions)[:, None]


def solution(mesh):
    row_count, col_count = mesh.shape["rows"], mesh.shape["cols"]
    chips = row_count // 2
    if col_count == 2 and row_count == 2 * chips:
        shards = functools.partial(paired_shards, row_count)
    else:
        shards = functools.partial(rotated_shards, col_count)
    return jax.shard_map(
        shards,
        mesh=mesh,
        in_specs=(
            P(None, "rows", None, None),
            P(None, "rows", "cols", None, None, None),
            P(None, "rows", None, None),
            P(None, "rows", "cols", None),
            P(None, "rows", "cols"),
        ),
        out_specs=P(None, "rows", "cols", None),
        check_vma=False,
    )
```

```python
import functools

import jax
import jax.numpy as jnp
from jax import lax
from jax.experimental import pallas as pl
from jax.experimental.pallas import tpu as pltpu
from jax.sharding import PartitionSpec as P

VMEM_LIMIT = 16 * 1024 * 1024


VMEM = pl.BlockSpec(memory_space=pltpu.VMEM)
SMEM = pl.BlockSpec(memory_space=pltpu.SMEM)
ANY = pl.BlockSpec(memory_space=pl.ANY)
HBM = pl.BlockSpec(memory_space=pltpu.HBM)
FIXED = pl.BlockSpec(memory_space=pltpu.VMEM)
PLACES = {id(HBM): pltpu.HBM, id(FIXED): pltpu.VMEM}


def flat_dot(gathered, factor_ref):
    slots, width = factor_ref.shape[0], factor_ref.shape[1]
    return jnp.dot(
        gathered[...],
        factor_ref[...].reshape(slots * width, width),
        preferred_element_type=jnp.float32,
    )


def run(kernel, outs, args, scratch=(), flops=0, transferred=0):
    out_shape = tuple(PLACES[id(spec)](x.shape, x.dtype) if id(spec) in PLACES else x for x, spec in outs)
    args = tuple(
        (pltpu.with_memory_space_constraint(x, PLACES[id(spec)]) if id(spec) in PLACES else x, spec)
        for x, spec in args
    )
    return pl.pallas_call(
        kernel,
        out_shape=out_shape,
        in_specs=[spec for _, spec in args],
        out_specs=tuple(spec for _, spec in outs),
        scratch_shapes=list(scratch),
        compiler_params=pltpu.CompilerParams(vmem_limit_bytes=VMEM_LIMIT),
        cost_estimate=pl.CostEstimate(flops=flops, bytes_accessed=transferred, transcendentals=0),
    )(*(x for x, _ in args))


def half_of(ref, level, half, rows):
    return ref.at[level, 0, pl.ds(pl.multiple_of(half * rows, rows), rows), :]


def solve(reduced, inverse):
    return jnp.dot(reduced.astype(jnp.bfloat16), inverse, preferred_element_type=jnp.float32)


def start_copies(pairs, sems):
    copies = [pltpu.make_async_copy(src, dst, sems.at[i]) for i, (src, dst) in enumerate(pairs)]
    for copy in copies:
        copy.start()
    return copies


def own_place():
    return lax.rem(lax.axis_index("rows"), 2), lax.axis_index("cols")


def first_kernel(
    ids_ref, counts_ref, rhs_ref, inverse_ref, out_ref, rounded_ref, live_ids_ref,
    ids, counts, rhs, inverse, sems,
):
    _, col = own_place()
    copies = start_copies(
        [
            (ids_ref, ids),
            (counts_ref, counts),
            (half_of(rhs_ref, 0, col, out_ref.shape[0]), rhs),
            (inverse_ref.at[0, 0], inverse),
        ],
        sems,
    )
    copies[0].wait()
    copies[1].wait()
    for l in range(ids.shape[0]):
        for k in range(ids.shape[3]):
            live_ids_ref[l, 0, 0, k] = jnp.where(k < counts[l], ids[l, 0, 0, k], -1)
    copies[2].wait()
    copies[3].wait()
    solved = solve(rhs[...], inverse[...])
    out_ref[...] = solved
    rounded_ref[...] = solved.astype(jnp.bfloat16)


def copies_kernel(rounded_ref, *refs):
    copies_ref = refs[-1]
    for i in range(copies_ref.shape[0]):
        copies_ref[i] = rounded_ref[...]


def slot_sum(level, store_level, chips, ids_ref, store_ref, factor_ref, gathered):
    slots, width = factor_ref.shape[0], factor_ref.shape[1]
    for k in range(slots):
        source_id = ids_ref[level - 1, 0, 0, k]
        source = jnp.maximum(source_id, 0)
        source_level, place = source // (2 * chips), source % (2 * chips) // 2
        live = source_id >= 0
        if store_level is None:
            live = jnp.logical_and(live, source_level < level - 1)
            place = jnp.minimum(source_level, level - 2) * chips + place
        else:
            live = jnp.logical_and(live, source_level == store_level)
        piece = store_ref[place]
        gathered[:, k * width:(k + 1) * width] = piece * jnp.where(live, 1.0, 0.0).astype(piece.dtype)
    return flat_dot(gathered, factor_ref)


def stage_kernel(level, later, chips, *refs):
    inner = level < later
    slot_refs = refs[:2]
    factor_ref, other_factor_ref, rhs_ref, other_rhs_ref, inverse_ref, other_inverse_ref = refs[2:8]
    store_refs = refs[8:7 + level]
    outs = refs[-7 if level == 1 else -11:]
    staged_ref, own_rhs_ref, own_inverse_ref = outs[:3]
    rhs, inverse, sems, factor_sems = outs[-4:]
    core, col = own_place()
    straight = core == col
    rows = own_rhs_ref.shape[0]
    if inner:
        pairs = [
            (half_of(rhs_ref, level, core, rows), rhs.at[0]),
            (half_of(other_rhs_ref, level, core, rows), rhs.at[1]),
            (inverse_ref.at[level, 0], inverse.at[0]),
            (other_inverse_ref.at[level, 0], inverse.at[1]),
        ]
    else:
        pairs = [
            (half_of(rhs_ref, level, col, rows), own_rhs_ref),
            (inverse_ref.at[level, 0], own_inverse_ref),
        ]
    factor_copies = start_copies(
        [
            (factor_ref.at[level - 1, 0, 0], staged_ref.at[0]),
            (other_factor_ref.at[level - 1, 0, 0], staged_ref.at[1]),
        ],
        factor_sems,
    )
    copies = start_copies(pairs, sems)
    if level > 1:
        older_refs, store, gathered = outs[3:5], outs[5], outs[6]
        for m, piece in enumerate(store_refs):
            store[m * chips:(m + 1) * chips] = piece[...]
    for g in range(2):
        factor_copies[g].wait()
        if level > 1:
            older_refs[g][...] = slot_sum(
                level, None, chips, slot_refs[g], store, staged_ref.at[g], gathered
            )
    for copy in copies:
        copy.wait()
    if inner:
        own_rhs_ref[...] = jnp.where(straight, rhs[0], rhs[1])
        own_inverse_ref[...] = jnp.where(straight, inverse[0], inverse[1])


def sums_kernel(level, chips, *refs):
    slot_refs, store_ref, staged_ref = refs[:2], refs[2], refs[3]
    older_refs = refs[4:6]
    kept_ref, sent_ref, gathered = refs[-3:]
    core, col = own_place()
    sums = []
    for g in range(2):
        total = slot_sum(level, level - 1, chips, slot_refs[g], store_ref, staged_ref.at[g], gathered)
        sums.append(total + older_refs[g][...] if level > 1 else total)
    straight = core == col
    kept_ref[...] = jnp.where(straight, sums[0], sums[1])
    sent_ref[...] = jnp.where(straight, sums[1], sums[0])


def inner_kernel(kept_ref, arrived_ref, rhs_ref, inverse_ref, out_ref, copies_ref):
    solved = solve(rhs_ref[...] - (kept_ref[...] + arrived_ref[...]), inverse_ref[...])
    out_ref[...] = solved
    rounded = solved.astype(jnp.bfloat16)
    for i in range(copies_ref.shape[0]):
        copies_ref[i] = rounded


def last_kernel(first_ref, second_ref, rhs_ref, inverse_ref, *refs):
    done_refs, out_ref = refs[:-1], refs[-1]
    level = len(done_refs)
    for m, done in enumerate(done_refs):
        out_ref[m, 0] = done[...]
    solved = solve(rhs_ref[...] - (first_ref[...] + second_ref[...]), inverse_ref[...])
    out_ref[level, 0] = solved


def paired_shards(row_count, right_sides, factor_blocks, diag_inverses, source_ids, block_counts):
    level_count, _, rhs_count, width = right_sides.shape
    slots = factor_blocks.shape[3]
    rows = rhs_count // 2
    chips = row_count // 2
    later = level_count - 1
    same_core = [[2 * j + k for j in range(chips)] for k in range(2)]
    part = jax.ShapeDtypeStruct((rows, width), jnp.float32)
    rounded_part = jax.ShapeDtypeStruct((rows, width), jnp.bfloat16)
    square = jax.ShapeDtypeStruct((width, width), jnp.bfloat16)
    copies = jax.ShapeDtypeStruct((chips, rows, width), jnp.bfloat16)
    solve_flops = 2 * rows * width * width

    def over_both(x, move):
        pairs = []
        for j in range(chips):
            for k in range(2):
                for c in range(2):
                    tj, tk, tc = move(j, k, c)
                    pairs.append(((2 * j + k) * 2 + c, (2 * tj + tk) * 2 + tc))
        return lax.ppermute(x, ("rows", "cols"), pairs)

    def swap_core(x):
        return lax.ppermute(x, "rows", [(i, i ^ 1) for i in range(row_count)])

    def transpose(x):
        return over_both(x, lambda j, k, c: (j, c, k))

    def spread(x):
        return lax.all_to_all(x, "rows", 0, 0, axis_index_groups=same_core)

    counts = block_counts.reshape(later)
    solved, rounded, live_ids = run(
        first_kernel,
        (
            (part, VMEM),
            (rounded_part, VMEM),
            (jax.ShapeDtypeStruct(source_ids.shape, source_ids.dtype), SMEM),
        ),
        ((source_ids, HBM), (counts, HBM), (right_sides, HBM), (diag_inverses, HBM)),
        scratch=(
            pltpu.SMEM(source_ids.shape, source_ids.dtype),
            pltpu.SMEM(counts.shape, counts.dtype),
            pltpu.VMEM((rows, width), jnp.float32),
            pltpu.VMEM((width, width), jnp.bfloat16),
            pltpu.SemaphoreType.DMA((4,)),
        ),
        flops=solve_flops,
    )
    finished = [solved]
    moved = transpose(rounded)
    other_ids = swap_core(live_ids)
    sent_factors, sent_rhs, sent_inverses, _ = lax.optimization_barrier(
        (factor_blocks, right_sides, diag_inverses, other_ids)
    )
    copied, = run(copies_kernel, ((copies, VMEM),), ((moved, VMEM), (other_ids, ANY)))
    stores = [spread(copied)]

    slot_args = ((live_ids, SMEM), (other_ids, SMEM))
    staged_args = (
        (factor_blocks, HBM),
        (swap_core(sent_factors), HBM),
        (right_sides, HBM),
        (swap_core(sent_rhs), HBM),
        (diag_inverses, HBM),
        (swap_core(sent_inverses), HBM),
    )
    staged_shape = jax.ShapeDtypeStruct((2, slots, width, width), jnp.bfloat16)
    gathered = pltpu.VMEM((rows, slots * width), jnp.bfloat16)
    after = ()
    for l in range(1, level_count):
        staged, rhs, inverse, *older = run(
            functools.partial(stage_kernel, l, later, chips),
            ((staged_shape, FIXED), (part, VMEM), (square, VMEM)) + ((part, VMEM), (part, VMEM)) * (l > 1),
            slot_args + staged_args + tuple((x, VMEM) for x in stores[:l - 1]) + after,
            scratch=((pltpu.VMEM(((l - 1) * chips, rows, width), jnp.bfloat16), gathered) if l > 1 else ())
            + (
                pltpu.VMEM((2, rows, width), jnp.float32),
                pltpu.VMEM((2, width, width), jnp.bfloat16),
                pltpu.SemaphoreType.DMA((4,)),
                pltpu.SemaphoreType.DMA((2,)),
            ),
            flops=2 * slots * solve_flops * (l > 1),
            transferred=2 * slots * width * width * 2,
        )
        kept, sent = run(
            functools.partial(sums_kernel, l, chips),
            ((part, VMEM), (part, VMEM)),
            slot_args
            + ((stores[-1], VMEM), (staged, FIXED))
            + tuple((x, VMEM) for x in older)
            + tuple((x, ANY) for x in finished[1:]),
            scratch=(gathered,),
            flops=2 * slots * solve_flops,
            transferred=2 * slots * width * width * 2,
        )
        after = ((kept, ANY),)
        if l < later:
            arrived = lax.ppermute(sent, "cols", [(0, 1), (1, 0)])
            solved, copied = run(
                inner_kernel,
                ((part, VMEM), (copies, VMEM)),
                tuple((x, VMEM) for x in (kept, arrived, rhs, inverse)),
                flops=solve_flops,
            )
            finished.append(transpose(solved))
            stores.append(spread(copied))
    first = over_both(kept, lambda j, k, c: (j, c, k))
    second = over_both(sent, lambda j, k, c: (j, 1 - c, k))
    out, = run(
        last_kernel,
        ((jax.ShapeDtypeStruct((level_count, 1, rows, width), jnp.float32), VMEM),),
        tuple((x, VMEM) for x in (first, second, rhs, inverse, *finished)),
        flops=solve_flops,
    )
    return out


def gather_slots(ids_ref, counts_ref, group, store_ref, gathered, slots, width):
    for k in range(slots):
        piece = store_ref[ids_ref[group, k]]
        live = jnp.where(k < counts_ref[group], 1.0, 0.0).astype(piece.dtype)
        gathered[:, k * width:(k + 1) * width] = piece * live


def level_kernel(groups, ids_ref, counts_ref, store_ref, *refs):
    factor_refs = refs[:groups]
    rhs_ref, inverse_ref, out_ref, rounded_ref, gathered = refs[groups:]
    slots, width = factor_refs[0].shape[0], factor_refs[0].shape[1]
    update = None
    for g in range(groups):
        gather_slots(ids_ref, counts_ref, g, store_ref, gathered, slots, width)
        term = flat_dot(gathered, factor_refs[g])
        update = term if update is None else update + term
    reduced = (rhs_ref[...] - update).astype(jnp.bfloat16)
    solved = jnp.dot(reduced, inverse_ref[...], preferred_element_type=jnp.float32)
    out_ref[...] = solved
    rounded_ref[...] = solved.astype(jnp.bfloat16)


def solve_level(ids, counts, store, factors, rhs, inverse):
    groups = len(factors)
    rows, width = rhs.shape
    slots = factors[0].shape[0]
    vmem = pl.BlockSpec(memory_space=pltpu.VMEM)
    smem = pl.BlockSpec(memory_space=pltpu.SMEM)
    return pl.pallas_call(
        functools.partial(level_kernel, groups),
        out_shape=(
            jax.ShapeDtypeStruct((rows, width), jnp.float32),
            jax.ShapeDtypeStruct((rows, width), jnp.bfloat16),
        ),
        in_specs=[smem, smem, vmem] + [vmem] * groups + [vmem, vmem],
        out_specs=(vmem, vmem),
        scratch_shapes=[pltpu.VMEM((rows, slots * width), jnp.bfloat16)],
        compiler_params=pltpu.CompilerParams(vmem_limit_bytes=VMEM_LIMIT),
        cost_estimate=pl.CostEstimate(
            flops=2 * rows * width * width * (groups * slots + 1),
            bytes_accessed=groups * slots * width * width * 2,
            transcendentals=0,
        ),
    )(ids, counts, store, *factors, rhs, inverse)


def rotated_shards(col_count, right_sides, factor_blocks, diag_inverses, source_ids, block_counts):
    level_count, _, rhs_count, width = right_sides.shape
    share_rows = rhs_count // col_count
    col_index = lax.axis_index("cols")

    described = jnp.concatenate([source_ids[:, 0, 0], block_counts[:, 0, 0][:, None]], axis=1)
    factors = [[factor_blocks[l, 0, 0]] for l in range(level_count - 1)]
    descriptions = [described]
    for shift in range(1, col_count):
        pairs = [(i, (i + shift) % col_count) for i in range(col_count)]
        descriptions.append(lax.ppermute(described, "cols", pairs))
    for l in range(level_count - 1):
        for shift in range(1, col_count):
            pairs = [(i, (i + shift) % col_count) for i in range(col_count)]
            factors[l].append(lax.ppermute(factor_blocks[l, 0, 0], "cols", pairs))
    descriptions = jnp.stack(descriptions)

    rhs = lax.dynamic_slice_in_dim(right_sides[:, 0], col_index * share_rows, share_rows, 1)
    solutions = []
    stores = []
    for l in range(level_count):
        if l == 0:
            own = jnp.dot(
                rhs[0].astype(jnp.bfloat16), diag_inverses[0, 0], preferred_element_type=jnp.float32
            )
            rounded = own.astype(jnp.bfloat16)
        else:
            ids = descriptions[:, l - 1, :-1]
            counts = descriptions[:, l - 1, -1]
            store = stores[0] if l == 1 else jnp.concatenate(stores, axis=0)
            own, rounded = solve_level(ids, counts, store, factors[l - 1], rhs[l], diag_inverses[l, 0])
        solutions.append(own)
        if l < level_count - 1:
            stores.append(lax.all_gather(rounded, "rows", axis=0))
    return jnp.stack(solutions)[:, None]


def solution(mesh):
    row_count, col_count = mesh.shape["rows"], mesh.shape["cols"]
    chips = row_count // 2
    if col_count == 2 and row_count == 2 * chips:
        shards = functools.partial(paired_shards, row_count)
    else:
        shards = functools.partial(rotated_shards, col_count)
    return jax.shard_map(
        shards,
        mesh=mesh,
        in_specs=(
            P(None, "rows", None, None),
            P(None, "rows", "cols", None, None, None),
            P(None, "rows", None, None),
            P(None, "rows", "cols", None),
            P(None, "rows", "cols"),
        ),
        out_specs=P(None, "rows", "cols", None),
        check_vma=False,
    )
```

```python
import functools

import jax
import jax.numpy as jnp
from jax import lax
from jax.experimental import pallas as pl
from jax.experimental.pallas import tpu as pltpu
from jax.sharding import PartitionSpec as P

VMEM_LIMIT = 16 * 1024 * 1024


VMEM = pl.BlockSpec(memory_space=pltpu.VMEM)
SMEM = pl.BlockSpec(memory_space=pltpu.SMEM)
ANY = pl.BlockSpec(memory_space=pl.ANY)
HBM = pl.BlockSpec(memory_space=pltpu.HBM)
FIXED = pl.BlockSpec(memory_space=pltpu.VMEM)
PLACES = {id(HBM): pltpu.HBM, id(FIXED): pltpu.VMEM}


def flat_dot(gathered, factor_ref):
    slots, width = factor_ref.shape[0], factor_ref.shape[1]
    return jnp.dot(
        gathered[...],
        factor_ref[...].reshape(slots * width, width),
        preferred_element_type=jnp.float32,
    )


def run(kernel, outs, args, scratch=(), flops=0, transferred=0):
    out_shape = tuple(PLACES[id(spec)](x.shape, x.dtype) if id(spec) in PLACES else x for x, spec in outs)
    args = tuple(
        (pltpu.with_memory_space_constraint(x, PLACES[id(spec)]) if id(spec) in PLACES else x, spec)
        for x, spec in args
    )
    return pl.pallas_call(
        kernel,
        out_shape=out_shape,
        in_specs=[spec for _, spec in args],
        out_specs=tuple(spec for _, spec in outs),
        scratch_shapes=list(scratch),
        compiler_params=pltpu.CompilerParams(vmem_limit_bytes=VMEM_LIMIT),
        cost_estimate=pl.CostEstimate(flops=flops, bytes_accessed=transferred, transcendentals=0),
    )(*(x for x, _ in args))


def half_of(ref, level, half, rows):
    return ref.at[level, 0, pl.ds(pl.multiple_of(half * rows, rows), rows), :]


def solve(reduced, inverse):
    return jnp.dot(reduced.astype(jnp.bfloat16), inverse, preferred_element_type=jnp.float32)


def start_copies(pairs, sems):
    copies = [pltpu.make_async_copy(src, dst, sems.at[i]) for i, (src, dst) in enumerate(pairs)]
    for copy in copies:
        copy.start()
    return copies


def own_place():
    return lax.rem(lax.axis_index("rows"), 2), lax.axis_index("cols")


def live_kernel(ids_ref, counts_ref, live_ids_ref, ids, counts, sems):
    for copy in start_copies([(ids_ref, ids), (counts_ref, counts)], sems):
        copy.wait()
    for l in range(ids.shape[0]):
        for k in range(ids.shape[3]):
            live_ids_ref[l, 0, 0, k] = jnp.where(k < counts[l], ids[l, 0, 0, k], -1)


def both_pairs(level, rows, core, rhs_refs, inverse_refs, rhs, inverse):
    pairs = [(half_of(ref, level, core, rows), rhs.at[g]) for g, ref in enumerate(rhs_refs)]
    return pairs + [(ref.at[level, 0], inverse.at[g]) for g, ref in enumerate(inverse_refs)]


def first_kernel(
    rhs_ref, other_rhs_ref, inverse_ref, other_inverse_ref, out_ref, copies_ref, rhs, inverse, sems
):
    core, col = own_place()
    straight = core == col
    pairs = both_pairs(
        0, out_ref.shape[0], core, (rhs_ref, other_rhs_ref), (inverse_ref, other_inverse_ref), rhs, inverse
    )
    for copy in start_copies(pairs, sems):
        copy.wait()
    solved = solve(jnp.where(straight, rhs[0], rhs[1]), jnp.where(straight, inverse[0], inverse[1]))
    out_ref[...] = solved
    rounded = solved.astype(jnp.bfloat16)
    for i in range(copies_ref.shape[0]):
        copies_ref[i] = rounded


def slot_sum(level, store_level, chips, ids_ref, store_ref, factor_ref, gathered):
    slots, width = factor_ref.shape[0], factor_ref.shape[1]
    for k in range(slots):
        source_id = ids_ref[level - 1, 0, 0, k]
        source = jnp.maximum(source_id, 0)
        source_level, place = source // (2 * chips), source % (2 * chips) // 2
        live = source_id >= 0
        if store_level is None:
            live = jnp.logical_and(live, source_level < level - 1)
            place = jnp.minimum(source_level, level - 2) * chips + place
        else:
            live = jnp.logical_and(live, source_level == store_level)
        piece = store_ref[place]
        gathered[:, k * width:(k + 1) * width] = piece * jnp.where(live, 1.0, 0.0).astype(piece.dtype)
    return flat_dot(gathered, factor_ref)


def stage_kernel(level, later, chips, *refs):
    inner = level < later
    slot_refs = refs[:2]
    factor_ref, other_factor_ref, rhs_ref, other_rhs_ref, inverse_ref, other_inverse_ref = refs[2:8]
    store_refs = refs[8:7 + level]
    outs = refs[-7 if level == 1 else -11:]
    staged_ref, own_rhs_ref, own_inverse_ref = outs[:3]
    rhs, inverse, sems, factor_sems = outs[-4:]
    core, col = own_place()
    straight = core == col
    rows = own_rhs_ref.shape[0]
    if inner:
        pairs = both_pairs(
            level, rows, core, (rhs_ref, other_rhs_ref), (inverse_ref, other_inverse_ref), rhs, inverse
        )
    else:
        pairs = [
            (half_of(rhs_ref, level, col, rows), own_rhs_ref),
            (inverse_ref.at[level, 0], own_inverse_ref),
        ]
    factor_copies = start_copies(
        [
            (factor_ref.at[level - 1, 0, 0], staged_ref.at[0]),
            (other_factor_ref.at[level - 1, 0, 0], staged_ref.at[1]),
        ],
        factor_sems,
    )
    copies = start_copies(pairs, sems)
    if level > 1:
        older_refs, store, gathered = outs[3:5], outs[5], outs[6]
        for m, piece in enumerate(store_refs):
            store[m * chips:(m + 1) * chips] = piece[...]
    for g in range(2):
        factor_copies[g].wait()
        if level > 1:
            older_refs[g][...] = slot_sum(
                level, None, chips, slot_refs[g], store, staged_ref.at[g], gathered
            )
    for copy in copies:
        copy.wait()
    if inner:
        own_rhs_ref[...] = jnp.where(straight, rhs[0], rhs[1])
        own_inverse_ref[...] = jnp.where(straight, inverse[0], inverse[1])


def sums_kernel(level, chips, *refs):
    slot_refs, store_ref, staged_ref = refs[:2], refs[2], refs[3]
    older_refs = refs[4:6]
    kept_ref, sent_ref, gathered = refs[-3:]
    core, col = own_place()
    sums = []
    for g in range(2):
        total = slot_sum(level, level - 1, chips, slot_refs[g], store_ref, staged_ref.at[g], gathered)
        sums.append(total + older_refs[g][...] if level > 1 else total)
    straight = core == col
    kept_ref[...] = jnp.where(straight, sums[0], sums[1])
    sent_ref[...] = jnp.where(straight, sums[1], sums[0])


def inner_kernel(kept_ref, arrived_ref, rhs_ref, inverse_ref, out_ref, copies_ref):
    solved = solve(rhs_ref[...] - (kept_ref[...] + arrived_ref[...]), inverse_ref[...])
    out_ref[...] = solved
    rounded = solved.astype(jnp.bfloat16)
    for i in range(copies_ref.shape[0]):
        copies_ref[i] = rounded


def last_kernel(first_ref, second_ref, rhs_ref, inverse_ref, *refs):
    done_refs, out_ref = refs[:-1], refs[-1]
    level = len(done_refs)
    for m, done in enumerate(done_refs):
        out_ref[m, 0] = done[...]
    solved = solve(rhs_ref[...] - (first_ref[...] + second_ref[...]), inverse_ref[...])
    out_ref[level, 0] = solved


def paired_shards(row_count, right_sides, factor_blocks, diag_inverses, source_ids, block_counts):
    level_count, _, rhs_count, width = right_sides.shape
    slots = factor_blocks.shape[3]
    rows = rhs_count // 2
    chips = row_count // 2
    later = level_count - 1
    same_core = [[2 * j + k for j in range(chips)] for k in range(2)]
    part = jax.ShapeDtypeStruct((rows, width), jnp.float32)
    square = jax.ShapeDtypeStruct((width, width), jnp.bfloat16)
    copies = jax.ShapeDtypeStruct((chips, rows, width), jnp.bfloat16)
    solve_flops = 2 * rows * width * width

    def over_both(x, move):
        pairs = []
        for j in range(chips):
            for k in range(2):
                for c in range(2):
                    tj, tk, tc = move(j, k, c)
                    pairs.append(((2 * j + k) * 2 + c, (2 * tj + tk) * 2 + tc))
        return lax.ppermute(x, ("rows", "cols"), pairs)

    def swap_core(x):
        return lax.ppermute(x, "rows", [(i, i ^ 1) for i in range(row_count)])

    def transpose(x):
        return over_both(x, lambda j, k, c: (j, c, k))

    def spread(x):
        return lax.all_to_all(x, "rows", 0, 0, axis_index_groups=same_core)

    other_inverses, other_rhs = swap_core(diag_inverses), swap_core(right_sides)
    solved, copied = run(
        first_kernel,
        ((part, VMEM), (copies, VMEM)),
        ((right_sides, HBM), (other_rhs, ANY), (diag_inverses, HBM), (other_inverses, ANY)),
        scratch=(
            pltpu.VMEM((2, rows, width), jnp.float32),
            pltpu.VMEM((2, width, width), jnp.bfloat16),
            pltpu.SemaphoreType.DMA((4,)),
        ),
        flops=solve_flops,
    )
    finished = [transpose(solved)]
    stores = [spread(copied)]

    first_ids, counts, _ = lax.optimization_barrier((source_ids, block_counts.reshape(later), solved))
    live_ids, = run(
        live_kernel,
        ((jax.ShapeDtypeStruct(source_ids.shape, source_ids.dtype), SMEM),),
        ((first_ids, HBM), (counts, HBM)),
        scratch=(
            pltpu.SMEM(source_ids.shape, source_ids.dtype),
            pltpu.SMEM(counts.shape, counts.dtype),
            pltpu.SemaphoreType.DMA((2,)),
        ),
    )
    other_ids = swap_core(live_ids)
    sent_factors, _, _ = lax.optimization_barrier((factor_blocks, other_rhs, other_inverses))
    slot_args = ((live_ids, SMEM), (other_ids, SMEM))
    staged_args = (
        (factor_blocks, HBM),
        (swap_core(sent_factors), HBM),
        (right_sides, HBM),
        (other_rhs, HBM),
        (diag_inverses, HBM),
        (other_inverses, HBM),
    )
    staged_shape = jax.ShapeDtypeStruct((2, slots, width, width), jnp.bfloat16)
    gathered = pltpu.VMEM((rows, slots * width), jnp.bfloat16)
    after = ()
    for l in range(1, level_count):
        staged, rhs, inverse, *older = run(
            functools.partial(stage_kernel, l, later, chips),
            ((staged_shape, FIXED), (part, VMEM), (square, VMEM)) + ((part, VMEM), (part, VMEM)) * (l > 1),
            slot_args + staged_args + tuple((x, VMEM) for x in stores[:l - 1]) + after,
            scratch=((pltpu.VMEM(((l - 1) * chips, rows, width), jnp.bfloat16), gathered) if l > 1 else ())
            + (
                pltpu.VMEM((2, rows, width), jnp.float32),
                pltpu.VMEM((2, width, width), jnp.bfloat16),
                pltpu.SemaphoreType.DMA((4,)),
                pltpu.SemaphoreType.DMA((2,)),
            ),
            flops=2 * slots * solve_flops * (l > 1),
            transferred=2 * slots * width * width * 2,
        )
        kept, sent = run(
            functools.partial(sums_kernel, l, chips),
            ((part, VMEM), (part, VMEM)),
            slot_args
            + ((stores[-1], VMEM), (staged, FIXED))
            + tuple((x, VMEM) for x in older)
            + tuple((x, ANY) for x in finished),
            scratch=(gathered,),
            flops=2 * slots * solve_flops,
            transferred=2 * slots * width * width * 2,
        )
        after = ((kept, ANY),)
        if l < later:
            arrived = lax.ppermute(sent, "cols", [(0, 1), (1, 0)])
            solved, copied = run(
                inner_kernel,
                ((part, VMEM), (copies, VMEM)),
                tuple((x, VMEM) for x in (kept, arrived, rhs, inverse)),
                flops=solve_flops,
            )
            finished.append(transpose(solved))
            stores.append(spread(copied))
    first = over_both(kept, lambda j, k, c: (j, c, k))
    second = over_both(sent, lambda j, k, c: (j, 1 - c, k))
    out, = run(
        last_kernel,
        ((jax.ShapeDtypeStruct((level_count, 1, rows, width), jnp.float32), VMEM),),
        tuple((x, VMEM) for x in (first, second, rhs, inverse, *finished)),
        flops=solve_flops,
    )
    return out


def gather_slots(ids_ref, counts_ref, group, store_ref, gathered, slots, width):
    for k in range(slots):
        piece = store_ref[ids_ref[group, k]]
        live = jnp.where(k < counts_ref[group], 1.0, 0.0).astype(piece.dtype)
        gathered[:, k * width:(k + 1) * width] = piece * live


def level_kernel(groups, ids_ref, counts_ref, store_ref, *refs):
    factor_refs = refs[:groups]
    rhs_ref, inverse_ref, out_ref, rounded_ref, gathered = refs[groups:]
    slots, width = factor_refs[0].shape[0], factor_refs[0].shape[1]
    update = None
    for g in range(groups):
        gather_slots(ids_ref, counts_ref, g, store_ref, gathered, slots, width)
        term = flat_dot(gathered, factor_refs[g])
        update = term if update is None else update + term
    reduced = (rhs_ref[...] - update).astype(jnp.bfloat16)
    solved = jnp.dot(reduced, inverse_ref[...], preferred_element_type=jnp.float32)
    out_ref[...] = solved
    rounded_ref[...] = solved.astype(jnp.bfloat16)


def solve_level(ids, counts, store, factors, rhs, inverse):
    groups = len(factors)
    rows, width = rhs.shape
    slots = factors[0].shape[0]
    vmem = pl.BlockSpec(memory_space=pltpu.VMEM)
    smem = pl.BlockSpec(memory_space=pltpu.SMEM)
    return pl.pallas_call(
        functools.partial(level_kernel, groups),
        out_shape=(
            jax.ShapeDtypeStruct((rows, width), jnp.float32),
            jax.ShapeDtypeStruct((rows, width), jnp.bfloat16),
        ),
        in_specs=[smem, smem, vmem] + [vmem] * groups + [vmem, vmem],
        out_specs=(vmem, vmem),
        scratch_shapes=[pltpu.VMEM((rows, slots * width), jnp.bfloat16)],
        compiler_params=pltpu.CompilerParams(vmem_limit_bytes=VMEM_LIMIT),
        cost_estimate=pl.CostEstimate(
            flops=2 * rows * width * width * (groups * slots + 1),
            bytes_accessed=groups * slots * width * width * 2,
            transcendentals=0,
        ),
    )(ids, counts, store, *factors, rhs, inverse)


def rotated_shards(col_count, right_sides, factor_blocks, diag_inverses, source_ids, block_counts):
    level_count, _, rhs_count, width = right_sides.shape
    share_rows = rhs_count // col_count
    col_index = lax.axis_index("cols")

    described = jnp.concatenate([source_ids[:, 0, 0], block_counts[:, 0, 0][:, None]], axis=1)
    factors = [[factor_blocks[l, 0, 0]] for l in range(level_count - 1)]
    descriptions = [described]
    for shift in range(1, col_count):
        pairs = [(i, (i + shift) % col_count) for i in range(col_count)]
        descriptions.append(lax.ppermute(described, "cols", pairs))
    for l in range(level_count - 1):
        for shift in range(1, col_count):
            pairs = [(i, (i + shift) % col_count) for i in range(col_count)]
            factors[l].append(lax.ppermute(factor_blocks[l, 0, 0], "cols", pairs))
    descriptions = jnp.stack(descriptions)

    rhs = lax.dynamic_slice_in_dim(right_sides[:, 0], col_index * share_rows, share_rows, 1)
    solutions = []
    stores = []
    for l in range(level_count):
        if l == 0:
            own = jnp.dot(
                rhs[0].astype(jnp.bfloat16), diag_inverses[0, 0], preferred_element_type=jnp.float32
            )
            rounded = own.astype(jnp.bfloat16)
        else:
            ids = descriptions[:, l - 1, :-1]
            counts = descriptions[:, l - 1, -1]
            store = stores[0] if l == 1 else jnp.concatenate(stores, axis=0)
            own, rounded = solve_level(ids, counts, store, factors[l - 1], rhs[l], diag_inverses[l, 0])
        solutions.append(own)
        if l < level_count - 1:
            stores.append(lax.all_gather(rounded, "rows", axis=0))
    return jnp.stack(solutions)[:, None]


def solution(mesh):
    row_count, col_count = mesh.shape["rows"], mesh.shape["cols"]
    chips = row_count // 2
    if col_count == 2 and row_count == 2 * chips:
        shards = functools.partial(paired_shards, row_count)
    else:
        shards = functools.partial(rotated_shards, col_count)
    return jax.shard_map(
        shards,
        mesh=mesh,
        in_specs=(
            P(None, "rows", None, None),
            P(None, "rows", "cols", None, None, None),
            P(None, "rows", None, None),
            P(None, "rows", "cols", None),
            P(None, "rows", "cols"),
        ),
        out_specs=P(None, "rows", "cols", None),
        check_vma=False,
    )
```

```python
import functools

import jax
import jax.numpy as jnp
from jax import lax
from jax.experimental import pallas as pl
from jax.experimental.pallas import tpu as pltpu
from jax.sharding import PartitionSpec as P

VMEM_LIMIT = 16 * 1024 * 1024


VMEM = pl.BlockSpec(memory_space=pltpu.VMEM)
SMEM = pl.BlockSpec(memory_space=pltpu.SMEM)
ANY = pl.BlockSpec(memory_space=pl.ANY)
HBM = pl.BlockSpec(memory_space=pltpu.HBM)
FIXED = pl.BlockSpec(memory_space=pltpu.VMEM)
PLACES = {id(HBM): pltpu.HBM, id(FIXED): pltpu.VMEM}


def flat_dot(gathered, factor_ref):
    slots, width = factor_ref.shape[0], factor_ref.shape[1]
    return jnp.dot(
        gathered[...],
        factor_ref[...].reshape(slots * width, width),
        preferred_element_type=jnp.float32,
    )


def run(kernel, outs, args, scratch=(), flops=0, transferred=0):
    out_shape = tuple(PLACES[id(spec)](x.shape, x.dtype) if id(spec) in PLACES else x for x, spec in outs)
    args = tuple(
        (pltpu.with_memory_space_constraint(x, PLACES[id(spec)]) if id(spec) in PLACES else x, spec)
        for x, spec in args
    )
    return pl.pallas_call(
        kernel,
        out_shape=out_shape,
        in_specs=[spec for _, spec in args],
        out_specs=tuple(spec for _, spec in outs),
        scratch_shapes=list(scratch),
        compiler_params=pltpu.CompilerParams(vmem_limit_bytes=VMEM_LIMIT),
        cost_estimate=pl.CostEstimate(flops=flops, bytes_accessed=transferred, transcendentals=0),
    )(*(x for x, _ in args))


def half_of(ref, level, half, rows):
    return ref.at[level, 0, pl.ds(pl.multiple_of(half * rows, rows), rows), :]


def solve(reduced, inverse):
    return jnp.dot(reduced.astype(jnp.bfloat16), inverse, preferred_element_type=jnp.float32)


def start_copies(pairs, sems):
    copies = [pltpu.make_async_copy(src, dst, sems.at[i]) for i, (src, dst) in enumerate(pairs)]
    for copy in copies:
        copy.start()
    return copies


def own_place():
    return lax.rem(lax.axis_index("rows"), 2), lax.axis_index("cols")


def prepare_kernel(
    ids_ref, counts_ref, rhs_ref, inverse_ref, live_ids_ref, own_rhs_ref, own_inverse_ref, ids, counts, sems
):
    core, _ = own_place()
    rows = own_rhs_ref.shape[0]
    copies = start_copies(
        [
            (ids_ref, ids),
            (counts_ref, counts),
            (half_of(rhs_ref, 0, core, rows), own_rhs_ref),
            (inverse_ref.at[0, 0], own_inverse_ref),
        ],
        sems,
    )
    copies[0].wait()
    copies[1].wait()
    for l in range(ids.shape[0]):
        for k in range(ids.shape[3]):
            live_ids_ref[l, 0, 0, k] = jnp.where(k < counts[l], ids[l, 0, 0, k], -1)
    copies[2].wait()
    copies[3].wait()


def both_pairs(level, rows, core, rhs_refs, inverse_refs, rhs, inverse):
    pairs = [(half_of(ref, level, core, rows), rhs.at[g]) for g, ref in enumerate(rhs_refs)]
    return pairs + [(ref.at[level, 0], inverse.at[g]) for g, ref in enumerate(inverse_refs)]


def first_kernel(rhs_ref, other_rhs_ref, inverse_ref, other_inverse_ref, *refs):
    out_ref, copies_ref = refs[-2:]
    core, col = own_place()
    straight = core == col
    other_rhs = half_of(other_rhs_ref, 0, core, out_ref.shape[0])[...]
    solved = solve(
        jnp.where(straight, rhs_ref[...], other_rhs),
        jnp.where(straight, inverse_ref[...], other_inverse_ref[0, 0]),
    )
    out_ref[...] = solved
    rounded = solved.astype(jnp.bfloat16)
    for i in range(copies_ref.shape[0]):
        copies_ref[i] = rounded


def slot_sum(level, store_level, chips, ids_ref, store_ref, factor_ref, gathered):
    slots, width = factor_ref.shape[0], factor_ref.shape[1]
    for k in range(slots):
        source_id = ids_ref[level - 1, 0, 0, k]
        source = jnp.maximum(source_id, 0)
        source_level, place = source // (2 * chips), source % (2 * chips) // 2
        live = source_id >= 0
        if store_level is None:
            live = jnp.logical_and(live, source_level < level - 1)
            place = jnp.minimum(source_level, level - 2) * chips + place
        else:
            live = jnp.logical_and(live, source_level == store_level)
        piece = store_ref[place]
        gathered[:, k * width:(k + 1) * width] = piece * jnp.where(live, 1.0, 0.0).astype(piece.dtype)
    return flat_dot(gathered, factor_ref)


def stage_kernel(level, later, chips, *refs):
    inner = level < later
    slot_refs = refs[:2]
    factor_ref, other_factor_ref, rhs_ref, other_rhs_ref, inverse_ref, other_inverse_ref = refs[2:8]
    store_refs = refs[8:7 + level]
    outs = refs[-7 if level == 1 else -11:]
    staged_ref, own_rhs_ref, own_inverse_ref = outs[:3]
    rhs, inverse, sems, factor_sems = outs[-4:]
    core, col = own_place()
    straight = core == col
    rows = own_rhs_ref.shape[0]
    if inner:
        pairs = both_pairs(
            level, rows, core, (rhs_ref, other_rhs_ref), (inverse_ref, other_inverse_ref), rhs, inverse
        )
    else:
        pairs = [
            (half_of(rhs_ref, level, col, rows), own_rhs_ref),
            (inverse_ref.at[level, 0], own_inverse_ref),
        ]
    factor_copies = start_copies(
        [
            (factor_ref.at[level - 1, 0, 0], staged_ref.at[0]),
            (other_factor_ref.at[level - 1, 0, 0], staged_ref.at[1]),
        ],
        factor_sems,
    )
    copies = start_copies(pairs, sems)
    if level > 1:
        older_refs, store, gathered = outs[3:5], outs[5], outs[6]
        for m, piece in enumerate(store_refs):
            store[m * chips:(m + 1) * chips] = piece[...]
    for g in range(2):
        factor_copies[g].wait()
        if level > 1:
            older_refs[g][...] = slot_sum(
                level, None, chips, slot_refs[g], store, staged_ref.at[g], gathered
            )
    for copy in copies:
        copy.wait()
    if inner:
        own_rhs_ref[...] = jnp.where(straight, rhs[0], rhs[1])
        own_inverse_ref[...] = jnp.where(straight, inverse[0], inverse[1])


def sums_kernel(level, chips, *refs):
    slot_refs, store_ref, staged_ref = refs[:2], refs[2], refs[3]
    older_refs = refs[4:6]
    kept_ref, sent_ref, gathered = refs[-3:]
    core, col = own_place()
    sums = []
    for g in range(2):
        total = slot_sum(level, level - 1, chips, slot_refs[g], store_ref, staged_ref.at[g], gathered)
        sums.append(total + older_refs[g][...] if level > 1 else total)
    straight = core == col
    kept_ref[...] = jnp.where(straight, sums[0], sums[1])
    sent_ref[...] = jnp.where(straight, sums[1], sums[0])


def inner_kernel(kept_ref, arrived_ref, rhs_ref, inverse_ref, out_ref, copies_ref):
    solved = solve(rhs_ref[...] - (kept_ref[...] + arrived_ref[...]), inverse_ref[...])
    out_ref[...] = solved
    rounded = solved.astype(jnp.bfloat16)
    for i in range(copies_ref.shape[0]):
        copies_ref[i] = rounded


def last_kernel(first_ref, second_ref, rhs_ref, inverse_ref, *refs):
    done_refs, out_ref = refs[:-1], refs[-1]
    level = len(done_refs)
    for m, done in enumerate(done_refs):
        out_ref[m, 0] = done[...]
    solved = solve(rhs_ref[...] - (first_ref[...] + second_ref[...]), inverse_ref[...])
    out_ref[level, 0] = solved


def paired_shards(row_count, right_sides, factor_blocks, diag_inverses, source_ids, block_counts):
    level_count, _, rhs_count, width = right_sides.shape
    slots = factor_blocks.shape[3]
    rows = rhs_count // 2
    chips = row_count // 2
    later = level_count - 1
    same_core = [[2 * j + k for j in range(chips)] for k in range(2)]
    part = jax.ShapeDtypeStruct((rows, width), jnp.float32)
    square = jax.ShapeDtypeStruct((width, width), jnp.bfloat16)
    copies = jax.ShapeDtypeStruct((chips, rows, width), jnp.bfloat16)
    solve_flops = 2 * rows * width * width

    def over_both(x, move):
        pairs = []
        for j in range(chips):
            for k in range(2):
                for c in range(2):
                    tj, tk, tc = move(j, k, c)
                    pairs.append(((2 * j + k) * 2 + c, (2 * tj + tk) * 2 + tc))
        return lax.ppermute(x, ("rows", "cols"), pairs)

    def swap_core(x):
        return lax.ppermute(x, "rows", [(i, i ^ 1) for i in range(row_count)])

    def transpose(x):
        return over_both(x, lambda j, k, c: (j, c, k))

    def spread(x):
        return lax.all_to_all(x, "rows", 0, 0, axis_index_groups=same_core)

    other_inverses, other_rhs = swap_core(diag_inverses), swap_core(right_sides)
    counts = block_counts.reshape(later)
    live_ids, own_rhs, own_inverse = run(
        prepare_kernel,
        (
            (jax.ShapeDtypeStruct(source_ids.shape, source_ids.dtype), SMEM),
            (part, VMEM),
            (square, VMEM),
        ),
        ((source_ids, HBM), (counts, HBM), (right_sides, HBM), (diag_inverses, HBM)),
        scratch=(
            pltpu.SMEM(source_ids.shape, source_ids.dtype),
            pltpu.SMEM(counts.shape, counts.dtype),
            pltpu.SemaphoreType.DMA((4,)),
        ),
    )
    other_ids = swap_core(live_ids)
    solved, copied = run(
        first_kernel,
        ((part, VMEM), (copies, VMEM)),
        ((own_rhs, VMEM), (other_rhs, VMEM), (own_inverse, VMEM), (other_inverses, VMEM), (other_ids, ANY)),
        flops=solve_flops,
    )
    finished = []
    stores = [spread(copied)]
    sent_factors, _, _, _ = lax.optimization_barrier((factor_blocks, other_rhs, other_inverses, other_ids))
    slot_args = ((live_ids, SMEM), (other_ids, SMEM))
    staged_args = (
        (factor_blocks, HBM),
        (swap_core(sent_factors), HBM),
        (right_sides, HBM),
        (other_rhs, HBM),
        (diag_inverses, HBM),
        (other_inverses, HBM),
    )
    staged_shape = jax.ShapeDtypeStruct((2, slots, width, width), jnp.bfloat16)
    gathered = pltpu.VMEM((rows, slots * width), jnp.bfloat16)
    after = ()
    for l in range(1, level_count):
        staged, rhs, inverse, *older = run(
            functools.partial(stage_kernel, l, later, chips),
            ((staged_shape, FIXED), (part, VMEM), (square, VMEM)) + ((part, VMEM), (part, VMEM)) * (l > 1),
            slot_args + staged_args + tuple((x, VMEM) for x in stores[:l - 1]) + after,
            scratch=((pltpu.VMEM(((l - 1) * chips, rows, width), jnp.bfloat16), gathered) if l > 1 else ())
            + (
                pltpu.VMEM((2, rows, width), jnp.float32),
                pltpu.VMEM((2, width, width), jnp.bfloat16),
                pltpu.SemaphoreType.DMA((4,)),
                pltpu.SemaphoreType.DMA((2,)),
            ),
            flops=2 * slots * solve_flops * (l > 1),
            transferred=2 * slots * width * width * 2,
        )
        kept, sent = run(
            functools.partial(sums_kernel, l, chips),
            ((part, VMEM), (part, VMEM)),
            slot_args
            + ((stores[-1], VMEM), (staged, FIXED))
            + tuple((x, VMEM) for x in older)
            + tuple((x, ANY) for x in finished),
            scratch=(gathered,),
            flops=2 * slots * solve_flops,
            transferred=2 * slots * width * width * 2,
        )
        after = ((kept, ANY),)
        if l < later:
            arrived = lax.ppermute(sent, "cols", [(0, 1), (1, 0)])
            before = solved
            solved, copied = run(
                inner_kernel,
                ((part, VMEM), (copies, VMEM)),
                tuple((x, VMEM) for x in (kept, arrived, rhs, inverse)),
                flops=solve_flops,
            )
            if l == 1:
                before, solved = lax.optimization_barrier((before, solved))
                finished.append(transpose(before))
            finished.append(transpose(solved))
            stores.append(spread(copied))
    first = over_both(kept, lambda j, k, c: (j, c, k))
    second = over_both(sent, lambda j, k, c: (j, 1 - c, k))
    out, = run(
        last_kernel,
        ((jax.ShapeDtypeStruct((level_count, 1, rows, width), jnp.float32), VMEM),),
        tuple((x, VMEM) for x in (first, second, rhs, inverse, *finished)),
        flops=solve_flops,
    )
    return out


def gather_slots(ids_ref, counts_ref, group, store_ref, gathered, slots, width):
    for k in range(slots):
        piece = store_ref[ids_ref[group, k]]
        live = jnp.where(k < counts_ref[group], 1.0, 0.0).astype(piece.dtype)
        gathered[:, k * width:(k + 1) * width] = piece * live


def level_kernel(groups, ids_ref, counts_ref, store_ref, *refs):
    factor_refs = refs[:groups]
    rhs_ref, inverse_ref, out_ref, rounded_ref, gathered = refs[groups:]
    slots, width = factor_refs[0].shape[0], factor_refs[0].shape[1]
    update = None
    for g in range(groups):
        gather_slots(ids_ref, counts_ref, g, store_ref, gathered, slots, width)
        term = flat_dot(gathered, factor_refs[g])
        update = term if update is None else update + term
    reduced = (rhs_ref[...] - update).astype(jnp.bfloat16)
    solved = jnp.dot(reduced, inverse_ref[...], preferred_element_type=jnp.float32)
    out_ref[...] = solved
    rounded_ref[...] = solved.astype(jnp.bfloat16)


def solve_level(ids, counts, store, factors, rhs, inverse):
    groups = len(factors)
    rows, width = rhs.shape
    slots = factors[0].shape[0]
    vmem = pl.BlockSpec(memory_space=pltpu.VMEM)
    smem = pl.BlockSpec(memory_space=pltpu.SMEM)
    return pl.pallas_call(
        functools.partial(level_kernel, groups),
        out_shape=(
            jax.ShapeDtypeStruct((rows, width), jnp.float32),
            jax.ShapeDtypeStruct((rows, width), jnp.bfloat16),
        ),
        in_specs=[smem, smem, vmem] + [vmem] * groups + [vmem, vmem],
        out_specs=(vmem, vmem),
        scratch_shapes=[pltpu.VMEM((rows, slots * width), jnp.bfloat16)],
        compiler_params=pltpu.CompilerParams(vmem_limit_bytes=VMEM_LIMIT),
        cost_estimate=pl.CostEstimate(
            flops=2 * rows * width * width * (groups * slots + 1),
            bytes_accessed=groups * slots * width * width * 2,
            transcendentals=0,
        ),
    )(ids, counts, store, *factors, rhs, inverse)


def rotated_shards(col_count, right_sides, factor_blocks, diag_inverses, source_ids, block_counts):
    level_count, _, rhs_count, width = right_sides.shape
    share_rows = rhs_count // col_count
    col_index = lax.axis_index("cols")

    described = jnp.concatenate([source_ids[:, 0, 0], block_counts[:, 0, 0][:, None]], axis=1)
    factors = [[factor_blocks[l, 0, 0]] for l in range(level_count - 1)]
    descriptions = [described]
    for shift in range(1, col_count):
        pairs = [(i, (i + shift) % col_count) for i in range(col_count)]
        descriptions.append(lax.ppermute(described, "cols", pairs))
    for l in range(level_count - 1):
        for shift in range(1, col_count):
            pairs = [(i, (i + shift) % col_count) for i in range(col_count)]
            factors[l].append(lax.ppermute(factor_blocks[l, 0, 0], "cols", pairs))
    descriptions = jnp.stack(descriptions)

    rhs = lax.dynamic_slice_in_dim(right_sides[:, 0], col_index * share_rows, share_rows, 1)
    solutions = []
    stores = []
    for l in range(level_count):
        if l == 0:
            own = jnp.dot(
                rhs[0].astype(jnp.bfloat16), diag_inverses[0, 0], preferred_element_type=jnp.float32
            )
            rounded = own.astype(jnp.bfloat16)
        else:
            ids = descriptions[:, l - 1, :-1]
            counts = descriptions[:, l - 1, -1]
            store = stores[0] if l == 1 else jnp.concatenate(stores, axis=0)
            own, rounded = solve_level(ids, counts, store, factors[l - 1], rhs[l], diag_inverses[l, 0])
        solutions.append(own)
        if l < level_count - 1:
            stores.append(lax.all_gather(rounded, "rows", axis=0))
    return jnp.stack(solutions)[:, None]


def solution(mesh):
    row_count, col_count = mesh.shape["rows"], mesh.shape["cols"]
    chips = row_count // 2
    if col_count == 2 and row_count == 2 * chips:
        shards = functools.partial(paired_shards, row_count)
    else:
        shards = functools.partial(rotated_shards, col_count)
    return jax.shard_map(
        shards,
        mesh=mesh,
        in_specs=(
            P(None, "rows", None, None),
            P(None, "rows", "cols", None, None, None),
            P(None, "rows", None, None),
            P(None, "rows", "cols", None),
            P(None, "rows", "cols"),
        ),
        out_specs=P(None, "rows", "cols", None),
        check_vma=False,
    )
```

```python
import functools

import jax
import jax.numpy as jnp
from jax import lax
from jax.experimental import pallas as pl
from jax.experimental.pallas import tpu as pltpu
from jax.sharding import PartitionSpec as P

VMEM_LIMIT = 16 * 1024 * 1024


VMEM = pl.BlockSpec(memory_space=pltpu.VMEM)
SMEM = pl.BlockSpec(memory_space=pltpu.SMEM)
ANY = pl.BlockSpec(memory_space=pl.ANY)
HBM = pl.BlockSpec(memory_space=pltpu.HBM)
FIXED = pl.BlockSpec(memory_space=pltpu.VMEM)
PLACES = {id(HBM): pltpu.HBM, id(FIXED): pltpu.VMEM}


def flat_dot(gathered, factor_ref):
    slots, width = factor_ref.shape[0], factor_ref.shape[1]
    return jnp.dot(
        gathered[...],
        factor_ref[...].reshape(slots * width, width),
        preferred_element_type=jnp.float32,
    )


def run(kernel, outs, args, scratch=(), flops=0, transferred=0):
    out_shape = tuple(PLACES[id(spec)](x.shape, x.dtype) if id(spec) in PLACES else x for x, spec in outs)
    args = tuple(
        (pltpu.with_memory_space_constraint(x, PLACES[id(spec)]) if id(spec) in PLACES else x, spec)
        for x, spec in args
    )
    return pl.pallas_call(
        kernel,
        out_shape=out_shape,
        in_specs=[spec for _, spec in args],
        out_specs=tuple(spec for _, spec in outs),
        scratch_shapes=list(scratch),
        compiler_params=pltpu.CompilerParams(vmem_limit_bytes=VMEM_LIMIT),
        cost_estimate=pl.CostEstimate(flops=flops, bytes_accessed=transferred, transcendentals=0),
    )(*(x for x, _ in args))


def half_of(ref, level, half, rows):
    return ref.at[level, 0, pl.ds(pl.multiple_of(half * rows, rows), rows), :]


def solve(reduced, inverse):
    return jnp.dot(reduced.astype(jnp.bfloat16), inverse, preferred_element_type=jnp.float32)


def start_copies(pairs, sems):
    copies = [pltpu.make_async_copy(src, dst, sems.at[i]) for i, (src, dst) in enumerate(pairs)]
    for copy in copies:
        copy.start()
    return copies


def own_place():
    return lax.rem(lax.axis_index("rows"), 2), lax.axis_index("cols")


def prepare_kernel(
    ids_ref, counts_ref, rhs_ref, inverse_ref, live_ids_ref, own_rhs_ref, own_inverse_ref, ids, counts, sems
):
    core, _ = own_place()
    rows = own_rhs_ref.shape[0]
    copies = start_copies(
        [
            (ids_ref, ids),
            (counts_ref, counts),
            (half_of(rhs_ref, 0, core, rows), own_rhs_ref),
            (inverse_ref.at[0, 0], own_inverse_ref),
        ],
        sems,
    )
    copies[0].wait()
    copies[1].wait()
    for l in range(ids.shape[0]):
        for k in range(ids.shape[3]):
            live_ids_ref[l, 0, 0, k] = jnp.where(k < counts[l], ids[l, 0, 0, k], -1)
    copies[2].wait()
    copies[3].wait()


def both_pairs(level, rows, core, rhs_refs, inverse_refs, rhs, inverse):
    pairs = [(half_of(ref, level, core, rows), rhs.at[g]) for g, ref in enumerate(rhs_refs)]
    return pairs + [(ref.at[level, 0], inverse.at[g]) for g, ref in enumerate(inverse_refs)]


def first_kernel(rhs_ref, other_rhs_ref, inverse_ref, other_inverse_ref, *refs):
    out_ref, copies_ref = refs[-2:]
    core, col = own_place()
    straight = core == col
    other_rhs = half_of(other_rhs_ref, 0, core, out_ref.shape[0])[...]
    solved = solve(
        jnp.where(straight, rhs_ref[...], other_rhs),
        jnp.where(straight, inverse_ref[...], other_inverse_ref[0, 0]),
    )
    out_ref[...] = solved
    rounded = solved.astype(jnp.bfloat16)
    for i in range(copies_ref.shape[0]):
        copies_ref[i] = rounded


def slot_sum(level, store_level, chips, ids_ref, store_ref, factor_ref, gathered):
    slots, width = factor_ref.shape[0], factor_ref.shape[1]
    for k in range(slots):
        source_id = ids_ref[level - 1, 0, 0, k]
        source = jnp.maximum(source_id, 0)
        source_level, place = source // (2 * chips), source % (2 * chips) // 2
        live = source_id >= 0
        if store_level is None:
            live = jnp.logical_and(live, source_level < level - 1)
            place = jnp.minimum(source_level, level - 2) * chips + place
        else:
            live = jnp.logical_and(live, source_level == store_level)
        piece = store_ref[place]
        gathered[:, k * width:(k + 1) * width] = piece * jnp.where(live, 1.0, 0.0).astype(piece.dtype)
    return flat_dot(gathered, factor_ref)


def stage_kernel(level, later, chips, *refs):
    inner = level < later
    slot_refs = refs[:2]
    factor_ref, other_factor_ref, rhs_ref, other_rhs_ref, inverse_ref, other_inverse_ref = refs[2:8]
    store_refs = refs[8:7 + level]
    outs = refs[-7 if level == 1 else -11:]
    staged_ref, own_rhs_ref, own_inverse_ref = outs[:3]
    rhs, inverse, sems, factor_sems = outs[-4:]
    core, col = own_place()
    straight = core == col
    rows = own_rhs_ref.shape[0]
    if inner:
        pairs = both_pairs(
            level, rows, core, (rhs_ref, other_rhs_ref), (inverse_ref, other_inverse_ref), rhs, inverse
        )
    else:
        pairs = [
            (half_of(rhs_ref, level, col, rows), own_rhs_ref),
            (inverse_ref.at[level, 0], own_inverse_ref),
        ]
    factor_copies = start_copies(
        [
            (factor_ref.at[level - 1, 0, 0], staged_ref.at[0]),
            (other_factor_ref.at[level - 1, 0, 0], staged_ref.at[1]),
        ],
        factor_sems,
    )
    copies = start_copies(pairs, sems)
    if level > 1:
        older_refs, store, gathered = outs[3:5], outs[5], outs[6]
        for m, piece in enumerate(store_refs):
            store[m * chips:(m + 1) * chips] = piece[...]
    for g in range(2):
        factor_copies[g].wait()
        if level > 1:
            older_refs[g][...] = slot_sum(
                level, None, chips, slot_refs[g], store, staged_ref.at[g], gathered
            )
    for copy in copies:
        copy.wait()
    if inner:
        own_rhs_ref[...] = jnp.where(straight, rhs[0], rhs[1])
        own_inverse_ref[...] = jnp.where(straight, inverse[0], inverse[1])


def sums_kernel(level, chips, *refs):
    slot_refs, store_ref, staged_ref = refs[:2], refs[2], refs[3]
    older_refs = refs[4:6]
    kept_ref, sent_ref, gathered = refs[-3:]
    core, col = own_place()
    sums = []
    for g in range(2):
        total = slot_sum(level, level - 1, chips, slot_refs[g], store_ref, staged_ref.at[g], gathered)
        sums.append(total + older_refs[g][...] if level > 1 else total)
    straight = core == col
    kept_ref[...] = jnp.where(straight, sums[0], sums[1]).astype(kept_ref.dtype)
    sent_ref[...] = jnp.where(straight, sums[1], sums[0]).astype(sent_ref.dtype)


def inner_kernel(kept_ref, arrived_ref, rhs_ref, inverse_ref, out_ref, copies_ref):
    update = kept_ref[...] + arrived_ref[...].astype(jnp.float32)
    solved = solve(rhs_ref[...] - update, inverse_ref[...])
    out_ref[...] = solved
    rounded = solved.astype(jnp.bfloat16)
    for i in range(copies_ref.shape[0]):
        copies_ref[i] = rounded


def last_kernel(first_ref, second_ref, rhs_ref, inverse_ref, *refs):
    done_refs, out_ref = refs[:-1], refs[-1]
    level = len(done_refs)
    for m, done in enumerate(done_refs):
        out_ref[m, 0] = done[...]
    update = first_ref[...].astype(jnp.float32) + second_ref[...].astype(jnp.float32)
    solved = solve(rhs_ref[...] - update, inverse_ref[...])
    out_ref[level, 0] = solved


def paired_shards(row_count, right_sides, factor_blocks, diag_inverses, source_ids, block_counts):
    level_count, _, rhs_count, width = right_sides.shape
    slots = factor_blocks.shape[3]
    rows = rhs_count // 2
    chips = row_count // 2
    later = level_count - 1
    same_core = [[2 * j + k for j in range(chips)] for k in range(2)]
    part = jax.ShapeDtypeStruct((rows, width), jnp.float32)
    rounded_part = jax.ShapeDtypeStruct((rows, width), jnp.bfloat16)
    square = jax.ShapeDtypeStruct((width, width), jnp.bfloat16)
    copies = jax.ShapeDtypeStruct((chips, rows, width), jnp.bfloat16)
    solve_flops = 2 * rows * width * width

    def over_both(x, move):
        pairs = []
        for j in range(chips):
            for k in range(2):
                for c in range(2):
                    tj, tk, tc = move(j, k, c)
                    pairs.append(((2 * j + k) * 2 + c, (2 * tj + tk) * 2 + tc))
        return lax.ppermute(x, ("rows", "cols"), pairs)

    def swap_core(x):
        return lax.ppermute(x, "rows", [(i, i ^ 1) for i in range(row_count)])

    def transpose(x):
        return over_both(x, lambda j, k, c: (j, c, k))

    def spread(x):
        return lax.all_to_all(x, "rows", 0, 0, axis_index_groups=same_core)

    other_inverses, other_rhs = swap_core(diag_inverses), swap_core(right_sides)
    counts = block_counts.reshape(later)
    live_ids, own_rhs, own_inverse = run(
        prepare_kernel,
        (
            (jax.ShapeDtypeStruct(source_ids.shape, source_ids.dtype), SMEM),
            (part, VMEM),
            (square, VMEM),
        ),
        ((source_ids, HBM), (counts, HBM), (right_sides, HBM), (diag_inverses, HBM)),
        scratch=(
            pltpu.SMEM(source_ids.shape, source_ids.dtype),
            pltpu.SMEM(counts.shape, counts.dtype),
            pltpu.SemaphoreType.DMA((4,)),
        ),
    )
    other_ids = swap_core(live_ids)
    solved, copied = run(
        first_kernel,
        ((part, VMEM), (copies, VMEM)),
        ((own_rhs, VMEM), (other_rhs, VMEM), (own_inverse, VMEM), (other_inverses, VMEM), (other_ids, ANY)),
        flops=solve_flops,
    )
    finished = [transpose(solved)]
    stores = [spread(copied)]
    sent_factors, _, _, _ = lax.optimization_barrier((factor_blocks, other_rhs, other_inverses, other_ids))
    slot_args = ((live_ids, SMEM), (other_ids, SMEM))
    staged_args = (
        (factor_blocks, HBM),
        (swap_core(sent_factors), HBM),
        (right_sides, HBM),
        (other_rhs, HBM),
        (diag_inverses, HBM),
        (other_inverses, HBM),
    )
    staged_shape = jax.ShapeDtypeStruct((2, slots, width, width), jnp.bfloat16)
    gathered = pltpu.VMEM((rows, slots * width), jnp.bfloat16)
    after = ()
    for l in range(1, level_count):
        staged, rhs, inverse, *older = run(
            functools.partial(stage_kernel, l, later, chips),
            ((staged_shape, FIXED), (part, VMEM), (square, VMEM)) + ((part, VMEM), (part, VMEM)) * (l > 1),
            slot_args + staged_args + tuple((x, VMEM) for x in stores[:l - 1]) + after,
            scratch=((pltpu.VMEM(((l - 1) * chips, rows, width), jnp.bfloat16), gathered) if l > 1 else ())
            + (
                pltpu.VMEM((2, rows, width), jnp.float32),
                pltpu.VMEM((2, width, width), jnp.bfloat16),
                pltpu.SemaphoreType.DMA((4,)),
                pltpu.SemaphoreType.DMA((2,)),
            ),
            flops=2 * slots * solve_flops * (l > 1),
            transferred=2 * slots * width * width * 2,
        )
        kept, sent = run(
            functools.partial(sums_kernel, l, chips),
            ((part if l < later else rounded_part, VMEM), (rounded_part, VMEM)),
            slot_args
            + ((stores[-1], VMEM), (staged, FIXED))
            + tuple((x, VMEM) for x in older)
            + tuple((x, ANY) for x in finished),
            scratch=(gathered,),
            flops=2 * slots * solve_flops,
            transferred=2 * slots * width * width * 2,
        )
        after = ((kept, ANY),)
        if l < later:
            arrived = lax.ppermute(sent, "cols", [(0, 1), (1, 0)])
            solved, copied = run(
                inner_kernel,
                ((part, VMEM), (copies, VMEM)),
                tuple((x, VMEM) for x in (kept, arrived, rhs, inverse)),
                flops=solve_flops,
            )
            finished.append(transpose(solved))
            stores.append(spread(copied))
    first = over_both(kept, lambda j, k, c: (j, c, k))
    second = over_both(sent, lambda j, k, c: (j, 1 - c, k))
    out, = run(
        last_kernel,
        ((jax.ShapeDtypeStruct((level_count, 1, rows, width), jnp.float32), VMEM),),
        tuple((x, VMEM) for x in (first, second, rhs, inverse, *finished)),
        flops=solve_flops,
    )
    return out


def gather_slots(ids_ref, counts_ref, group, store_ref, gathered, slots, width):
    for k in range(slots):
        piece = store_ref[ids_ref[group, k]]
        live = jnp.where(k < counts_ref[group], 1.0, 0.0).astype(piece.dtype)
        gathered[:, k * width:(k + 1) * width] = piece * live


def level_kernel(groups, ids_ref, counts_ref, store_ref, *refs):
    factor_refs = refs[:groups]
    rhs_ref, inverse_ref, out_ref, rounded_ref, gathered = refs[groups:]
    slots, width = factor_refs[0].shape[0], factor_refs[0].shape[1]
    update = None
    for g in range(groups):
        gather_slots(ids_ref, counts_ref, g, store_ref, gathered, slots, width)
        term = flat_dot(gathered, factor_refs[g])
        update = term if update is None else update + term
    reduced = (rhs_ref[...] - update).astype(jnp.bfloat16)
    solved = jnp.dot(reduced, inverse_ref[...], preferred_element_type=jnp.float32)
    out_ref[...] = solved
    rounded_ref[...] = solved.astype(jnp.bfloat16)


def solve_level(ids, counts, store, factors, rhs, inverse):
    groups = len(factors)
    rows, width = rhs.shape
    slots = factors[0].shape[0]
    vmem = pl.BlockSpec(memory_space=pltpu.VMEM)
    smem = pl.BlockSpec(memory_space=pltpu.SMEM)
    return pl.pallas_call(
        functools.partial(level_kernel, groups),
        out_shape=(
            jax.ShapeDtypeStruct((rows, width), jnp.float32),
            jax.ShapeDtypeStruct((rows, width), jnp.bfloat16),
        ),
        in_specs=[smem, smem, vmem] + [vmem] * groups + [vmem, vmem],
        out_specs=(vmem, vmem),
        scratch_shapes=[pltpu.VMEM((rows, slots * width), jnp.bfloat16)],
        compiler_params=pltpu.CompilerParams(vmem_limit_bytes=VMEM_LIMIT),
        cost_estimate=pl.CostEstimate(
            flops=2 * rows * width * width * (groups * slots + 1),
            bytes_accessed=groups * slots * width * width * 2,
            transcendentals=0,
        ),
    )(ids, counts, store, *factors, rhs, inverse)


def rotated_shards(col_count, right_sides, factor_blocks, diag_inverses, source_ids, block_counts):
    level_count, _, rhs_count, width = right_sides.shape
    share_rows = rhs_count // col_count
    col_index = lax.axis_index("cols")

    described = jnp.concatenate([source_ids[:, 0, 0], block_counts[:, 0, 0][:, None]], axis=1)
    factors = [[factor_blocks[l, 0, 0]] for l in range(level_count - 1)]
    descriptions = [described]
    for shift in range(1, col_count):
        pairs = [(i, (i + shift) % col_count) for i in range(col_count)]
        descriptions.append(lax.ppermute(described, "cols", pairs))
    for l in range(level_count - 1):
        for shift in range(1, col_count):
            pairs = [(i, (i + shift) % col_count) for i in range(col_count)]
            factors[l].append(lax.ppermute(factor_blocks[l, 0, 0], "cols", pairs))
    descriptions = jnp.stack(descriptions)

    rhs = lax.dynamic_slice_in_dim(right_sides[:, 0], col_index * share_rows, share_rows, 1)
    solutions = []
    stores = []
    for l in range(level_count):
        if l == 0:
            own = jnp.dot(
                rhs[0].astype(jnp.bfloat16), diag_inverses[0, 0], preferred_element_type=jnp.float32
            )
            rounded = own.astype(jnp.bfloat16)
        else:
            ids = descriptions[:, l - 1, :-1]
            counts = descriptions[:, l - 1, -1]
            store = stores[0] if l == 1 else jnp.concatenate(stores, axis=0)
            own, rounded = solve_level(ids, counts, store, factors[l - 1], rhs[l], diag_inverses[l, 0])
        solutions.append(own)
        if l < level_count - 1:
            stores.append(lax.all_gather(rounded, "rows", axis=0))
    return jnp.stack(solutions)[:, None]


def solution(mesh):
    row_count, col_count = mesh.shape["rows"], mesh.shape["cols"]
    chips = row_count // 2
    if col_count == 2 and row_count == 2 * chips:
        shards = functools.partial(paired_shards, row_count)
    else:
        shards = functools.partial(rotated_shards, col_count)
    return jax.shard_map(
        shards,
        mesh=mesh,
        in_specs=(
            P(None, "rows", None, None),
            P(None, "rows", "cols", None, None, None),
            P(None, "rows", None, None),
            P(None, "rows", "cols", None),
            P(None, "rows", "cols"),
        ),
        out_specs=P(None, "rows", "cols", None),
        check_vma=False,
    )
```

```python
import functools

import jax
import jax.numpy as jnp
from jax import lax
from jax.experimental import pallas as pl
from jax.experimental.pallas import tpu as pltpu
from jax.sharding import PartitionSpec as P

VMEM_LIMIT = 16 * 1024 * 1024


VMEM = pl.BlockSpec(memory_space=pltpu.VMEM)
SMEM = pl.BlockSpec(memory_space=pltpu.SMEM)
ANY = pl.BlockSpec(memory_space=pl.ANY)
HBM = pl.BlockSpec(memory_space=pltpu.HBM)
FIXED = pl.BlockSpec(memory_space=pltpu.VMEM)
PLACES = {id(HBM): pltpu.HBM, id(FIXED): pltpu.VMEM}


def flat_dot(gathered, factor_ref):
    slots, width = factor_ref.shape[0], factor_ref.shape[1]
    return jnp.dot(
        gathered[...],
        factor_ref[...].reshape(slots * width, width),
        preferred_element_type=jnp.float32,
    )


def run(kernel, outs, args, scratch=(), flops=0, transferred=0):
    out_shape = tuple(PLACES[id(spec)](x.shape, x.dtype) if id(spec) in PLACES else x for x, spec in outs)
    args = tuple(
        (pltpu.with_memory_space_constraint(x, PLACES[id(spec)]) if id(spec) in PLACES else x, spec)
        for x, spec in args
    )
    return pl.pallas_call(
        kernel,
        out_shape=out_shape,
        in_specs=[spec for _, spec in args],
        out_specs=tuple(spec for _, spec in outs),
        scratch_shapes=list(scratch),
        compiler_params=pltpu.CompilerParams(vmem_limit_bytes=VMEM_LIMIT),
        cost_estimate=pl.CostEstimate(flops=flops, bytes_accessed=transferred, transcendentals=0),
    )(*(x for x, _ in args))


def half_of(ref, level, half, rows):
    return ref.at[level, 0, pl.ds(pl.multiple_of(half * rows, rows), rows), :]


def solve(reduced, inverse):
    return jnp.dot(reduced.astype(jnp.bfloat16), inverse, preferred_element_type=jnp.float32)


def start_copies(pairs, sems):
    copies = [pltpu.make_async_copy(src, dst, sems.at[i]) for i, (src, dst) in enumerate(pairs)]
    for copy in copies:
        copy.start()
    return copies


def own_place():
    return lax.rem(lax.axis_index("rows"), 2), lax.axis_index("cols")


def prepare_kernel(
    ids_ref, counts_ref, rhs_ref, inverse_ref, live_ids_ref, own_rhs_ref, own_inverse_ref, ids, counts, sems
):
    core, _ = own_place()
    rows = own_rhs_ref.shape[0]
    copies = start_copies(
        [
            (ids_ref, ids),
            (counts_ref, counts),
            (half_of(rhs_ref, 0, core, rows), own_rhs_ref),
            (inverse_ref.at[0, 0], own_inverse_ref),
        ],
        sems,
    )
    copies[0].wait()
    copies[1].wait()
    for l in range(ids.shape[0]):
        for k in range(ids.shape[3]):
            live_ids_ref[l, 0, 0, k] = jnp.where(k < counts[l], ids[l, 0, 0, k], -1)
    copies[2].wait()
    copies[3].wait()


def both_pairs(level, rows, core, rhs_refs, inverse_refs, rhs, inverse):
    pairs = [(half_of(ref, level, core, rows), rhs.at[g]) for g, ref in enumerate(rhs_refs)]
    return pairs + [(ref.at[level, 0], inverse.at[g]) for g, ref in enumerate(inverse_refs)]


def first_kernel(rhs_ref, other_rhs_ref, inverse_ref, other_inverse_ref, *refs):
    out_ref, copies_ref = refs[-2:]
    core, col = own_place()
    straight = core == col
    other_rhs = half_of(other_rhs_ref, 0, core, out_ref.shape[0])[...]
    solved = solve(
        jnp.where(straight, rhs_ref[...], other_rhs),
        jnp.where(straight, inverse_ref[...], other_inverse_ref[0, 0]),
    )
    out_ref[...] = solved
    rounded = solved.astype(jnp.bfloat16)
    for i in range(copies_ref.shape[0]):
        copies_ref[i] = rounded


def slot_sum(level, store_level, chips, ids_ref, store_ref, factor_ref, gathered):
    slots, width = factor_ref.shape[0], factor_ref.shape[1]
    for k in range(slots):
        source_id = ids_ref[level - 1, 0, 0, k]
        source = jnp.maximum(source_id, 0)
        source_level, place = source // (2 * chips), source % (2 * chips) // 2
        live = source_id >= 0
        if store_level is None:
            live = jnp.logical_and(live, source_level < level - 1)
            place = jnp.minimum(source_level, level - 2) * chips + place
        else:
            live = jnp.logical_and(live, source_level == store_level)
        piece = store_ref[place]
        gathered[:, k * width:(k + 1) * width] = piece * jnp.where(live, 1.0, 0.0).astype(piece.dtype)
    return flat_dot(gathered, factor_ref)


def stage_kernel(level, later, chips, *refs):
    inner = level < later
    slot_refs = refs[:2]
    factor_ref, other_factor_ref, rhs_ref, other_rhs_ref, inverse_ref, other_inverse_ref = refs[2:8]
    store_refs = refs[8:7 + level]
    outs = refs[-7 if level == 1 else -11:]
    staged_ref, own_rhs_ref, own_inverse_ref = outs[:3]
    rhs, inverse, sems, factor_sems = outs[-4:]
    core, col = own_place()
    straight = core == col
    rows = own_rhs_ref.shape[0]
    if inner:
        pairs = both_pairs(
            level, rows, core, (rhs_ref, other_rhs_ref), (inverse_ref, other_inverse_ref), rhs, inverse
        )
    else:
        pairs = [
            (half_of(rhs_ref, level, col, rows), own_rhs_ref),
            (inverse_ref.at[level, 0], own_inverse_ref),
        ]
    factor_copies = start_copies(
        [
            (factor_ref.at[level - 1, 0, 0], staged_ref.at[0]),
            (other_factor_ref.at[level - 1, 0, 0], staged_ref.at[1]),
        ],
        factor_sems,
    )
    copies = start_copies(pairs, sems)
    if level > 1:
        older_refs, store, gathered = outs[3:5], outs[5], outs[6]
        for m, piece in enumerate(store_refs):
            store[m * chips:(m + 1) * chips] = piece[...]
    for g in range(2):
        factor_copies[g].wait()
        if level > 1:
            older_refs[g][...] = slot_sum(
                level, None, chips, slot_refs[g], store, staged_ref.at[g], gathered
            )
    for copy in copies:
        copy.wait()
    if inner:
        own_rhs_ref[...] = jnp.where(straight, rhs[0], rhs[1])
        own_inverse_ref[...] = jnp.where(straight, inverse[0], inverse[1])


def sums_kernel(level, chips, *refs):
    slot_refs, store_ref, staged_ref = refs[:2], refs[2], refs[3]
    older_refs = refs[4:6]
    kept_ref, sent_ref, gathered = refs[-3:]
    core, col = own_place()
    sums = []
    for g in range(2):
        total = slot_sum(level, level - 1, chips, slot_refs[g], store_ref, staged_ref.at[g], gathered)
        sums.append(total + older_refs[g][...] if level > 1 else total)
    straight = core == col
    kept_ref[...] = jnp.where(straight, sums[0], sums[1]).astype(kept_ref.dtype)
    sent_ref[...] = jnp.where(straight, sums[1], sums[0]).astype(sent_ref.dtype)


def inner_kernel(kept_ref, arrived_ref, rhs_ref, inverse_ref, out_ref, copies_ref):
    update = kept_ref[...] + arrived_ref[...].astype(jnp.float32)
    solved = solve(rhs_ref[...] - update, inverse_ref[...])
    out_ref[...] = solved
    rounded = solved.astype(jnp.bfloat16)
    for i in range(copies_ref.shape[0]):
        copies_ref[i] = rounded


def last_kernel(first_ref, second_ref, rhs_ref, inverse_ref, *refs):
    done_refs, out_ref = refs[:-1], refs[-1]
    level = len(done_refs)
    for m, done in enumerate(done_refs):
        out_ref[m, 0] = done[...]
    update = first_ref[...].astype(jnp.float32) + second_ref[...].astype(jnp.float32)
    solved = solve(rhs_ref[...] - update, inverse_ref[...])
    out_ref[level, 0] = solved


def paired_shards(row_count, right_sides, factor_blocks, diag_inverses, source_ids, block_counts):
    level_count, _, rhs_count, width = right_sides.shape
    slots = factor_blocks.shape[3]
    rows = rhs_count // 2
    chips = row_count // 2
    later = level_count - 1
    same_core = [[2 * j + k for j in range(chips)] for k in range(2)]
    part = jax.ShapeDtypeStruct((rows, width), jnp.float32)
    rounded_part = jax.ShapeDtypeStruct((rows, width), jnp.bfloat16)
    square = jax.ShapeDtypeStruct((width, width), jnp.bfloat16)
    copies = jax.ShapeDtypeStruct((chips, rows, width), jnp.bfloat16)
    solve_flops = 2 * rows * width * width

    def over_both(x, move):
        pairs = []
        for j in range(chips):
            for k in range(2):
                for c in range(2):
                    tj, tk, tc = move(j, k, c)
                    pairs.append(((2 * j + k) * 2 + c, (2 * tj + tk) * 2 + tc))
        return lax.ppermute(x, ("rows", "cols"), pairs)

    def swap_core(x):
        return lax.ppermute(x, "rows", [(i, i ^ 1) for i in range(row_count)])

    def transpose(x):
        return over_both(x, lambda j, k, c: (j, c, k))

    def spread(x):
        return lax.all_to_all(x, "rows", 0, 0, axis_index_groups=same_core)

    other_inverses, other_rhs = swap_core(diag_inverses), swap_core(right_sides)
    counts = block_counts.reshape(later)
    live_ids, own_rhs, own_inverse = run(
        prepare_kernel,
        (
            (jax.ShapeDtypeStruct(source_ids.shape, source_ids.dtype), SMEM),
            (part, VMEM),
            (square, VMEM),
        ),
        ((source_ids, HBM), (counts, HBM), (right_sides, HBM), (diag_inverses, HBM)),
        scratch=(
            pltpu.SMEM(source_ids.shape, source_ids.dtype),
            pltpu.SMEM(counts.shape, counts.dtype),
            pltpu.SemaphoreType.DMA((4,)),
        ),
    )
    solved, copied = run(
        first_kernel,
        ((part, VMEM), (copies, VMEM)),
        ((own_rhs, VMEM), (other_rhs, VMEM), (own_inverse, VMEM), (other_inverses, VMEM)),
        flops=solve_flops,
    )
    finished = [transpose(solved)]
    stores = [spread(copied)]
    sent_factors, _, _ = lax.optimization_barrier((factor_blocks, other_rhs, other_inverses))
    sent_ids, solved = lax.optimization_barrier((live_ids, solved))
    other_ids = swap_core(sent_ids)
    slot_args = ((live_ids, SMEM), (other_ids, SMEM))
    staged_args = (
        (factor_blocks, HBM),
        (swap_core(sent_factors), HBM),
        (right_sides, HBM),
        (other_rhs, HBM),
        (diag_inverses, HBM),
        (other_inverses, HBM),
    )
    staged_shape = jax.ShapeDtypeStruct((2, slots, width, width), jnp.bfloat16)
    gathered = pltpu.VMEM((rows, slots * width), jnp.bfloat16)
    after = ()
    for l in range(1, level_count):
        staged, rhs, inverse, *older = run(
            functools.partial(stage_kernel, l, later, chips),
            ((staged_shape, FIXED), (part, VMEM), (square, VMEM)) + ((part, VMEM), (part, VMEM)) * (l > 1),
            slot_args + staged_args + tuple((x, VMEM) for x in stores[:l - 1]) + after,
            scratch=((pltpu.VMEM(((l - 1) * chips, rows, width), jnp.bfloat16), gathered) if l > 1 else ())
            + (
                pltpu.VMEM((2, rows, width), jnp.float32),
                pltpu.VMEM((2, width, width), jnp.bfloat16),
                pltpu.SemaphoreType.DMA((4,)),
                pltpu.SemaphoreType.DMA((2,)),
            ),
            flops=2 * slots * solve_flops * (l > 1),
            transferred=2 * slots * width * width * 2,
        )
        kept, sent = run(
            functools.partial(sums_kernel, l, chips),
            ((part if l < later else rounded_part, VMEM), (rounded_part, VMEM)),
            slot_args
            + ((stores[-1], VMEM), (staged, FIXED))
            + tuple((x, VMEM) for x in older)
            + tuple((x, ANY) for x in finished),
            scratch=(gathered,),
            flops=2 * slots * solve_flops,
            transferred=2 * slots * width * width * 2,
        )
        after = ((kept, ANY),)
        if l < later:
            arrived = lax.ppermute(sent, "cols", [(0, 1), (1, 0)])
            solved, copied = run(
                inner_kernel,
                ((part, VMEM), (copies, VMEM)),
                tuple((x, VMEM) for x in (kept, arrived, rhs, inverse)),
                flops=solve_flops,
            )
            finished.append(transpose(solved))
            stores.append(spread(copied))
    first = over_both(kept, lambda j, k, c: (j, c, k))
    second = over_both(sent, lambda j, k, c: (j, 1 - c, k))
    out, = run(
        last_kernel,
        ((jax.ShapeDtypeStruct((level_count, 1, rows, width), jnp.float32), VMEM),),
        tuple((x, VMEM) for x in (first, second, rhs, inverse, *finished)),
        flops=solve_flops,
    )
    return out


def gather_slots(ids_ref, counts_ref, group, store_ref, gathered, slots, width):
    for k in range(slots):
        piece = store_ref[ids_ref[group, k]]
        live = jnp.where(k < counts_ref[group], 1.0, 0.0).astype(piece.dtype)
        gathered[:, k * width:(k + 1) * width] = piece * live


def level_kernel(groups, ids_ref, counts_ref, store_ref, *refs):
    factor_refs = refs[:groups]
    rhs_ref, inverse_ref, out_ref, rounded_ref, gathered = refs[groups:]
    slots, width = factor_refs[0].shape[0], factor_refs[0].shape[1]
    update = None
    for g in range(groups):
        gather_slots(ids_ref, counts_ref, g, store_ref, gathered, slots, width)
        term = flat_dot(gathered, factor_refs[g])
        update = term if update is None else update + term
    reduced = (rhs_ref[...] - update).astype(jnp.bfloat16)
    solved = jnp.dot(reduced, inverse_ref[...], preferred_element_type=jnp.float32)
    out_ref[...] = solved
    rounded_ref[...] = solved.astype(jnp.bfloat16)


def solve_level(ids, counts, store, factors, rhs, inverse):
    groups = len(factors)
    rows, width = rhs.shape
    slots = factors[0].shape[0]
    vmem = pl.BlockSpec(memory_space=pltpu.VMEM)
    smem = pl.BlockSpec(memory_space=pltpu.SMEM)
    return pl.pallas_call(
        functools.partial(level_kernel, groups),
        out_shape=(
            jax.ShapeDtypeStruct((rows, width), jnp.float32),
            jax.ShapeDtypeStruct((rows, width), jnp.bfloat16),
        ),
        in_specs=[smem, smem, vmem] + [vmem] * groups + [vmem, vmem],
        out_specs=(vmem, vmem),
        scratch_shapes=[pltpu.VMEM((rows, slots * width), jnp.bfloat16)],
        compiler_params=pltpu.CompilerParams(vmem_limit_bytes=VMEM_LIMIT),
        cost_estimate=pl.CostEstimate(
            flops=2 * rows * width * width * (groups * slots + 1),
            bytes_accessed=groups * slots * width * width * 2,
            transcendentals=0,
        ),
    )(ids, counts, store, *factors, rhs, inverse)


def rotated_shards(col_count, right_sides, factor_blocks, diag_inverses, source_ids, block_counts):
    level_count, _, rhs_count, width = right_sides.shape
    share_rows = rhs_count // col_count
    col_index = lax.axis_index("cols")

    described = jnp.concatenate([source_ids[:, 0, 0], block_counts[:, 0, 0][:, None]], axis=1)
    factors = [[factor_blocks[l, 0, 0]] for l in range(level_count - 1)]
    descriptions = [described]
    for shift in range(1, col_count):
        pairs = [(i, (i + shift) % col_count) for i in range(col_count)]
        descriptions.append(lax.ppermute(described, "cols", pairs))
    for l in range(level_count - 1):
        for shift in range(1, col_count):
            pairs = [(i, (i + shift) % col_count) for i in range(col_count)]
            factors[l].append(lax.ppermute(factor_blocks[l, 0, 0], "cols", pairs))
    descriptions = jnp.stack(descriptions)

    rhs = lax.dynamic_slice_in_dim(right_sides[:, 0], col_index * share_rows, share_rows, 1)
    solutions = []
    stores = []
    for l in range(level_count):
        if l == 0:
            own = jnp.dot(
                rhs[0].astype(jnp.bfloat16), diag_inverses[0, 0], preferred_element_type=jnp.float32
            )
            rounded = own.astype(jnp.bfloat16)
        else:
            ids = descriptions[:, l - 1, :-1]
            counts = descriptions[:, l - 1, -1]
            store = stores[0] if l == 1 else jnp.concatenate(stores, axis=0)
            own, rounded = solve_level(ids, counts, store, factors[l - 1], rhs[l], diag_inverses[l, 0])
        solutions.append(own)
        if l < level_count - 1:
            stores.append(lax.all_gather(rounded, "rows", axis=0))
    return jnp.stack(solutions)[:, None]


def solution(mesh):
    row_count, col_count = mesh.shape["rows"], mesh.shape["cols"]
    chips = row_count // 2
    if col_count == 2 and row_count == 2 * chips:
        shards = functools.partial(paired_shards, row_count)
    else:
        shards = functools.partial(rotated_shards, col_count)
    return jax.shard_map(
        shards,
        mesh=mesh,
        in_specs=(
            P(None, "rows", None, None),
            P(None, "rows", "cols", None, None, None),
            P(None, "rows", None, None),
            P(None, "rows", "cols", None),
            P(None, "rows", "cols"),
        ),
        out_specs=P(None, "rows", "cols", None),
        check_vma=False,
    )
```

```python
import functools

import jax
import jax.numpy as jnp
from jax import lax
from jax.experimental import pallas as pl
from jax.experimental.pallas import tpu as pltpu
from jax.sharding import PartitionSpec as P

VMEM_LIMIT = 16 * 1024 * 1024


VMEM = pl.BlockSpec(memory_space=pltpu.VMEM)
SMEM = pl.BlockSpec(memory_space=pltpu.SMEM)
ANY = pl.BlockSpec(memory_space=pl.ANY)
HBM = pl.BlockSpec(memory_space=pltpu.HBM)
FIXED = pl.BlockSpec(memory_space=pltpu.VMEM)
PLACES = {id(HBM): pltpu.HBM, id(FIXED): pltpu.VMEM}


def flat_dot(gathered, factor_ref):
    slots, width = factor_ref.shape[0], factor_ref.shape[1]
    return jnp.dot(
        gathered[...],
        factor_ref[...].reshape(slots * width, width),
        preferred_element_type=jnp.float32,
    )


def run(kernel, outs, args, scratch=(), flops=0, transferred=0):
    out_shape = tuple(PLACES[id(spec)](x.shape, x.dtype) if id(spec) in PLACES else x for x, spec in outs)
    args = tuple(
        (pltpu.with_memory_space_constraint(x, PLACES[id(spec)]) if id(spec) in PLACES else x, spec)
        for x, spec in args
    )
    return pl.pallas_call(
        kernel,
        out_shape=out_shape,
        in_specs=[spec for _, spec in args],
        out_specs=tuple(spec for _, spec in outs),
        scratch_shapes=list(scratch),
        compiler_params=pltpu.CompilerParams(vmem_limit_bytes=VMEM_LIMIT),
        cost_estimate=pl.CostEstimate(flops=flops, bytes_accessed=transferred, transcendentals=0),
    )(*(x for x, _ in args))


def half_of(ref, level, half, rows):
    return ref.at[level, 0, pl.ds(pl.multiple_of(half * rows, rows), rows), :]


def solve(reduced, inverse):
    return jnp.dot(reduced.astype(jnp.bfloat16), inverse, preferred_element_type=jnp.float32)


def start_copies(pairs, sems):
    copies = [pltpu.make_async_copy(src, dst, sems.at[i]) for i, (src, dst) in enumerate(pairs)]
    for copy in copies:
        copy.start()
    return copies


def own_place():
    return lax.rem(lax.axis_index("rows"), 2), lax.axis_index("cols")


def prepare_kernel(
    ids_ref, counts_ref, rhs_ref, inverse_ref, live_ids_ref, own_rhs_ref, own_inverse_ref, ids, counts, sems
):
    core, _ = own_place()
    rows = own_rhs_ref.shape[0]
    copies = start_copies(
        [
            (ids_ref, ids),
            (counts_ref, counts),
            (half_of(rhs_ref, 0, core, rows), own_rhs_ref),
            (inverse_ref.at[0, 0], own_inverse_ref),
        ],
        sems,
    )
    copies[0].wait()
    copies[1].wait()
    for l in range(ids.shape[0]):
        for k in range(ids.shape[3]):
            live_ids_ref[l, 0, 0, k] = jnp.where(k < counts[l], ids[l, 0, 0, k], -1)
    copies[2].wait()
    copies[3].wait()


def both_pairs(level, rows, core, rhs_refs, inverse_refs, rhs, inverse):
    pairs = [(half_of(ref, level, core, rows), rhs.at[g]) for g, ref in enumerate(rhs_refs)]
    return pairs + [(ref.at[level, 0], inverse.at[g]) for g, ref in enumerate(inverse_refs)]


def first_kernel(rhs_ref, other_rhs_ref, inverse_ref, other_inverse_ref, *refs):
    out_ref, copies_ref = refs[-2:]
    core, col = own_place()
    straight = core == col
    other_rhs = half_of(other_rhs_ref, 0, core, out_ref.shape[0])[...]
    solved = solve(
        jnp.where(straight, rhs_ref[...], other_rhs),
        jnp.where(straight, inverse_ref[...], other_inverse_ref[0, 0]),
    )
    out_ref[...] = solved
    rounded = solved.astype(jnp.bfloat16)
    for i in range(copies_ref.shape[0]):
        copies_ref[i] = rounded


def slot_sum(level, store_level, chips, ids_ref, store_ref, factor_ref, gathered):
    slots, width = factor_ref.shape[0], factor_ref.shape[1]
    for k in range(slots):
        source_id = ids_ref[level - 1, 0, 0, k]
        source = jnp.maximum(source_id, 0)
        source_level, place = source // (2 * chips), source % (2 * chips) // 2
        live = source_id >= 0
        if store_level is None:
            live = jnp.logical_and(live, source_level < level - 1)
            place = jnp.minimum(source_level, level - 2) * chips + place
        else:
            live = jnp.logical_and(live, source_level == store_level)
        piece = store_ref[place]
        gathered[:, k * width:(k + 1) * width] = piece * jnp.where(live, 1.0, 0.0).astype(piece.dtype)
    return flat_dot(gathered, factor_ref)


def stage_kernel(level, later, chips, *refs):
    inner = level < later
    slot_refs = refs[:2]
    factor_ref, other_factor_ref, rhs_ref, other_rhs_ref, inverse_ref, other_inverse_ref = refs[2:8]
    store_refs = refs[8:7 + level]
    outs = refs[-7 if level == 1 else -11:]
    staged_ref, own_rhs_ref, own_inverse_ref = outs[:3]
    rhs, inverse, sems, factor_sems = outs[-4:]
    core, col = own_place()
    straight = core == col
    rows = own_rhs_ref.shape[0]
    if inner:
        pairs = both_pairs(
            level, rows, core, (rhs_ref, other_rhs_ref), (inverse_ref, other_inverse_ref), rhs, inverse
        )
    else:
        pairs = [
            (half_of(rhs_ref, level, col, rows), own_rhs_ref),
            (inverse_ref.at[level, 0], own_inverse_ref),
        ]
    factor_copies = start_copies(
        [
            (factor_ref.at[level - 1, 0, 0], staged_ref.at[0]),
            (other_factor_ref.at[level - 1, 0, 0], staged_ref.at[1]),
        ],
        factor_sems,
    )
    copies = start_copies(pairs, sems)
    if level > 1:
        older_refs, store, gathered = outs[3:5], outs[5], outs[6]
        for m, piece in enumerate(store_refs):
            store[m * chips:(m + 1) * chips] = piece[...]
    for g in range(2):
        factor_copies[g].wait()
        if level > 1:
            older_refs[g][...] = slot_sum(
                level, None, chips, slot_refs[g], store, staged_ref.at[g], gathered
            )
    for copy in copies:
        copy.wait()
    if inner:
        own_rhs_ref[...] = jnp.where(straight, rhs[0], rhs[1])
        own_inverse_ref[...] = jnp.where(straight, inverse[0], inverse[1])


def sums_kernel(level, chips, *refs):
    slot_refs, store_ref, staged_ref = refs[:2], refs[2], refs[3]
    older_refs = refs[4:6]
    kept_ref, sent_ref, gathered = refs[-3:]
    core, col = own_place()
    sums = []
    for g in range(2):
        total = slot_sum(level, level - 1, chips, slot_refs[g], store_ref, staged_ref.at[g], gathered)
        sums.append(total + older_refs[g][...] if level > 1 else total)
    straight = core == col
    kept_ref[...] = jnp.where(straight, sums[0], sums[1]).astype(kept_ref.dtype)
    sent_ref[...] = jnp.where(straight, sums[1], sums[0]).astype(sent_ref.dtype)


def inner_kernel(kept_ref, arrived_ref, rhs_ref, inverse_ref, out_ref, copies_ref):
    update = kept_ref[...] + arrived_ref[...].astype(jnp.float32)
    solved = solve(rhs_ref[...] - update, inverse_ref[...])
    out_ref[...] = solved
    rounded = solved.astype(jnp.bfloat16)
    for i in range(copies_ref.shape[0]):
        copies_ref[i] = rounded


def last_kernel(first_ref, second_ref, rhs_ref, inverse_ref, *refs):
    done_refs, out_ref = refs[:-1], refs[-1]
    level = len(done_refs)
    for m, done in enumerate(done_refs):
        out_ref[m, 0] = done[...]
    update = first_ref[...].astype(jnp.float32) + second_ref[...].astype(jnp.float32)
    solved = solve(rhs_ref[...] - update, inverse_ref[...])
    out_ref[level, 0] = solved


def paired_shards(row_count, right_sides, factor_blocks, diag_inverses, source_ids, block_counts):
    level_count, _, rhs_count, width = right_sides.shape
    slots = factor_blocks.shape[3]
    rows = rhs_count // 2
    chips = row_count // 2
    later = level_count - 1
    same_core = [[2 * j + k for j in range(chips)] for k in range(2)]
    part = jax.ShapeDtypeStruct((rows, width), jnp.float32)
    rounded_part = jax.ShapeDtypeStruct((rows, width), jnp.bfloat16)
    square = jax.ShapeDtypeStruct((width, width), jnp.bfloat16)
    copies = jax.ShapeDtypeStruct((chips, rows, width), jnp.bfloat16)
    solve_flops = 2 * rows * width * width

    def over_both(x, move):
        pairs = []
        for j in range(chips):
            for k in range(2):
                for c in range(2):
                    tj, tk, tc = move(j, k, c)
                    pairs.append(((2 * j + k) * 2 + c, (2 * tj + tk) * 2 + tc))
        return lax.ppermute(x, ("rows", "cols"), pairs)

    def swap_core(x):
        return lax.ppermute(x, "rows", [(i, i ^ 1) for i in range(row_count)])

    def transpose(x):
        return over_both(x, lambda j, k, c: (j, c, k))

    def spread(x):
        return lax.all_to_all(x, "rows", 0, 0, axis_index_groups=same_core)

    other_inverses, other_rhs = swap_core(diag_inverses), swap_core(right_sides)
    counts = block_counts.reshape(later)
    live_ids, own_rhs, own_inverse = run(
        prepare_kernel,
        (
            (jax.ShapeDtypeStruct(source_ids.shape, source_ids.dtype), SMEM),
            (part, VMEM),
            (square, VMEM),
        ),
        ((source_ids, HBM), (counts, HBM), (right_sides, HBM), (diag_inverses, HBM)),
        scratch=(
            pltpu.SMEM(source_ids.shape, source_ids.dtype),
            pltpu.SMEM(counts.shape, counts.dtype),
            pltpu.SemaphoreType.DMA((4,)),
        ),
    )
    solved, copied = run(
        first_kernel,
        ((part, VMEM), (copies, VMEM)),
        ((own_rhs, VMEM), (other_rhs, VMEM), (own_inverse, VMEM), (other_inverses, VMEM)),
        flops=solve_flops,
    )
    finished = [transpose(solved)]
    stores = [spread(copied)]
    sent_factors, _, _, _ = lax.optimization_barrier((factor_blocks, other_rhs, other_inverses, live_ids))
    sent_ids, solved = lax.optimization_barrier((live_ids, solved))
    other_ids = swap_core(sent_ids)
    slot_args = ((live_ids, SMEM), (other_ids, SMEM))
    staged_args = (
        (factor_blocks, HBM),
        (swap_core(sent_factors), HBM),
        (right_sides, HBM),
        (other_rhs, HBM),
        (diag_inverses, HBM),
        (other_inverses, HBM),
    )
    staged_shape = jax.ShapeDtypeStruct((2, slots, width, width), jnp.bfloat16)
    gathered = pltpu.VMEM((rows, slots * width), jnp.bfloat16)
    after = ()
    for l in range(1, level_count):
        staged, rhs, inverse, *older = run(
            functools.partial(stage_kernel, l, later, chips),
            ((staged_shape, FIXED), (part, VMEM), (square, VMEM)) + ((part, VMEM), (part, VMEM)) * (l > 1),
            slot_args + staged_args + tuple((x, VMEM) for x in stores[:l - 1]) + after,
            scratch=((pltpu.VMEM(((l - 1) * chips, rows, width), jnp.bfloat16), gathered) if l > 1 else ())
            + (
                pltpu.VMEM((2, rows, width), jnp.float32),
                pltpu.VMEM((2, width, width), jnp.bfloat16),
                pltpu.SemaphoreType.DMA((4,)),
                pltpu.SemaphoreType.DMA((2,)),
            ),
            flops=2 * slots * solve_flops * (l > 1),
            transferred=2 * slots * width * width * 2,
        )
        kept, sent = run(
            functools.partial(sums_kernel, l, chips),
            ((part if l < later else rounded_part, VMEM), (rounded_part, VMEM)),
            slot_args
            + ((stores[-1], VMEM), (staged, FIXED))
            + tuple((x, VMEM) for x in older)
            + tuple((x, ANY) for x in finished),
            scratch=(gathered,),
            flops=2 * slots * solve_flops,
            transferred=2 * slots * width * width * 2,
        )
        after = ((kept, ANY),)
        if l < later:
            arrived = lax.ppermute(sent, "cols", [(0, 1), (1, 0)])
            solved, copied = run(
                inner_kernel,
                ((part, VMEM), (copies, VMEM)),
                tuple((x, VMEM) for x in (kept, arrived, rhs, inverse)),
                flops=solve_flops,
            )
            finished.append(transpose(solved))
            stores.append(spread(copied))
    first = over_both(kept, lambda j, k, c: (j, c, k))
    second = over_both(sent, lambda j, k, c: (j, 1 - c, k))
    out, = run(
        last_kernel,
        ((jax.ShapeDtypeStruct((level_count, 1, rows, width), jnp.float32), VMEM),),
        tuple((x, VMEM) for x in (first, second, rhs, inverse, *finished)),
        flops=solve_flops,
    )
    return out


def gather_slots(ids_ref, counts_ref, group, store_ref, gathered, slots, width):
    for k in range(slots):
        piece = store_ref[ids_ref[group, k]]
        live = jnp.where(k < counts_ref[group], 1.0, 0.0).astype(piece.dtype)
        gathered[:, k * width:(k + 1) * width] = piece * live


def level_kernel(groups, ids_ref, counts_ref, store_ref, *refs):
    factor_refs = refs[:groups]
    rhs_ref, inverse_ref, out_ref, rounded_ref, gathered = refs[groups:]
    slots, width = factor_refs[0].shape[0], factor_refs[0].shape[1]
    update = None
    for g in range(groups):
        gather_slots(ids_ref, counts_ref, g, store_ref, gathered, slots, width)
        term = flat_dot(gathered, factor_refs[g])
        update = term if update is None else update + term
    reduced = (rhs_ref[...] - update).astype(jnp.bfloat16)
    solved = jnp.dot(reduced, inverse_ref[...], preferred_element_type=jnp.float32)
    out_ref[...] = solved
    rounded_ref[...] = solved.astype(jnp.bfloat16)


def solve_level(ids, counts, store, factors, rhs, inverse):
    groups = len(factors)
    rows, width = rhs.shape
    slots = factors[0].shape[0]
    vmem = pl.BlockSpec(memory_space=pltpu.VMEM)
    smem = pl.BlockSpec(memory_space=pltpu.SMEM)
    return pl.pallas_call(
        functools.partial(level_kernel, groups),
        out_shape=(
            jax.ShapeDtypeStruct((rows, width), jnp.float32),
            jax.ShapeDtypeStruct((rows, width), jnp.bfloat16),
        ),
        in_specs=[smem, smem, vmem] + [vmem] * groups + [vmem, vmem],
        out_specs=(vmem, vmem),
        scratch_shapes=[pltpu.VMEM((rows, slots * width), jnp.bfloat16)],
        compiler_params=pltpu.CompilerParams(vmem_limit_bytes=VMEM_LIMIT),
        cost_estimate=pl.CostEstimate(
            flops=2 * rows * width * width * (groups * slots + 1),
            bytes_accessed=groups * slots * width * width * 2,
            transcendentals=0,
        ),
    )(ids, counts, store, *factors, rhs, inverse)


def rotated_shards(col_count, right_sides, factor_blocks, diag_inverses, source_ids, block_counts):
    level_count, _, rhs_count, width = right_sides.shape
    share_rows = rhs_count // col_count
    col_index = lax.axis_index("cols")

    described = jnp.concatenate([source_ids[:, 0, 0], block_counts[:, 0, 0][:, None]], axis=1)
    factors = [[factor_blocks[l, 0, 0]] for l in range(level_count - 1)]
    descriptions = [described]
    for shift in range(1, col_count):
        pairs = [(i, (i + shift) % col_count) for i in range(col_count)]
        descriptions.append(lax.ppermute(described, "cols", pairs))
    for l in range(level_count - 1):
        for shift in range(1, col_count):
            pairs = [(i, (i + shift) % col_count) for i in range(col_count)]
            factors[l].append(lax.ppermute(factor_blocks[l, 0, 0], "cols", pairs))
    descriptions = jnp.stack(descriptions)

    rhs = lax.dynamic_slice_in_dim(right_sides[:, 0], col_index * share_rows, share_rows, 1)
    solutions = []
    stores = []
    for l in range(level_count):
        if l == 0:
            own = jnp.dot(
                rhs[0].astype(jnp.bfloat16), diag_inverses[0, 0], preferred_element_type=jnp.float32
            )
            rounded = own.astype(jnp.bfloat16)
        else:
            ids = descriptions[:, l - 1, :-1]
            counts = descriptions[:, l - 1, -1]
            store = stores[0] if l == 1 else jnp.concatenate(stores, axis=0)
            own, rounded = solve_level(ids, counts, store, factors[l - 1], rhs[l], diag_inverses[l, 0])
        solutions.append(own)
        if l < level_count - 1:
            stores.append(lax.all_gather(rounded, "rows", axis=0))
    return jnp.stack(solutions)[:, None]


def solution(mesh):
    row_count, col_count = mesh.shape["rows"], mesh.shape["cols"]
    chips = row_count // 2
    if col_count == 2 and row_count == 2 * chips:
        shards = functools.partial(paired_shards, row_count)
    else:
        shards = functools.partial(rotated_shards, col_count)
    return jax.shard_map(
        shards,
        mesh=mesh,
        in_specs=(
            P(None, "rows", None, None),
            P(None, "rows", "cols", None, None, None),
            P(None, "rows", None, None),
            P(None, "rows", "cols", None),
            P(None, "rows", "cols"),
        ),
        out_specs=P(None, "rows", "cols", None),
        check_vma=False,
    )
```

```python
import functools

import jax
import jax.numpy as jnp
from jax import lax
from jax.experimental import pallas as pl
from jax.experimental.pallas import tpu as pltpu
from jax.sharding import PartitionSpec as P

VMEM_LIMIT = 16 * 1024 * 1024


VMEM = pl.BlockSpec(memory_space=pltpu.VMEM)
SMEM = pl.BlockSpec(memory_space=pltpu.SMEM)
ANY = pl.BlockSpec(memory_space=pl.ANY)
HBM = pl.BlockSpec(memory_space=pltpu.HBM)
FIXED = pl.BlockSpec(memory_space=pltpu.VMEM)
PLACES = {id(HBM): pltpu.HBM, id(FIXED): pltpu.VMEM}


def flat_dot(gathered, factor_ref):
    slots, width = factor_ref.shape[0], factor_ref.shape[1]
    return jnp.dot(
        gathered[...],
        factor_ref[...].reshape(slots * width, width),
        preferred_element_type=jnp.float32,
    )


def run(kernel, outs, args, scratch=(), flops=0, transferred=0):
    out_shape = tuple(PLACES[id(spec)](x.shape, x.dtype) if id(spec) in PLACES else x for x, spec in outs)
    args = tuple(
        (pltpu.with_memory_space_constraint(x, PLACES[id(spec)]) if id(spec) in PLACES else x, spec)
        for x, spec in args
    )
    return pl.pallas_call(
        kernel,
        out_shape=out_shape,
        in_specs=[spec for _, spec in args],
        out_specs=tuple(spec for _, spec in outs),
        scratch_shapes=list(scratch),
        compiler_params=pltpu.CompilerParams(vmem_limit_bytes=VMEM_LIMIT),
        cost_estimate=pl.CostEstimate(flops=flops, bytes_accessed=transferred, transcendentals=0),
    )(*(x for x, _ in args))


def half_of(ref, level, half, rows):
    return ref.at[level, 0, pl.ds(pl.multiple_of(half * rows, rows), rows), :]


def solve(reduced, inverse):
    return jnp.dot(reduced.astype(jnp.bfloat16), inverse, preferred_element_type=jnp.float32)


def start_copies(pairs, sems):
    copies = [pltpu.make_async_copy(src, dst, sems.at[i]) for i, (src, dst) in enumerate(pairs)]
    for copy in copies:
        copy.start()
    return copies


def own_place():
    return lax.rem(lax.axis_index("rows"), 2), lax.axis_index("cols")


def prepare_kernel(
    ids_ref, counts_ref, rhs_ref, inverse_ref, live_ids_ref, own_rhs_ref, own_inverse_ref, ids, counts, sems
):
    core, _ = own_place()
    rows = own_rhs_ref.shape[0]
    copies = start_copies(
        [
            (ids_ref, ids),
            (counts_ref, counts),
            (half_of(rhs_ref, 0, core, rows), own_rhs_ref),
            (inverse_ref.at[0, 0], own_inverse_ref),
        ],
        sems,
    )
    copies[0].wait()
    copies[1].wait()
    for l in range(ids.shape[0]):
        for k in range(ids.shape[3]):
            live_ids_ref[l, 0, 0, k] = jnp.where(k < counts[l], ids[l, 0, 0, k], -1)
    copies[2].wait()
    copies[3].wait()


def both_pairs(level, rows, core, rhs_refs, inverse_refs, rhs, inverse):
    pairs = [(half_of(ref, level, core, rows), rhs.at[g]) for g, ref in enumerate(rhs_refs)]
    return pairs + [(ref.at[level, 0], inverse.at[g]) for g, ref in enumerate(inverse_refs)]


def first_kernel(rhs_ref, other_rhs_ref, inverse_ref, other_inverse_ref, *refs):
    out_ref, copies_ref = refs[-2:]
    core, col = own_place()
    straight = core == col
    other_rhs = half_of(other_rhs_ref, 0, core, out_ref.shape[0])[...]
    solved = solve(
        jnp.where(straight, rhs_ref[...], other_rhs),
        jnp.where(straight, inverse_ref[...], other_inverse_ref[0, 0]),
    )
    out_ref[...] = solved
    rounded = solved.astype(jnp.bfloat16)
    for i in range(copies_ref.shape[0]):
        copies_ref[i] = rounded


def slot_sum(level, store_level, chips, ids_ref, store_ref, factor_ref, gathered):
    slots, width = factor_ref.shape[0], factor_ref.shape[1]
    for k in range(slots):
        source_id = ids_ref[level - 1, 0, 0, k]
        source = jnp.maximum(source_id, 0)
        source_level, place = source // (2 * chips), source % (2 * chips) // 2
        live = source_id >= 0
        if store_level is None:
            live = jnp.logical_and(live, source_level < level - 1)
            place = jnp.minimum(source_level, level - 2) * chips + place
        else:
            live = jnp.logical_and(live, source_level == store_level)
        piece = store_ref[place]
        gathered[:, k * width:(k + 1) * width] = piece * jnp.where(live, 1.0, 0.0).astype(piece.dtype)
    return flat_dot(gathered, factor_ref)


def stage_kernel(level, later, chips, *refs):
    inner = level < later
    slot_refs = refs[:2]
    factor_ref, other_factor_ref, rhs_ref, other_rhs_ref, inverse_ref, other_inverse_ref = refs[2:8]
    store_refs = refs[8:7 + level]
    outs = refs[-7 if level == 1 else -11:]
    staged_ref, own_rhs_ref, own_inverse_ref = outs[:3]
    rhs, inverse, sems, factor_sems = outs[-4:]
    core, col = own_place()
    straight = core == col
    rows = own_rhs_ref.shape[0]
    if inner:
        pairs = both_pairs(
            level, rows, core, (rhs_ref, other_rhs_ref), (inverse_ref, other_inverse_ref), rhs, inverse
        )
    else:
        pairs = [
            (half_of(rhs_ref, level, col, rows), own_rhs_ref),
            (inverse_ref.at[level, 0], own_inverse_ref),
        ]
    factor_copies = start_copies(
        [
            (factor_ref.at[level - 1, 0, 0], staged_ref.at[0]),
            (other_factor_ref.at[level - 1, 0, 0], staged_ref.at[1]),
        ],
        factor_sems,
    )
    copies = start_copies(pairs, sems)
    if level > 1:
        older_refs, store, gathered = outs[3:5], outs[5], outs[6]
        for m, piece in enumerate(store_refs):
            store[m * chips:(m + 1) * chips] = piece[...]
    for g in range(2):
        factor_copies[g].wait()
        if level > 1:
            older_refs[g][...] = slot_sum(
                level, None, chips, slot_refs[g], store, staged_ref.at[g], gathered
            )
    for copy in copies:
        copy.wait()
    if inner:
        own_rhs_ref[...] = jnp.where(straight, rhs[0], rhs[1])
        own_inverse_ref[...] = jnp.where(straight, inverse[0], inverse[1])


def sums_kernel(level, chips, *refs):
    slot_refs, store_ref, staged_ref = refs[:2], refs[2], refs[3]
    older_refs = refs[4:6]
    kept_ref, sent_ref, gathered = refs[-3:]
    core, col = own_place()
    sums = []
    for g in range(2):
        total = slot_sum(level, level - 1, chips, slot_refs[g], store_ref, staged_ref.at[g], gathered)
        sums.append(total + older_refs[g][...] if level > 1 else total)
    straight = core == col
    kept_ref[...] = jnp.where(straight, sums[0], sums[1]).astype(kept_ref.dtype)
    sent_ref[...] = jnp.where(straight, sums[1], sums[0]).astype(sent_ref.dtype)


def inner_kernel(kept_ref, arrived_ref, rhs_ref, inverse_ref, out_ref, copies_ref):
    solved = solve(rhs_ref[...] - (kept_ref[...] + arrived_ref[...]), inverse_ref[...])
    out_ref[...] = solved
    rounded = solved.astype(jnp.bfloat16)
    for i in range(copies_ref.shape[0]):
        copies_ref[i] = rounded


def last_kernel(first_ref, second_ref, rhs_ref, inverse_ref, *refs):
    done_refs, out_ref = refs[:-1], refs[-1]
    level = len(done_refs)
    for m, done in enumerate(done_refs):
        out_ref[m, 0] = done[...]
    update = first_ref[...].astype(jnp.float32) + second_ref[...].astype(jnp.float32)
    solved = solve(rhs_ref[...] - update, inverse_ref[...])
    out_ref[level, 0] = solved


def paired_shards(row_count, right_sides, factor_blocks, diag_inverses, source_ids, block_counts):
    level_count, _, rhs_count, width = right_sides.shape
    slots = factor_blocks.shape[3]
    rows = rhs_count // 2
    chips = row_count // 2
    later = level_count - 1
    same_core = [[2 * j + k for j in range(chips)] for k in range(2)]
    part = jax.ShapeDtypeStruct((rows, width), jnp.float32)
    rounded_part = jax.ShapeDtypeStruct((rows, width), jnp.bfloat16)
    square = jax.ShapeDtypeStruct((width, width), jnp.bfloat16)
    copies = jax.ShapeDtypeStruct((chips, rows, width), jnp.bfloat16)
    solve_flops = 2 * rows * width * width

    def over_both(x, move):
        pairs = []
        for j in range(chips):
            for k in range(2):
                for c in range(2):
                    tj, tk, tc = move(j, k, c)
                    pairs.append(((2 * j + k) * 2 + c, (2 * tj + tk) * 2 + tc))
        return lax.ppermute(x, ("rows", "cols"), pairs)

    def swap_core(x):
        return lax.ppermute(x, "rows", [(i, i ^ 1) for i in range(row_count)])

    def transpose(x):
        return over_both(x, lambda j, k, c: (j, c, k))

    def spread(x):
        return lax.all_to_all(x, "rows", 0, 0, axis_index_groups=same_core)

    other_inverses, other_rhs = swap_core(diag_inverses), swap_core(right_sides)
    counts = block_counts.reshape(later)
    live_ids, own_rhs, own_inverse = run(
        prepare_kernel,
        (
            (jax.ShapeDtypeStruct(source_ids.shape, source_ids.dtype), SMEM),
            (part, VMEM),
            (square, VMEM),
        ),
        ((source_ids, HBM), (counts, HBM), (right_sides, HBM), (diag_inverses, HBM)),
        scratch=(
            pltpu.SMEM(source_ids.shape, source_ids.dtype),
            pltpu.SMEM(counts.shape, counts.dtype),
            pltpu.SemaphoreType.DMA((4,)),
        ),
    )
    solved, copied = run(
        first_kernel,
        ((part, VMEM), (copies, VMEM)),
        ((own_rhs, VMEM), (other_rhs, VMEM), (own_inverse, VMEM), (other_inverses, VMEM)),
        flops=solve_flops,
    )
    finished = [transpose(solved)]
    stores = [spread(copied)]
    sent_factors, _, _, _ = lax.optimization_barrier((factor_blocks, other_rhs, other_inverses, live_ids))
    sent_ids, solved = lax.optimization_barrier((live_ids, solved))
    other_ids = swap_core(sent_ids)
    slot_args = ((live_ids, SMEM), (other_ids, SMEM))
    staged_args = (
        (factor_blocks, HBM),
        (swap_core(sent_factors), HBM),
        (right_sides, HBM),
        (other_rhs, HBM),
        (diag_inverses, HBM),
        (other_inverses, HBM),
    )
    staged_shape = jax.ShapeDtypeStruct((2, slots, width, width), jnp.bfloat16)
    gathered = pltpu.VMEM((rows, slots * width), jnp.bfloat16)
    after = ()
    for l in range(1, level_count):
        staged, rhs, inverse, *older = run(
            functools.partial(stage_kernel, l, later, chips),
            ((staged_shape, FIXED), (part, VMEM), (square, VMEM)) + ((part, VMEM), (part, VMEM)) * (l > 1),
            slot_args + staged_args + tuple((x, VMEM) for x in stores[:l - 1]) + after,
            scratch=((pltpu.VMEM(((l - 1) * chips, rows, width), jnp.bfloat16), gathered) if l > 1 else ())
            + (
                pltpu.VMEM((2, rows, width), jnp.float32),
                pltpu.VMEM((2, width, width), jnp.bfloat16),
                pltpu.SemaphoreType.DMA((4,)),
                pltpu.SemaphoreType.DMA((2,)),
            ),
            flops=2 * slots * solve_flops * (l > 1),
            transferred=2 * slots * width * width * 2,
        )
        kept, sent = run(
            functools.partial(sums_kernel, l, chips),
            ((part if l < later else rounded_part, VMEM),) * 2,
            slot_args
            + ((stores[-1], VMEM), (staged, FIXED))
            + tuple((x, VMEM) for x in older)
            + tuple((x, ANY) for x in finished),
            scratch=(gathered,),
            flops=2 * slots * solve_flops,
            transferred=2 * slots * width * width * 2,
        )
        after = ((kept, ANY),)
        if l < later:
            arrived = lax.ppermute(sent, "cols", [(0, 1), (1, 0)])
            solved, copied = run(
                inner_kernel,
                ((part, VMEM), (copies, VMEM)),
                tuple((x, VMEM) for x in (kept, arrived, rhs, inverse)),
                flops=solve_flops,
            )
            finished.append(transpose(solved))
            stores.append(spread(copied))
    first = over_both(kept, lambda j, k, c: (j, c, k))
    second = over_both(sent, lambda j, k, c: (j, 1 - c, k))
    out, = run(
        last_kernel,
        ((jax.ShapeDtypeStruct((level_count, 1, rows, width), jnp.float32), VMEM),),
        tuple((x, VMEM) for x in (first, second, rhs, inverse, *finished)),
        flops=solve_flops,
    )
    return out


def gather_slots(ids_ref, counts_ref, group, store_ref, gathered, slots, width):
    for k in range(slots):
        piece = store_ref[ids_ref[group, k]]
        live = jnp.where(k < counts_ref[group], 1.0, 0.0).astype(piece.dtype)
        gathered[:, k * width:(k + 1) * width] = piece * live


def level_kernel(groups, ids_ref, counts_ref, store_ref, *refs):
    factor_refs = refs[:groups]
    rhs_ref, inverse_ref, out_ref, rounded_ref, gathered = refs[groups:]
    slots, width = factor_refs[0].shape[0], factor_refs[0].shape[1]
    update = None
    for g in range(groups):
        gather_slots(ids_ref, counts_ref, g, store_ref, gathered, slots, width)
        term = flat_dot(gathered, factor_refs[g])
        update = term if update is None else update + term
    reduced = (rhs_ref[...] - update).astype(jnp.bfloat16)
    solved = jnp.dot(reduced, inverse_ref[...], preferred_element_type=jnp.float32)
    out_ref[...] = solved
    rounded_ref[...] = solved.astype(jnp.bfloat16)


def solve_level(ids, counts, store, factors, rhs, inverse):
    groups = len(factors)
    rows, width = rhs.shape
    slots = factors[0].shape[0]
    vmem = pl.BlockSpec(memory_space=pltpu.VMEM)
    smem = pl.BlockSpec(memory_space=pltpu.SMEM)
    return pl.pallas_call(
        functools.partial(level_kernel, groups),
        out_shape=(
            jax.ShapeDtypeStruct((rows, width), jnp.float32),
            jax.ShapeDtypeStruct((rows, width), jnp.bfloat16),
        ),
        in_specs=[smem, smem, vmem] + [vmem] * groups + [vmem, vmem],
        out_specs=(vmem, vmem),
        scratch_shapes=[pltpu.VMEM((rows, slots * width), jnp.bfloat16)],
        compiler_params=pltpu.CompilerParams(vmem_limit_bytes=VMEM_LIMIT),
        cost_estimate=pl.CostEstimate(
            flops=2 * rows * width * width * (groups * slots + 1),
            bytes_accessed=groups * slots * width * width * 2,
            transcendentals=0,
        ),
    )(ids, counts, store, *factors, rhs, inverse)


def rotated_shards(col_count, right_sides, factor_blocks, diag_inverses, source_ids, block_counts):
    level_count, _, rhs_count, width = right_sides.shape
    share_rows = rhs_count // col_count
    col_index = lax.axis_index("cols")

    described = jnp.concatenate([source_ids[:, 0, 0], block_counts[:, 0, 0][:, None]], axis=1)
    factors = [[factor_blocks[l, 0, 0]] for l in range(level_count - 1)]
    descriptions = [described]
    for shift in range(1, col_count):
        pairs = [(i, (i + shift) % col_count) for i in range(col_count)]
        descriptions.append(lax.ppermute(described, "cols", pairs))
    for l in range(level_count - 1):
        for shift in range(1, col_count):
            pairs = [(i, (i + shift) % col_count) for i in range(col_count)]
            factors[l].append(lax.ppermute(factor_blocks[l, 0, 0], "cols", pairs))
    descriptions = jnp.stack(descriptions)

    rhs = lax.dynamic_slice_in_dim(right_sides[:, 0], col_index * share_rows, share_rows, 1)
    solutions = []
    stores = []
    for l in range(level_count):
        if l == 0:
            own = jnp.dot(
                rhs[0].astype(jnp.bfloat16), diag_inverses[0, 0], preferred_element_type=jnp.float32
            )
            rounded = own.astype(jnp.bfloat16)
        else:
            ids = descriptions[:, l - 1, :-1]
            counts = descriptions[:, l - 1, -1]
            store = stores[0] if l == 1 else jnp.concatenate(stores, axis=0)
            own, rounded = solve_level(ids, counts, store, factors[l - 1], rhs[l], diag_inverses[l, 0])
        solutions.append(own)
        if l < level_count - 1:
            stores.append(lax.all_gather(rounded, "rows", axis=0))
    return jnp.stack(solutions)[:, None]


def solution(mesh):
    row_count, col_count = mesh.shape["rows"], mesh.shape["cols"]
    chips = row_count // 2
    if col_count == 2 and row_count == 2 * chips:
        shards = functools.partial(paired_shards, row_count)
    else:
        shards = functools.partial(rotated_shards, col_count)
    return jax.shard_map(
        shards,
        mesh=mesh,
        in_specs=(
            P(None, "rows", None, None),
            P(None, "rows", "cols", None, None, None),
            P(None, "rows", None, None),
            P(None, "rows", "cols", None),
            P(None, "rows", "cols"),
        ),
        out_specs=P(None, "rows", "cols", None),
        check_vma=False,
    )
```

```python
import functools

import jax
import jax.numpy as jnp
from jax import lax
from jax.experimental import pallas as pl
from jax.experimental.pallas import tpu as pltpu
from jax.sharding import PartitionSpec as P

VMEM_LIMIT = 16 * 1024 * 1024


VMEM = pl.BlockSpec(memory_space=pltpu.VMEM)
SMEM = pl.BlockSpec(memory_space=pltpu.SMEM)
ANY = pl.BlockSpec(memory_space=pl.ANY)
HBM = pl.BlockSpec(memory_space=pltpu.HBM)
FIXED = pl.BlockSpec(memory_space=pltpu.VMEM)
PLACES = {id(HBM): pltpu.HBM, id(FIXED): pltpu.VMEM}


def flat_dot(gathered, factor_ref):
    slots, width = factor_ref.shape[0], factor_ref.shape[1]
    return jnp.dot(
        gathered[...],
        factor_ref[...].reshape(slots * width, width),
        preferred_element_type=jnp.float32,
    )


def run(kernel, outs, args, scratch=(), flops=0, transferred=0):
    out_shape = tuple(PLACES[id(spec)](x.shape, x.dtype) if id(spec) in PLACES else x for x, spec in outs)
    args = tuple(
        (pltpu.with_memory_space_constraint(x, PLACES[id(spec)]) if id(spec) in PLACES else x, spec)
        for x, spec in args
    )
    return pl.pallas_call(
        kernel,
        out_shape=out_shape,
        in_specs=[spec for _, spec in args],
        out_specs=tuple(spec for _, spec in outs),
        scratch_shapes=list(scratch),
        compiler_params=pltpu.CompilerParams(vmem_limit_bytes=VMEM_LIMIT),
        cost_estimate=pl.CostEstimate(flops=flops, bytes_accessed=transferred, transcendentals=0),
    )(*(x for x, _ in args))


def half_of(ref, level, half, rows):
    return ref.at[level, 0, pl.ds(pl.multiple_of(half * rows, rows), rows), :]


def solve(reduced, inverse):
    return jnp.dot(reduced.astype(jnp.bfloat16), inverse, preferred_element_type=jnp.float32)


def start_copies(pairs, sems):
    copies = [pltpu.make_async_copy(src, dst, sems.at[i]) for i, (src, dst) in enumerate(pairs)]
    for copy in copies:
        copy.start()
    return copies


def own_place():
    return lax.rem(lax.axis_index("rows"), 2), lax.axis_index("cols")


def prepare_kernel(
    ids_ref, counts_ref, rhs_ref, inverse_ref, live_ids_ref, own_rhs_ref, own_inverse_ref, ids, counts, sems
):
    core, _ = own_place()
    rows = own_rhs_ref.shape[0]
    copies = start_copies(
        [
            (ids_ref, ids),
            (counts_ref, counts),
            (half_of(rhs_ref, 0, core, rows), own_rhs_ref),
            (inverse_ref.at[0, 0], own_inverse_ref),
        ],
        sems,
    )
    copies[0].wait()
    copies[1].wait()
    for l in range(ids.shape[0]):
        for k in range(ids.shape[3]):
            live_ids_ref[l, 0, 0, k] = jnp.where(k < counts[l], ids[l, 0, 0, k], -1)
    copies[2].wait()
    copies[3].wait()


def both_pairs(level, rows, core, rhs_refs, inverse_refs, rhs, inverse):
    pairs = [(half_of(ref, level, core, rows), rhs.at[g]) for g, ref in enumerate(rhs_refs)]
    return pairs + [(ref.at[level, 0], inverse.at[g]) for g, ref in enumerate(inverse_refs)]


def first_kernel(rhs_ref, other_rhs_ref, inverse_ref, other_inverse_ref, *refs):
    out_ref, copies_ref = refs[-2:]
    core, col = own_place()
    straight = core == col
    other_rhs = half_of(other_rhs_ref, 0, core, out_ref.shape[0])[...]
    solved = solve(
        jnp.where(straight, rhs_ref[...], other_rhs),
        jnp.where(straight, inverse_ref[...], other_inverse_ref[0, 0]),
    )
    out_ref[...] = solved
    rounded = solved.astype(jnp.bfloat16)
    for i in range(copies_ref.shape[0]):
        copies_ref[i] = rounded


def slot_sum(level, store_level, chips, ids_ref, store_ref, factor_ref, gathered):
    slots, width = factor_ref.shape[0], factor_ref.shape[1]
    for k in range(slots):
        source_id = ids_ref[level - 1, 0, 0, k]
        source = jnp.maximum(source_id, 0)
        source_level, place = source // (2 * chips), source % (2 * chips) // 2
        live = source_id >= 0
        if store_level is None:
            live = jnp.logical_and(live, source_level < level - 1)
            place = jnp.minimum(source_level, level - 2) * chips + place
        else:
            live = jnp.logical_and(live, source_level == store_level)
        piece = store_ref[place]
        gathered[:, k * width:(k + 1) * width] = piece * jnp.where(live, 1.0, 0.0).astype(piece.dtype)
    return flat_dot(gathered, factor_ref)


def stage_kernel(level, later, chips, *refs):
    inner = level < later
    slot_refs = refs[:2]
    factor_ref, other_factor_ref, rhs_ref, other_rhs_ref, inverse_ref, other_inverse_ref = refs[2:8]
    store_refs = refs[8:7 + level]
    outs = refs[-7 if level == 1 else -11:]
    staged_ref, own_rhs_ref, own_inverse_ref = outs[:3]
    rhs, inverse, sems, factor_sems = outs[-4:]
    core, col = own_place()
    straight = core == col
    rows = own_rhs_ref.shape[0]
    if inner:
        pairs = both_pairs(
            level, rows, core, (rhs_ref, other_rhs_ref), (inverse_ref, other_inverse_ref), rhs, inverse
        )
    else:
        pairs = [
            (half_of(rhs_ref, level, col, rows), own_rhs_ref),
            (inverse_ref.at[level, 0], own_inverse_ref),
        ]
    factor_copies = start_copies(
        [
            (factor_ref.at[level - 1, 0, 0], staged_ref.at[0]),
            (other_factor_ref.at[level - 1, 0, 0], staged_ref.at[1]),
        ],
        factor_sems,
    )
    copies = start_copies(pairs, sems)
    if level > 1:
        older_refs, store, gathered = outs[3:5], outs[5], outs[6]
        for m, piece in enumerate(store_refs):
            store[m * chips:(m + 1) * chips] = piece[...]
    for g in range(2):
        factor_copies[g].wait()
        if level > 1:
            older_refs[g][...] = slot_sum(
                level, None, chips, slot_refs[g], store, staged_ref.at[g], gathered
            )
    for copy in copies:
        copy.wait()
    if inner:
        own_rhs_ref[...] = jnp.where(straight, rhs[0], rhs[1])
        own_inverse_ref[...] = jnp.where(straight, inverse[0], inverse[1])


def sums_kernel(level, chips, *refs):
    slot_refs, store_ref, staged_ref = refs[:2], refs[2], refs[3]
    older_refs = refs[4:6]
    kept_ref, sent_ref, gathered = refs[-3:]
    core, col = own_place()
    sums = []
    for g in range(2):
        total = slot_sum(level, level - 1, chips, slot_refs[g], store_ref, staged_ref.at[g], gathered)
        sums.append(total + older_refs[g][...] if level > 1 else total)
    straight = core == col
    kept_ref[...] = jnp.where(straight, sums[0], sums[1]).astype(kept_ref.dtype)
    sent_ref[...] = jnp.where(straight, sums[1], sums[0]).astype(sent_ref.dtype)


def inner_kernel(kept_ref, arrived_ref, rhs_ref, inverse_ref, out_ref, copies_ref):
    solved = solve(rhs_ref[...] - (kept_ref[...] + arrived_ref[...]), inverse_ref[...])
    out_ref[...] = solved
    rounded = solved.astype(jnp.bfloat16)
    for i in range(copies_ref.shape[0]):
        copies_ref[i] = rounded


def last_kernel(first_ref, second_ref, rhs_ref, inverse_ref, *refs):
    done_refs, out_ref = refs[:-1], refs[-1]
    level = len(done_refs)
    for m, done in enumerate(done_refs):
        out_ref[m, 0] = done[...]
    update = first_ref[...].astype(jnp.float32) + second_ref[...].astype(jnp.float32)
    solved = solve(rhs_ref[...] - update, inverse_ref[...])
    out_ref[level, 0] = solved


def paired_shards(row_count, right_sides, factor_blocks, diag_inverses, source_ids, block_counts):
    level_count, _, rhs_count, width = right_sides.shape
    slots = factor_blocks.shape[3]
    rows = rhs_count // 2
    chips = row_count // 2
    later = level_count - 1
    same_core = [[2 * j + k for j in range(chips)] for k in range(2)]
    part = jax.ShapeDtypeStruct((rows, width), jnp.float32)
    rounded_part = jax.ShapeDtypeStruct((rows, width), jnp.bfloat16)
    square = jax.ShapeDtypeStruct((width, width), jnp.bfloat16)
    copies = jax.ShapeDtypeStruct((chips, rows, width), jnp.bfloat16)
    solve_flops = 2 * rows * width * width

    def over_both(x, move):
        pairs = []
        for j in range(chips):
            for k in range(2):
                for c in range(2):
                    tj, tk, tc = move(j, k, c)
                    pairs.append(((2 * j + k) * 2 + c, (2 * tj + tk) * 2 + tc))
        return lax.ppermute(x, ("rows", "cols"), pairs)

    def swap_core(x):
        return lax.ppermute(x, "rows", [(i, i ^ 1) for i in range(row_count)])

    def transpose(x):
        return over_both(x, lambda j, k, c: (j, c, k))

    def spread(x):
        return lax.all_to_all(x, "rows", 0, 0, axis_index_groups=same_core)

    other_inverses, other_rhs = swap_core(diag_inverses), swap_core(right_sides)
    counts = block_counts.reshape(later)
    live_ids, own_rhs, own_inverse = run(
        prepare_kernel,
        (
            (jax.ShapeDtypeStruct(source_ids.shape, source_ids.dtype), SMEM),
            (part, VMEM),
            (square, VMEM),
        ),
        ((source_ids, HBM), (counts, HBM), (right_sides, HBM), (diag_inverses, HBM)),
        scratch=(
            pltpu.SMEM(source_ids.shape, source_ids.dtype),
            pltpu.SMEM(counts.shape, counts.dtype),
            pltpu.SemaphoreType.DMA((4,)),
        ),
    )
    solved, copied = run(
        first_kernel,
        ((part, VMEM), (copies, VMEM)),
        ((own_rhs, VMEM), (other_rhs, VMEM), (own_inverse, VMEM), (other_inverses, VMEM)),
        flops=solve_flops,
    )
    finished = [transpose(solved)]
    stores = [spread(copied)]
    sent_factors, _, _, _ = lax.optimization_barrier((factor_blocks, other_rhs, other_inverses, live_ids))
    sent_ids, solved = lax.optimization_barrier((live_ids, solved))
    other_ids = swap_core(sent_ids)
    slot_args = ((live_ids, SMEM), (other_ids, SMEM))
    staged_args = (
        (factor_blocks, HBM),
        (swap_core(sent_factors), HBM),
        (right_sides, HBM),
        (other_rhs, HBM),
        (diag_inverses, HBM),
        (other_inverses, HBM),
    )
    staged_shape = jax.ShapeDtypeStruct((2, slots, width, width), jnp.bfloat16)
    gathered = pltpu.VMEM((rows, slots * width), jnp.bfloat16)
    after = ()
    for l in range(1, level_count):
        staged, rhs, inverse, *older = run(
            functools.partial(stage_kernel, l, later, chips),
            ((staged_shape, FIXED), (part, VMEM), (square, VMEM)) + ((part, VMEM), (part, VMEM)) * (l > 1),
            slot_args + staged_args + tuple((x, VMEM) for x in stores[:l - 1]) + after,
            scratch=((pltpu.VMEM(((l - 1) * chips, rows, width), jnp.bfloat16), gathered) if l > 1 else ())
            + (
                pltpu.VMEM((2, rows, width), jnp.float32),
                pltpu.VMEM((2, width, width), jnp.bfloat16),
                pltpu.SemaphoreType.DMA((4,)),
                pltpu.SemaphoreType.DMA((2,)),
            ),
            flops=2 * slots * solve_flops * (l > 1),
            transferred=2 * slots * width * width * 2,
        )
        kept, sent = run(
            functools.partial(sums_kernel, l, chips),
            ((part if l < later else rounded_part, VMEM),) * 2,
            slot_args
            + ((stores[-1], VMEM), (staged, FIXED))
            + tuple((x, VMEM) for x in older)
            + tuple((x, ANY) for x in finished),
            scratch=(gathered,),
            flops=2 * slots * solve_flops,
            transferred=2 * slots * width * width * 2,
        )
        after = ((kept, ANY),)
        if l < later:
            arrived = lax.ppermute(sent, "cols", [(0, 1), (1, 0)])
            solved, copied = run(
                inner_kernel,
                ((part, VMEM), (copies, VMEM)),
                tuple((x, VMEM) for x in (kept, arrived, rhs, inverse)),
                flops=solve_flops,
            )
            finished.append(transpose(solved))
            stores.append(spread(copied))
    second = over_both(sent, lambda j, k, c: (j, 1 - c, k))
    first = over_both(kept, lambda j, k, c: (j, c, k))
    out, = run(
        last_kernel,
        ((jax.ShapeDtypeStruct((level_count, 1, rows, width), jnp.float32), VMEM),),
        tuple((x, VMEM) for x in (second, first, rhs, inverse, *finished)),
        flops=solve_flops,
    )
    return out


def gather_slots(ids_ref, counts_ref, group, store_ref, gathered, slots, width):
    for k in range(slots):
        piece = store_ref[ids_ref[group, k]]
        live = jnp.where(k < counts_ref[group], 1.0, 0.0).astype(piece.dtype)
        gathered[:, k * width:(k + 1) * width] = piece * live


def level_kernel(groups, ids_ref, counts_ref, store_ref, *refs):
    factor_refs = refs[:groups]
    rhs_ref, inverse_ref, out_ref, rounded_ref, gathered = refs[groups:]
    slots, width = factor_refs[0].shape[0], factor_refs[0].shape[1]
    update = None
    for g in range(groups):
        gather_slots(ids_ref, counts_ref, g, store_ref, gathered, slots, width)
        term = flat_dot(gathered, factor_refs[g])
        update = term if update is None else update + term
    reduced = (rhs_ref[...] - update).astype(jnp.bfloat16)
    solved = jnp.dot(reduced, inverse_ref[...], preferred_element_type=jnp.float32)
    out_ref[...] = solved
    rounded_ref[...] = solved.astype(jnp.bfloat16)


def solve_level(ids, counts, store, factors, rhs, inverse):
    groups = len(factors)
    rows, width = rhs.shape
    slots = factors[0].shape[0]
    vmem = pl.BlockSpec(memory_space=pltpu.VMEM)
    smem = pl.BlockSpec(memory_space=pltpu.SMEM)
    return pl.pallas_call(
        functools.partial(level_kernel, groups),
        out_shape=(
            jax.ShapeDtypeStruct((rows, width), jnp.float32),
            jax.ShapeDtypeStruct((rows, width), jnp.bfloat16),
        ),
        in_specs=[smem, smem, vmem] + [vmem] * groups + [vmem, vmem],
        out_specs=(vmem, vmem),
        scratch_shapes=[pltpu.VMEM((rows, slots * width), jnp.bfloat16)],
        compiler_params=pltpu.CompilerParams(vmem_limit_bytes=VMEM_LIMIT),
        cost_estimate=pl.CostEstimate(
            flops=2 * rows * width * width * (groups * slots + 1),
            bytes_accessed=groups * slots * width * width * 2,
            transcendentals=0,
        ),
    )(ids, counts, store, *factors, rhs, inverse)


def rotated_shards(col_count, right_sides, factor_blocks, diag_inverses, source_ids, block_counts):
    level_count, _, rhs_count, width = right_sides.shape
    share_rows = rhs_count // col_count
    col_index = lax.axis_index("cols")

    described = jnp.concatenate([source_ids[:, 0, 0], block_counts[:, 0, 0][:, None]], axis=1)
    factors = [[factor_blocks[l, 0, 0]] for l in range(level_count - 1)]
    descriptions = [described]
    for shift in range(1, col_count):
        pairs = [(i, (i + shift) % col_count) for i in range(col_count)]
        descriptions.append(lax.ppermute(described, "cols", pairs))
    for l in range(level_count - 1):
        for shift in range(1, col_count):
            pairs = [(i, (i + shift) % col_count) for i in range(col_count)]
            factors[l].append(lax.ppermute(factor_blocks[l, 0, 0], "cols", pairs))
    descriptions = jnp.stack(descriptions)

    rhs = lax.dynamic_slice_in_dim(right_sides[:, 0], col_index * share_rows, share_rows, 1)
    solutions = []
    stores = []
    for l in range(level_count):
        if l == 0:
            own = jnp.dot(
                rhs[0].astype(jnp.bfloat16), diag_inverses[0, 0], preferred_element_type=jnp.float32
            )
            rounded = own.astype(jnp.bfloat16)
        else:
            ids = descriptions[:, l - 1, :-1]
            counts = descriptions[:, l - 1, -1]
            store = stores[0] if l == 1 else jnp.concatenate(stores, axis=0)
            own, rounded = solve_level(ids, counts, store, factors[l - 1], rhs[l], diag_inverses[l, 0])
        solutions.append(own)
        if l < level_count - 1:
            stores.append(lax.all_gather(rounded, "rows", axis=0))
    return jnp.stack(solutions)[:, None]


def solution(mesh):
    row_count, col_count = mesh.shape["rows"], mesh.shape["cols"]
    chips = row_count // 2
    if col_count == 2 and row_count == 2 * chips:
        shards = functools.partial(paired_shards, row_count)
    else:
        shards = functools.partial(rotated_shards, col_count)
    return jax.shard_map(
        shards,
        mesh=mesh,
        in_specs=(
            P(None, "rows", None, None),
            P(None, "rows", "cols", None, None, None),
            P(None, "rows", None, None),
            P(None, "rows", "cols", None),
            P(None, "rows", "cols"),
        ),
        out_specs=P(None, "rows", "cols", None),
        check_vma=False,
    )
```

```python
import functools

import jax
import jax.numpy as jnp
from jax import lax
from jax.experimental import pallas as pl
from jax.experimental.pallas import tpu as pltpu
from jax.sharding import PartitionSpec as P

VMEM_LIMIT = 16 * 1024 * 1024


VMEM = pl.BlockSpec(memory_space=pltpu.VMEM)
SMEM = pl.BlockSpec(memory_space=pltpu.SMEM)
ANY = pl.BlockSpec(memory_space=pl.ANY)
HBM = pl.BlockSpec(memory_space=pltpu.HBM)
FIXED = pl.BlockSpec(memory_space=pltpu.VMEM)
PLACES = {id(HBM): pltpu.HBM, id(FIXED): pltpu.VMEM}


def flat_dot(gathered, factor_ref):
    slots, width = factor_ref.shape[0], factor_ref.shape[1]
    return jnp.dot(
        gathered[...],
        factor_ref[...].reshape(slots * width, width),
        preferred_element_type=jnp.float32,
    )


def run(kernel, outs, args, scratch=(), flops=0, transferred=0):
    out_shape = tuple(PLACES[id(spec)](x.shape, x.dtype) if id(spec) in PLACES else x for x, spec in outs)
    args = tuple(
        (pltpu.with_memory_space_constraint(x, PLACES[id(spec)]) if id(spec) in PLACES else x, spec)
        for x, spec in args
    )
    return pl.pallas_call(
        kernel,
        out_shape=out_shape,
        in_specs=[spec for _, spec in args],
        out_specs=tuple(spec for _, spec in outs),
        scratch_shapes=list(scratch),
        compiler_params=pltpu.CompilerParams(vmem_limit_bytes=VMEM_LIMIT),
        cost_estimate=pl.CostEstimate(flops=flops, bytes_accessed=transferred, transcendentals=0),
    )(*(x for x, _ in args))


def half_of(ref, level, half, rows):
    return ref.at[level, 0, pl.ds(pl.multiple_of(half * rows, rows), rows), :]


def solve(reduced, inverse):
    return jnp.dot(reduced.astype(jnp.bfloat16), inverse, preferred_element_type=jnp.float32)


def start_copies(pairs, sems):
    copies = [pltpu.make_async_copy(src, dst, sems.at[i]) for i, (src, dst) in enumerate(pairs)]
    for copy in copies:
        copy.start()
    return copies


def own_place():
    return lax.rem(lax.axis_index("rows"), 2), lax.axis_index("cols")


def prepare_kernel(
    ids_ref, counts_ref, rhs_ref, inverse_ref, live_ids_ref, own_rhs_ref, own_inverse_ref, ids, counts, sems
):
    core, _ = own_place()
    rows = own_rhs_ref.shape[0]
    copies = start_copies(
        [
            (ids_ref, ids),
            (counts_ref, counts),
            (half_of(rhs_ref, 0, core, rows), own_rhs_ref),
            (inverse_ref.at[0, 0], own_inverse_ref),
        ],
        sems,
    )
    copies[0].wait()
    copies[1].wait()
    for l in range(ids.shape[0]):
        for k in range(ids.shape[3]):
            live_ids_ref[l, 0, 0, k] = jnp.where(k < counts[l], ids[l, 0, 0, k], -1)
    copies[2].wait()
    copies[3].wait()


def both_pairs(level, rows, core, rhs_refs, inverse_refs, rhs, inverse):
    pairs = [(half_of(ref, level, core, rows), rhs.at[g]) for g, ref in enumerate(rhs_refs)]
    return pairs + [(ref.at[level, 0], inverse.at[g]) for g, ref in enumerate(inverse_refs)]


def first_kernel(rhs_ref, other_rhs_ref, inverse_ref, other_inverse_ref, *refs):
    out_ref, copies_ref = refs[-2:]
    core, col = own_place()
    straight = core == col
    other_rhs = half_of(other_rhs_ref, 0, core, out_ref.shape[0])[...]
    solved = solve(
        jnp.where(straight, rhs_ref[...], other_rhs),
        jnp.where(straight, inverse_ref[...], other_inverse_ref[0, 0]),
    )
    out_ref[...] = solved
    rounded = solved.astype(jnp.bfloat16)
    for i in range(copies_ref.shape[0]):
        copies_ref[i] = rounded


def slot_sum(level, store_level, chips, ids_ref, store_ref, factor_ref, gathered):
    slots, width = factor_ref.shape[0], factor_ref.shape[1]
    for k in range(slots):
        source_id = ids_ref[level - 1, 0, 0, k]
        source = jnp.maximum(source_id, 0)
        source_level, place = source // (2 * chips), source % (2 * chips) // 2
        live = source_id >= 0
        if store_level is None:
            live = jnp.logical_and(live, source_level < level - 1)
            place = jnp.minimum(source_level, level - 2) * chips + place
        else:
            live = jnp.logical_and(live, source_level == store_level)
        piece = store_ref[place]
        gathered[:, k * width:(k + 1) * width] = piece * jnp.where(live, 1.0, 0.0).astype(piece.dtype)
    return flat_dot(gathered, factor_ref)


def stage_kernel(level, later, chips, *refs):
    inner = level < later
    slot_refs = refs[:2]
    factor_ref, other_factor_ref, rhs_ref, other_rhs_ref, inverse_ref, other_inverse_ref = refs[2:8]
    store_refs = refs[8:7 + level]
    outs = refs[-7 if level == 1 else -11:]
    staged_ref, own_rhs_ref, own_inverse_ref = outs[:3]
    rhs, inverse, sems, factor_sems = outs[-4:]
    core, col = own_place()
    straight = core == col
    rows = own_rhs_ref.shape[0]
    if inner:
        pairs = both_pairs(
            level, rows, core, (rhs_ref, other_rhs_ref), (inverse_ref, other_inverse_ref), rhs, inverse
        )
    else:
        pairs = [
            (half_of(rhs_ref, level, col, rows), own_rhs_ref),
            (inverse_ref.at[level, 0], own_inverse_ref),
        ]
    factor_copies = start_copies(
        [
            (factor_ref.at[level - 1, 0, 0], staged_ref.at[0]),
            (other_factor_ref.at[level - 1, 0, 0], staged_ref.at[1]),
        ],
        factor_sems,
    )
    copies = start_copies(pairs, sems)
    if level > 1:
        older_refs, store, gathered = outs[3:5], outs[5], outs[6]
        for m, piece in enumerate(store_refs):
            store[m * chips:(m + 1) * chips] = piece[...]
    for g in range(2):
        factor_copies[g].wait()
        if level > 1:
            older_refs[g][...] = slot_sum(
                level, None, chips, slot_refs[g], store, staged_ref.at[g], gathered.at[g]
            )
    for copy in copies:
        copy.wait()
    if inner:
        own_rhs_ref[...] = jnp.where(straight, rhs[0], rhs[1])
        own_inverse_ref[...] = jnp.where(straight, inverse[0], inverse[1])


def sums_kernel(level, chips, *refs):
    slot_refs, store_ref, staged_ref = refs[:2], refs[2], refs[3]
    older_refs = refs[4:6]
    kept_ref, sent_ref, gathered = refs[-3:]
    core, col = own_place()
    sums = []
    for g in range(2):
        total = slot_sum(level, level - 1, chips, slot_refs[g], store_ref, staged_ref.at[g], gathered.at[g])
        sums.append(total + older_refs[g][...] if level > 1 else total)
    straight = core == col
    kept_ref[...] = jnp.where(straight, sums[0], sums[1]).astype(kept_ref.dtype)
    sent_ref[...] = jnp.where(straight, sums[1], sums[0]).astype(sent_ref.dtype)


def inner_kernel(kept_ref, arrived_ref, rhs_ref, inverse_ref, out_ref, copies_ref):
    solved = solve(rhs_ref[...] - (kept_ref[...] + arrived_ref[...]), inverse_ref[...])
    out_ref[...] = solved
    rounded = solved.astype(jnp.bfloat16)
    for i in range(copies_ref.shape[0]):
        copies_ref[i] = rounded


def last_kernel(first_ref, second_ref, rhs_ref, inverse_ref, *refs):
    done_refs, out_ref = refs[:-1], refs[-1]
    level = len(done_refs)
    for m, done in enumerate(done_refs):
        out_ref[m, 0] = done[...]
    update = first_ref[...].astype(jnp.float32) + second_ref[...].astype(jnp.float32)
    solved = solve(rhs_ref[...] - update, inverse_ref[...])
    out_ref[level, 0] = solved


def paired_shards(row_count, right_sides, factor_blocks, diag_inverses, source_ids, block_counts):
    level_count, _, rhs_count, width = right_sides.shape
    slots = factor_blocks.shape[3]
    rows = rhs_count // 2
    chips = row_count // 2
    later = level_count - 1
    same_core = [[2 * j + k for j in range(chips)] for k in range(2)]
    part = jax.ShapeDtypeStruct((rows, width), jnp.float32)
    rounded_part = jax.ShapeDtypeStruct((rows, width), jnp.bfloat16)
    square = jax.ShapeDtypeStruct((width, width), jnp.bfloat16)
    copies = jax.ShapeDtypeStruct((chips, rows, width), jnp.bfloat16)
    solve_flops = 2 * rows * width * width

    def over_both(x, move):
        pairs = []
        for j in range(chips):
            for k in range(2):
                for c in range(2):
                    tj, tk, tc = move(j, k, c)
                    pairs.append(((2 * j + k) * 2 + c, (2 * tj + tk) * 2 + tc))
        return lax.ppermute(x, ("rows", "cols"), pairs)

    def swap_core(x):
        return lax.ppermute(x, "rows", [(i, i ^ 1) for i in range(row_count)])

    def transpose(x):
        return over_both(x, lambda j, k, c: (j, c, k))

    def spread(x):
        return lax.all_to_all(x, "rows", 0, 0, axis_index_groups=same_core)

    other_inverses, other_rhs = swap_core(diag_inverses), swap_core(right_sides)
    counts = block_counts.reshape(later)
    live_ids, own_rhs, own_inverse = run(
        prepare_kernel,
        (
            (jax.ShapeDtypeStruct(source_ids.shape, source_ids.dtype), SMEM),
            (part, VMEM),
            (square, VMEM),
        ),
        ((source_ids, HBM), (counts, HBM), (right_sides, HBM), (diag_inverses, HBM)),
        scratch=(
            pltpu.SMEM(source_ids.shape, source_ids.dtype),
            pltpu.SMEM(counts.shape, counts.dtype),
            pltpu.SemaphoreType.DMA((4,)),
        ),
    )
    solved, copied = run(
        first_kernel,
        ((part, VMEM), (copies, VMEM)),
        ((own_rhs, VMEM), (other_rhs, VMEM), (own_inverse, VMEM), (other_inverses, VMEM)),
        flops=solve_flops,
    )
    finished = [transpose(solved)]
    stores = [spread(copied)]
    sent_factors, _, _, _ = lax.optimization_barrier((factor_blocks, other_rhs, other_inverses, live_ids))
    sent_ids, solved = lax.optimization_barrier((live_ids, solved))
    other_ids = swap_core(sent_ids)
    slot_args = ((live_ids, SMEM), (other_ids, SMEM))
    staged_args = (
        (factor_blocks, HBM),
        (swap_core(sent_factors), HBM),
        (right_sides, HBM),
        (other_rhs, HBM),
        (diag_inverses, HBM),
        (other_inverses, HBM),
    )
    staged_shape = jax.ShapeDtypeStruct((2, slots, width, width), jnp.bfloat16)
    gathered = pltpu.VMEM((2, rows, slots * width), jnp.bfloat16)
    after = ()
    for l in range(1, level_count):
        staged, rhs, inverse, *older = run(
            functools.partial(stage_kernel, l, later, chips),
            ((staged_shape, FIXED), (part, VMEM), (square, VMEM)) + ((part, VMEM), (part, VMEM)) * (l > 1),
            slot_args + staged_args + tuple((x, VMEM) for x in stores[:l - 1]) + after,
            scratch=((pltpu.VMEM(((l - 1) * chips, rows, width), jnp.bfloat16), gathered) if l > 1 else ())
            + (
                pltpu.VMEM((2, rows, width), jnp.float32),
                pltpu.VMEM((2, width, width), jnp.bfloat16),
                pltpu.SemaphoreType.DMA((4,)),
                pltpu.SemaphoreType.DMA((2,)),
            ),
            flops=2 * slots * solve_flops * (l > 1),
            transferred=2 * slots * width * width * 2,
        )
        kept, sent = run(
            functools.partial(sums_kernel, l, chips),
            ((part if l < later else rounded_part, VMEM),) * 2,
            slot_args
            + ((stores[-1], VMEM), (staged, FIXED))
            + tuple((x, VMEM) for x in older)
            + tuple((x, ANY) for x in finished),
            scratch=(gathered,),
            flops=2 * slots * solve_flops,
            transferred=2 * slots * width * width * 2,
        )
        after = ((kept, ANY),)
        if l < later:
            arrived = lax.ppermute(sent, "cols", [(0, 1), (1, 0)])
            solved, copied = run(
                inner_kernel,
                ((part, VMEM), (copies, VMEM)),
                tuple((x, VMEM) for x in (kept, arrived, rhs, inverse)),
                flops=solve_flops,
            )
            finished.append(transpose(solved))
            stores.append(spread(copied))
    first = over_both(kept, lambda j, k, c: (j, c, k))
    second = over_both(sent, lambda j, k, c: (j, 1 - c, k))
    out, = run(
        last_kernel,
        ((jax.ShapeDtypeStruct((level_count, 1, rows, width), jnp.float32), VMEM),),
        tuple((x, VMEM) for x in (first, second, rhs, inverse, *finished)),
        flops=solve_flops,
    )
    return out


def gather_slots(ids_ref, counts_ref, group, store_ref, gathered, slots, width):
    for k in range(slots):
        piece = store_ref[ids_ref[group, k]]
        live = jnp.where(k < counts_ref[group], 1.0, 0.0).astype(piece.dtype)
        gathered[:, k * width:(k + 1) * width] = piece * live


def level_kernel(groups, ids_ref, counts_ref, store_ref, *refs):
    factor_refs = refs[:groups]
    rhs_ref, inverse_ref, out_ref, rounded_ref, gathered = refs[groups:]
    slots, width = factor_refs[0].shape[0], factor_refs[0].shape[1]
    update = None
    for g in range(groups):
        gather_slots(ids_ref, counts_ref, g, store_ref, gathered, slots, width)
        term = flat_dot(gathered, factor_refs[g])
        update = term if update is None else update + term
    reduced = (rhs_ref[...] - update).astype(jnp.bfloat16)
    solved = jnp.dot(reduced, inverse_ref[...], preferred_element_type=jnp.float32)
    out_ref[...] = solved
    rounded_ref[...] = solved.astype(jnp.bfloat16)


def solve_level(ids, counts, store, factors, rhs, inverse):
    groups = len(factors)
    rows, width = rhs.shape
    slots = factors[0].shape[0]
    vmem = pl.BlockSpec(memory_space=pltpu.VMEM)
    smem = pl.BlockSpec(memory_space=pltpu.SMEM)
    return pl.pallas_call(
        functools.partial(level_kernel, groups),
        out_shape=(
            jax.ShapeDtypeStruct((rows, width), jnp.float32),
            jax.ShapeDtypeStruct((rows, width), jnp.bfloat16),
        ),
        in_specs=[smem, smem, vmem] + [vmem] * groups + [vmem, vmem],
        out_specs=(vmem, vmem),
        scratch_shapes=[pltpu.VMEM((rows, slots * width), jnp.bfloat16)],
        compiler_params=pltpu.CompilerParams(vmem_limit_bytes=VMEM_LIMIT),
        cost_estimate=pl.CostEstimate(
            flops=2 * rows * width * width * (groups * slots + 1),
            bytes_accessed=groups * slots * width * width * 2,
            transcendentals=0,
        ),
    )(ids, counts, store, *factors, rhs, inverse)


def rotated_shards(col_count, right_sides, factor_blocks, diag_inverses, source_ids, block_counts):
    level_count, _, rhs_count, width = right_sides.shape
    share_rows = rhs_count // col_count
    col_index = lax.axis_index("cols")

    described = jnp.concatenate([source_ids[:, 0, 0], block_counts[:, 0, 0][:, None]], axis=1)
    factors = [[factor_blocks[l, 0, 0]] for l in range(level_count - 1)]
    descriptions = [described]
    for shift in range(1, col_count):
        pairs = [(i, (i + shift) % col_count) for i in range(col_count)]
        descriptions.append(lax.ppermute(described, "cols", pairs))
    for l in range(level_count - 1):
        for shift in range(1, col_count):
            pairs = [(i, (i + shift) % col_count) for i in range(col_count)]
            factors[l].append(lax.ppermute(factor_blocks[l, 0, 0], "cols", pairs))
    descriptions = jnp.stack(descriptions)

    rhs = lax.dynamic_slice_in_dim(right_sides[:, 0], col_index * share_rows, share_rows, 1)
    solutions = []
    stores = []
    for l in range(level_count):
        if l == 0:
            own = jnp.dot(
                rhs[0].astype(jnp.bfloat16), diag_inverses[0, 0], preferred_element_type=jnp.float32
            )
            rounded = own.astype(jnp.bfloat16)
        else:
            ids = descriptions[:, l - 1, :-1]
            counts = descriptions[:, l - 1, -1]
            store = stores[0] if l == 1 else jnp.concatenate(stores, axis=0)
            own, rounded = solve_level(ids, counts, store, factors[l - 1], rhs[l], diag_inverses[l, 0])
        solutions.append(own)
        if l < level_count - 1:
            stores.append(lax.all_gather(rounded, "rows", axis=0))
    return jnp.stack(solutions)[:, None]


def solution(mesh):
    row_count, col_count = mesh.shape["rows"], mesh.shape["cols"]
    chips = row_count // 2
    if col_count == 2 and row_count == 2 * chips:
        shards = functools.partial(paired_shards, row_count)
    else:
        shards = functools.partial(rotated_shards, col_count)
    return jax.shard_map(
        shards,
        mesh=mesh,
        in_specs=(
            P(None, "rows", None, None),
            P(None, "rows", "cols", None, None, None),
            P(None, "rows", None, None),
            P(None, "rows", "cols", None),
            P(None, "rows", "cols"),
        ),
        out_specs=P(None, "rows", "cols", None),
        check_vma=False,
    )
```
